32 devices in a mesh: island: 2 (over x), dp: 2 (over y), expert: 8 (over z, core).
Axes of the slice: x: 2, y: 2, z: 4, core: 2. Of those that a mesh axis runs over, the one named last changes fastest.
Arguments:
- theta: bfloat16 [2, 8, 384, 2048], P('island', 'expert', 'dp'), may hold values from -7.5 to 7.5
- first_moment: bfloat16 [2, 8, 384, 2048], P('island', 'expert', 'dp'), may hold values from -0.119628906 to 0.119628906
- second_moment: bfloat16 [2, 8, 384, 2048], P('island', 'expert', 'dp'), may hold values from 9.9658966e-05 to 0.0099487305
- anchor: float32 [8, 384, 2048], P('expert', 'dp', 'island'), may hold values from -4.5 to 4.5
- momentum: float32 [8, 384, 2048], P('expert', 'dp', 'island'), may hold values from -1.8 to 1.8
- cotangent: bfloat16 [4096, 2048], P(('island', 'dp', 'expert')), may hold values from -6 to 6
- weights: float32 [4096, 8], P(('island', 'dp', 'expert')), may hold values from 0.05 to 0.3
- expert_ids: int32 [4096, 8], P(('island', 'dp', 'expert')), may hold values from 0 to 127, as said below
- expert_counts: int32 [32, 4], P(('island', 'dp', 'expert')), may hold values from 1 to 16, as said below
- hidden_saved: bfloat16 [2, 2, 8, 128, 384], P('island', 'dp', 'expert'), may hold values from -6 to 6
Outputs:
- anchor_new: float32 [8, 384, 2048], P('expert', 'dp', 'island')
- momentum_new: float32 [8, 384, 2048], P('expert', 'dp', 'island')
- d_hidden: bfloat16 [2, 2, 8, 128, 384], P('island', 'dp', 'expert')
The draws below stay inside these ranges and needn't reach their ends.
Inputs may be any that keep to these rules, and one draw needn't show every extreme that they name: `expert_ids`: in each block of 128 rows a row's ids are distinct, every id below 4 is named by 1 to 16 pairs of the block, and those counts equal expert_counts of the block. expert_counts[b, e] is the number of pairs of block b naming expert e.
All inputs are finite; a program needn't handle non-finite values.
Results may differ from the reference program's by a relative error of at most 0.014.
Values may be sent and summed in bfloat16 or wider, within the bound.
No kernel may reach another device: no remote copies, remote signals or barrier semaphores. Data moves between devices by JAX's collectives and lax.ppermute only.
A program may use at most 64 MiB of HBM per device.

```python
import math
import jax
import jax.numpy as jnp
from jax import lax

D = 2048
FF = 768
EXPERTS_ALL = 128
TOP = 8
TOK_DEV = 128
CAP = 16
EXPERTS = 4
UNITS = 8
FF_UNIT = 384
SLOTS = 128
TOKENS = 4096
N_ISLAND = 2
N_DP = 2
N_EXPERT = 8


def routing_tables(key):
    blocks = TOKENS // TOK_DEV
    keys = jax.random.split(key, 8)
    hotness = jax.random.randint(keys[0], (EXPERTS,), 0, 4)
    is_hot = hotness == 0
    cold_counts = 1 + jax.random.randint(keys[1], (blocks, EXPERTS), 0, max(CAP // 2, 1))
    hot_low = 3 * CAP // 4
    hot_counts = hot_low + jax.random.randint(keys[7], (blocks, EXPERTS), 0, CAP - hot_low + 1)
    counts = jnp.where(is_hot[None, :], hot_counts, cold_counts).astype(jnp.int32)
    full_expert = jax.random.randint(keys[2], (), 0, EXPERTS)
    second_expert = jax.random.randint(keys[3], (blocks,), 0, EXPERTS)
    expert_range = jnp.arange(EXPERTS, dtype=jnp.int32)
    forced = (expert_range[None, :] == full_expert) | (expert_range[None, :] == second_expert[:, None])
    counts = jnp.where(forced, CAP, counts).astype(jnp.int32)
    run_ends = jnp.cumsum(counts, axis=1)
    position = jnp.arange(TOK_DEV * TOP, dtype=jnp.int32)
    owner = jnp.sum((position[None, :, None] >= run_ends[:, None, :]).astype(jnp.int32), axis=2)
    inside = position[None, :] < run_ends[:, -1:]
    window_ids = jnp.where(inside, owner, -1).reshape(blocks, TOP, TOK_DEV).transpose(0, 2, 1)
    others = EXPERTS_ALL - EXPERTS
    scores = jax.random.randint(keys[4], (blocks, TOK_DEV, others), 0, 1 << 20) * others + jnp.arange(others, dtype=jnp.int32)
    picks = lax.top_k(scores, TOP)[1].astype(jnp.int32) + EXPERTS
    combined = jnp.where(window_ids >= 0, window_ids, picks)
    row_keys = jax.random.randint(keys[5], (blocks, TOK_DEV), 0, 1 << 20) * TOK_DEV + jnp.arange(TOK_DEV, dtype=jnp.int32)
    row_order = jnp.argsort(row_keys, axis=1, stable=True)
    combined = jnp.take_along_axis(combined, row_order[:, :, None], axis=1)
    column_keys = jax.random.randint(keys[6], (blocks, TOK_DEV, TOP), 0, 1 << 20) * TOP + jnp.arange(TOP, dtype=jnp.int32)
    column_order = jnp.argsort(column_keys, axis=2, stable=True)
    combined = jnp.take_along_axis(combined, column_order, axis=2)
    return (combined.reshape(blocks * TOK_DEV, TOP).astype(jnp.int32), counts)


def draw_expert_ids(key, part):
    return routing_tables(jax.random.fold_in(key, 11))[0]


def draw_expert_counts(key, part):
    return routing_tables(jax.random.fold_in(key, 11))[1]


def outer_state(key):
    keys = jax.random.split(jax.random.fold_in(key, 23), 5)
    field_shape = (UNITS, FF_UNIT, D)
    anchor = 0.7 * jnp.clip(jax.random.normal(keys[1], field_shape, jnp.float32), -6.0, 6.0)
    drift = 0.6 * jnp.clip(jax.random.normal(keys[4], (N_ISLAND,) + field_shape, jnp.float32), -4.0, 4.0)
    theta = (anchor[None] + drift).astype(jnp.bfloat16)
    return (theta, anchor)


def draw_theta(key, part):
    return outer_state(key)[0]


def draw_anchor(key, part):
    return outer_state(key)[1]


def level_of(stream_key, dims, pieces, smallest, largest):
    def one(axis_at, parts):
        steps = jax.random.uniform(jax.random.fold_in(jax.random.fold_in(stream_key, 6), axis_at), (parts,), jnp.float32, smallest / len(pieces), largest / len(pieces))
        return jnp.repeat(jnp.exp(steps), dims[axis_at] // parts).reshape((-1,) + (1,) * (len(dims) - axis_at - 1))

    level = one(*pieces[0])
    for cut in pieces[1:]:
        level = level * one(*cut)
    return level


def noise(rng, extent, spread, bound, pieces=(), kind=jnp.bfloat16):
    level = level_of(rng, extent, pieces, -0.22, 0.18) if pieces else 1.0
    values = jax.random.normal(rng, extent, jnp.float32) * spread * level
    return jnp.minimum(jnp.maximum(values, -bound), bound).astype(kind)


def setup_inputs(seed: int = 0) -> dict:
    streams_of = jax.random.split(jax.random.key(seed), 11)
    return {
        "theta": draw_theta(jax.random.fold_in(streams_of[10], 71), 0),
        "first_moment": noise(streams_of[1], (N_ISLAND, UNITS, FF_UNIT, D), 0.02, 0.119628906, ((0, 2), (1, 8), (2, 2))),
        "second_moment": jnp.clip(jnp.exp(math.log(0.0099487305) - 4.603446 * jax.random.uniform(streams_of[2], (N_ISLAND, UNITS, FF_UNIT, D), jnp.float32) ** level_of(streams_of[2], (N_ISLAND, UNITS, FF_UNIT, D), ((0, 2), (1, 8), (2, 2)), -0.2, 0.2)), 9.965896606445312e-05, 0.0099487305).astype(jnp.bfloat16),
        "anchor": draw_anchor(jax.random.fold_in(streams_of[10], 71), 0),
        "momentum": noise(streams_of[4], (UNITS, FF_UNIT, D), 0.3, 1.8, ((0, 8), (1, 2), (2, 2)), jnp.float32),
        "cotangent": noise(streams_of[5], (TOKENS, D), 1.0, 6.0, ((0, 32),)),
        "weights": jnp.clip(0.05 + 0.25 * jax.random.uniform(streams_of[6], (TOKENS, TOP), jnp.float32) ** level_of(streams_of[6], (TOKENS, TOP), ((0, 32),), -0.2, 0.2), 0.05, 0.3),
        "expert_ids": draw_expert_ids(jax.random.fold_in(streams_of[10], 71), 0),
        "expert_counts": draw_expert_counts(jax.random.fold_in(streams_of[10], 71), 0),
        "hidden_saved": noise(streams_of[9], (N_ISLAND, N_DP, UNITS, SLOTS, FF_UNIT), 1.0, 6.0, ((0, 2), (1, 2), (2, 8))),
    }


beta_one = 0.9
beta_two = 0.95
adam_epsilon = 1e-08
inner_rate = 0.1
decay_rate = 0.1
outer_beta = 0.9
outer_rate = 0.7

def pack_rows(capacity, cotangent, weights, expert_ids, counts):
    window_experts = counts.shape[0]
    route_width = expert_ids.shape[1]
    flat_ids = expert_ids.reshape(-1)
    match_table = (flat_ids[:, None] == jnp.arange(window_experts, dtype=jnp.int32)[None, :]).astype(jnp.int32)
    earlier = jnp.cumsum(match_table, axis=0) - match_table
    pair_rank = lax.optimization_barrier(jnp.sum(earlier * match_table, axis=1))
    slot_limit = lax.optimization_barrier(jnp.sum(match_table * counts[None, :], axis=1))
    is_live = pair_rank < slot_limit
    slot_index = jnp.where(is_live, flat_ids * capacity + pair_rank, window_experts * capacity).astype(jnp.int32)
    source_row = (jnp.arange(flat_ids.shape[0], dtype=jnp.int32) // route_width).astype(jnp.int32)
    slot_source = jnp.zeros((window_experts * capacity + 1,), jnp.int32).at[slot_index].set(source_row)[:-1]
    live_weight = jnp.where(is_live, weights.reshape(-1), jnp.zeros_like(weights.reshape(-1)))
    slot_scale = jnp.zeros((window_experts * capacity + 1,), jnp.float32).at[slot_index].set(live_weight)[:-1]
    packed = (cotangent[slot_source].astype(jnp.float32) * slot_scale[:, None]).astype(jnp.bfloat16)
    return packed.reshape(window_experts, capacity, cotangent.shape[1])

def reference(theta, first_moment, second_moment, anchor, momentum, cotangent, weights, expert_ids, expert_counts, hidden_saved):
    scale = FF ** (-0.5)
    group_cot = cotangent.reshape(N_ISLAND, N_DP, N_EXPERT, TOK_DEV, D)
    group_weights = weights.reshape(N_ISLAND, N_DP, N_EXPERT, TOK_DEV, TOP)
    group_ids = expert_ids.reshape(N_ISLAND, N_DP, N_EXPERT, TOK_DEV, TOP)
    group_counts = expert_counts.reshape(N_ISLAND, N_DP, N_EXPERT, EXPERTS)
    packer = jax.vmap(pack_rows, in_axes=(None, 0, 0, 0, 0))

    def island_step(inputs):
        own_theta, own_first, own_second, own_cot, own_weights, own_ids, own_counts, own_saved = inputs
        grad = jnp.zeros((UNITS, FF_UNIT, D), jnp.float32)
        hidden_grads = []
        for data_index in range(N_DP):
            packed = packer(CAP, own_cot[data_index], own_weights[data_index], own_ids[data_index], own_counts[data_index])
            saved_group = own_saved[data_index]

            def unit_step(unit_index):
                chosen = lax.dynamic_index_in_dim(packed, unit_index // 2, 1, keepdims=False).reshape(SLOTS, D)
                saved = lax.dynamic_index_in_dim(saved_group, unit_index, 0, keepdims=False)
                weight_unit = lax.dynamic_index_in_dim(own_theta, unit_index, 0, keepdims=False)
                hidden_grad = (scale * jnp.dot(chosen, weight_unit.T, preferred_element_type=jnp.float32)).astype(jnp.bfloat16)
                partial_grad = (scale * jnp.dot(saved.T, chosen, preferred_element_type=jnp.float32)).astype(jnp.bfloat16)
                return (hidden_grad, partial_grad)
            hidden_part, partial_part = lax.map(unit_step, jnp.arange(UNITS, dtype=jnp.int32))
            partial_part = lax.optimization_barrier(partial_part)
            grad = grad + partial_part.astype(jnp.float32)
            hidden_grads.append(hidden_part)
        first_new = beta_one * own_first.astype(jnp.float32) + (1.0 - beta_one) * grad
        second_new = beta_two * own_second.astype(jnp.float32) + (1.0 - beta_two) * grad * grad
        theta_wide = own_theta.astype(jnp.float32)
        step_size = first_new / (jnp.sqrt(second_new) + adam_epsilon) + decay_rate * theta_wide
        theta_new = (theta_wide - inner_rate * step_size).astype(jnp.bfloat16)
        return (theta_new, jnp.stack(hidden_grads))
    new_thetas, d_hidden = lax.map(island_step, (theta, first_moment, second_moment, group_cot, group_weights, group_ids, group_counts, hidden_saved))
    delta_total = jnp.zeros_like(anchor)
    for island_index in range(N_ISLAND):
        delta_total = delta_total + (anchor - new_thetas[island_index].astype(jnp.float32))
    mean_delta = delta_total / N_ISLAND
    momentum_new = outer_beta * momentum + mean_delta
    anchor_new = anchor - outer_rate * (mean_delta + outer_beta * momentum_new)
    return (anchor_new, momentum_new, d_hidden)
```

```python
import functools

import jax
import jax.numpy as jnp
from jax import lax
from jax.experimental import pallas as pl
from jax.experimental.pallas import tpu as pltpu
from jax.sharding import PartitionSpec as P

FF = 768
CAP = 16

beta_one = 0.9
beta_two = 0.95
adam_epsilon = 1e-08
inner_rate = 0.1
decay_rate = 0.1
outer_beta = 0.9
outer_rate = 0.7

VMEM = pl.BlockSpec(memory_space=pltpu.VMEM)
SMEM = pl.BlockSpec(memory_space=pltpu.SMEM)
PARAMS = pltpu.CompilerParams(vmem_limit_bytes=48 * 1024 * 1024)


def wrap(value, size):
    return lax.rem(value + size, size)


def pack_body(experts, ids_ref, weights_ref, counts_ref, cot_ref, *outs):
    width, tokens = ids_ref.shape
    rows = experts * CAP
    first = lax.div(lax.axis_index("expert"), 2)
    expert = lax.broadcasted_iota(jnp.int32, (experts, CAP, tokens), 0).reshape(rows, tokens) + first
    expert = jnp.where(expert >= experts, expert - experts, expert)
    rank = lax.broadcasted_iota(jnp.int32, (experts, CAP, tokens), 1).reshape(rows, tokens)
    named = jnp.zeros((rows, tokens), jnp.float32)
    weight = jnp.zeros((rows, tokens), jnp.float32)
    for slot in range(width):
        hit = ids_ref[slot : slot + 1, :] == expert
        named = jnp.where(hit, 1.0, named)
        weight = jnp.where(hit, weights_ref[slot : slot + 1, :], weight)
    limit = jnp.zeros((rows, tokens), jnp.int32)
    for index in range(experts):
        limit = jnp.where(expert == index, counts_ref[0, index], limit)
    earlier = (
        lax.broadcasted_iota(jnp.int32, (tokens, tokens), 0)
        < lax.broadcasted_iota(jnp.int32, (tokens, tokens), 1)
    )
    earlier = jnp.where(earlier, 1.0, 0.0).astype(jnp.bfloat16)
    found = jnp.dot(named.astype(jnp.bfloat16), earlier, preferred_element_type=jnp.float32)
    found = found.astype(jnp.int32)
    picked = (named > 0.0) & (found < limit) & (found == rank)
    pick = jnp.where(picked, 1.0, 0.0)
    scale = jnp.sum(pick * weight, axis=1, keepdims=True)
    gathered = jnp.dot(pick.astype(jnp.bfloat16), cot_ref[...], preferred_element_type=jnp.float32)
    packed = (gathered * scale).astype(jnp.bfloat16)
    for index, out in enumerate(outs):
        out[...] = packed[index * CAP : (index + 1) * CAP]


def pack_rows(cotangent, weights, expert_ids, counts):
    experts = counts.shape[1]
    out = jax.ShapeDtypeStruct((CAP, cotangent.shape[1]), jnp.bfloat16)
    return pl.pallas_call(
        functools.partial(pack_body, experts),
        out_shape=[out] * experts,
        in_specs=[VMEM, VMEM, SMEM, VMEM],
        out_specs=[VMEM] * experts,
        compiler_params=PARAMS,
        name="pack",
    )(expert_ids.T, weights.T, counts, cotangent)


def adam(grad, first, second, theta):
    first_new = beta_one * first.astype(jnp.float32) + (1.0 - beta_one) * grad
    second_new = beta_two * second.astype(jnp.float32) + (1.0 - beta_two) * grad * grad
    wide = theta.astype(jnp.float32)
    step_size = first_new / (jnp.sqrt(second_new) + adam_epsilon) + decay_rate * wide
    return (wide - inner_rate * step_size).astype(jnp.bfloat16)


def far_body(n_dp, n_island, pairs, *refs):
    quarters = refs[: 2 * n_dp]
    saved = refs[2 * n_dp : 3 * n_dp]
    theta_ref, first_ref, second_ref = refs[3 * n_dp : 3 * n_dp + 3]
    outs = refs[3 * n_dp + 3 : 3 * n_dp + 3 + n_island - 1]
    slots_ref, left_ref, scratch = refs[3 * n_dp + 3 + n_island - 1 :]
    units = theta_ref.shape[0]
    island, data, position = (lax.axis_index(name) for name in ("island", "dp", "expert"))
    core = lax.rem(position, 2)
    first = lax.div(position, 2)
    length = 2 * pairs * CAP
    for shift in range(n_dp):
        group = wrap(data - shift, n_dp)
        for flip in range(2):
            source = core if flip == 0 else 1 - core
            block = quarters[2 * shift + flip]
            for k in range(pairs):
                row = group * length + (2 * wrap(first - k, pairs) + source) * CAP
                row = pl.multiple_of(row, CAP)
                slots_ref[pl.ds(row, CAP), :] = block[k * CAP : (k + 1) * CAP, :]
        scratch[...] = saved[shift][...].astype(jnp.float32).T
        own = scratch[pl.ds(pl.multiple_of(data * units, 8), units), :]
        column = pl.multiple_of(group * length, 128)
        left_ref[:, pl.ds(column, length)] = own.astype(jnp.bfloat16)
    part = theta_ref.shape[1] // n_island
    for shift, out in enumerate(outs):
        columns = pl.ds(pl.multiple_of(lax.rem(island + shift + 1, n_island) * part, 128), part)
        grad = FF ** (-0.5) * jnp.dot(
            left_ref[...], slots_ref[:, columns], preferred_element_type=jnp.float32
        )
        out[...] = adam(grad, first_ref[:, columns], second_ref[:, columns], theta_ref[:, columns])


def near_body(n_dp, n_island, slots_ref, left_ref, theta_ref, first_ref, second_ref, own_ref, *outs):
    island, data = lax.axis_index("island"), lax.axis_index("dp")
    part = theta_ref.shape[1] // n_island
    length = slots_ref.shape[0] // n_dp
    hidden = FF ** (-0.5) * lax.dot_general(
        theta_ref[...],
        slots_ref[...],
        (((1,), (1,)), ((), ())),
        preferred_element_type=jnp.float32,
    )
    hidden = hidden.astype(jnp.bfloat16)
    for shift, out in enumerate(outs):
        for group in range(n_dp):

            @pl.when(lax.rem(data + shift, n_dp) == group)
            def _():
                out[...] = hidden[:, group * length : (group + 1) * length]

    columns = pl.ds(pl.multiple_of(island * part, 128), part)
    grad = FF ** (-0.5) * jnp.dot(
        left_ref[...], slots_ref[:, columns], preferred_element_type=jnp.float32
    )
    own_ref[...] = adam(grad, first_ref[:, columns], second_ref[:, columns], theta_ref[:, columns])


def outer_body(n_island, anchor_ref, momentum_ref, *refs):
    thetas, (anchor_out, momentum_out) = refs[:n_island], refs[n_island:]
    total = thetas[0][...].astype(jnp.float32)
    for theta in thetas[1:]:
        total = total + theta[...].astype(jnp.float32)
    anchor = anchor_ref[...]
    mean_delta = anchor - total * (1.0 / n_island)
    momentum_new = outer_beta * momentum_ref[...] + mean_delta
    momentum_out[...] = momentum_new
    anchor_out[...] = anchor - outer_rate * (mean_delta + outer_beta * momentum_new)


def hidden_body(n_dp, *refs):
    parts, out_ref, scratch = refs[:n_dp], refs[n_dp], refs[n_dp + 1]
    data = lax.axis_index("dp")
    units = parts[0].shape[0]
    for shift, part in enumerate(parts):
        row = pl.multiple_of(wrap(data - shift, n_dp) * units, 8)
        scratch[pl.ds(row, units), :] = part[...].astype(jnp.float32)
    out_ref[...] = scratch[...].T.astype(jnp.bfloat16)


def call(body, out_shape, ins, name, scratch=()):
    return pl.pallas_call(
        body,
        out_shape=out_shape,
        in_specs=[VMEM] * len(ins),
        out_specs=[VMEM] * len(out_shape),
        scratch_shapes=list(scratch),
        compiler_params=PARAMS,
        name=name,
    )(*ins)


def per_device(
    theta,
    first_moment,
    second_moment,
    anchor,
    momentum,
    cotangent,
    weights,
    expert_ids,
    expert_counts,
    hidden_saved,
):
    n_island, n_dp, n_expert = (lax.axis_size(name) for name in ("island", "dp", "expert"))
    pairs = n_expert // 2
    units, width = theta.shape[2:]
    length, full_units = hidden_saved.shape[3:]
    part = width // n_island

    def ring(value, name, size, shift):
        return lax.ppermute(value, name, [(k, (k + shift) % size) for k in range(size)])

    saved = hidden_saved.reshape(length, full_units)
    saved_all = [saved] + [ring(saved, "dp", n_dp, shift) for shift in range(1, n_dp)]

    packed = pack_rows(cotangent, weights, expert_ids, expert_counts)
    blocks = [packed[0]]
    for k in range(1, pairs):
        perm = [(2 * z + c, 2 * ((z + k) % pairs) + c) for z in range(pairs) for c in range(2)]
        blocks.append(lax.ppermute(packed[k], "expert", perm))
    mine = jnp.concatenate(blocks, axis=0)
    swap = [(j, j ^ 1) for j in range(n_expert)]
    quarters = []
    for shift in range(n_dp):
        value = mine if shift == 0 else ring(mine, "dp", n_dp, shift)
        quarters += [value, lax.ppermute(value, "expert", swap)]

    local_theta, local_first, local_second = (
        value.reshape(units, width) for value in (theta, first_moment, second_moment)
    )
    slots_type = jax.ShapeDtypeStruct((n_dp * length, width), jnp.bfloat16)
    left_type = jax.ShapeDtypeStruct((units, n_dp * length), jnp.bfloat16)
    theta_type = jax.ShapeDtypeStruct((units, part), jnp.bfloat16)
    hidden_type = jax.ShapeDtypeStruct((units, length), jnp.bfloat16)
    *far, slots, left = call(
        functools.partial(far_body, n_dp, n_island, pairs),
        [theta_type] * (n_island - 1) + [slots_type, left_type],
        quarters + saved_all + [local_theta, local_first, local_second],
        "far_update",
        [pltpu.VMEM((full_units, length), jnp.float32)],
    )
    arrived = [ring(value, "island", n_island, shift + 1) for shift, value in enumerate(far)]
    own, *hidden = call(
        functools.partial(near_body, n_dp, n_island),
        [theta_type] + [hidden_type] * n_dp,
        [slots, left, local_theta, local_first, local_second],
        "near_update",
    )
    hidden = [hidden[0]] + [ring(hidden[s], "dp", n_dp, s) for s in range(1, n_dp)]
    (d_hidden,) = call(
        functools.partial(hidden_body, n_dp),
        [jax.ShapeDtypeStruct((length, full_units), jnp.bfloat16)],
        hidden,
        "join_hidden",
        [pltpu.VMEM((full_units, length), jnp.float32)],
    )
    outer_type = jax.ShapeDtypeStruct((units, part), jnp.float32)
    anchor_new, momentum_new = call(
        functools.partial(outer_body, n_island),
        [outer_type, outer_type],
        [anchor.reshape(units, part), momentum.reshape(units, part), own] + arrived,
        "outer_update",
    )
    return (
        anchor_new.reshape(anchor.shape),
        momentum_new.reshape(momentum.shape),
        d_hidden.reshape(hidden_saved.shape),
    )


def solution(mesh):
    return jax.shard_map(
        per_device,
        mesh=mesh,
        in_specs=(
            P("island", "expert", "dp", None),
            P("island", "expert", "dp", None),
            P("island", "expert", "dp", None),
            P("expert", "dp", "island"),
            P("expert", "dp", "island"),
            P(("island", "dp", "expert"), None),
            P(("island", "dp", "expert"), None),
            P(("island", "dp", "expert"), None),
            P(("island", "dp", "expert"), None),
            P("island", "dp", "expert", None, None),
        ),
        out_specs=(
            P("expert", "dp", "island"),
            P("expert", "dp", "island"),
            P("island", "dp", "expert", None, None),
        ),
        check_vma=False,
    )
```

```python
import functools

import jax
import jax.numpy as jnp
from jax import lax
from jax.experimental import pallas as pl
from jax.experimental.pallas import tpu as pltpu
from jax.sharding import PartitionSpec as P

FF = 768
CAP = 16

beta_one = 0.9
beta_two = 0.95
adam_epsilon = 1e-08
inner_rate = 0.1
decay_rate = 0.1
outer_beta = 0.9
outer_rate = 0.7

VMEM = pl.BlockSpec(memory_space=pltpu.VMEM)
HBM = pl.BlockSpec(memory_space=pltpu.HBM)
PARAMS = pltpu.CompilerParams(vmem_limit_bytes=48 * 1024 * 1024)


def wrap(value, size):
    return lax.rem(value + size, size)


def target(place, step, size):
    return place ^ step if size & (size - 1) == 0 else (place + step) % size


def source(place, step, size):
    return place ^ step if size & (size - 1) == 0 else (place - step) % size


def pack_body(experts, n_island, ids_hbm, weights_hbm, counts_hbm, cot_hbm, *refs):
    outs = refs[: 2 * experts]
    ids_ref, weights_ref, counts_ref, cot_ref, sems = refs[2 * experts :]
    copies = [
        pltpu.make_async_copy(src, dst, sems.at[index])
        for index, (src, dst) in enumerate(
            [
                (ids_hbm, ids_ref),
                (weights_hbm, weights_ref),
                (counts_hbm, counts_ref),
                (cot_hbm, cot_ref),
            ]
        )
    ]
    for copy in copies:
        copy.start()
    width, tokens = ids_ref.shape
    rows = experts * CAP
    island = lax.axis_index("island")
    place = lax.div(lax.axis_index("expert"), 2)
    step = lax.broadcasted_iota(jnp.int32, (experts, CAP, tokens), 0).reshape(rows, tokens)
    expert = target(place, step, experts)
    rank = lax.broadcasted_iota(jnp.int32, (experts, CAP, tokens), 1).reshape(rows, tokens)
    earlier = (
        lax.broadcasted_iota(jnp.int32, (tokens, tokens), 0)
        < lax.broadcasted_iota(jnp.int32, (tokens, tokens), 1)
    )
    earlier = jnp.where(earlier, 1.0, 0.0).astype(jnp.bfloat16)
    for copy in copies[:3]:
        copy.wait()
    named = jnp.zeros((rows, tokens), jnp.float32)
    weight = jnp.zeros((rows, tokens), jnp.float32)
    for slot in range(width):
        hit = ids_ref[slot : slot + 1, :] == expert
        named = jnp.where(hit, 1.0, named)
        weight = jnp.where(hit, weights_ref[slot : slot + 1, :], weight)
    limit = jnp.zeros((rows, tokens), jnp.int32)
    for index in range(experts):
        limit = jnp.where(expert == index, counts_ref[:, index : index + 1], limit)
    found = jnp.dot(named.astype(jnp.bfloat16), earlier, preferred_element_type=jnp.float32)
    found = found.astype(jnp.int32)
    picked = (named > 0.0) & (found < limit) & (found == rank)
    pick = jnp.where(picked, 1.0, 0.0)
    scale = jnp.sum(pick * weight, axis=1, keepdims=True)
    pick = pick.astype(jnp.bfloat16)
    copies[3].wait()
    part = cot_ref.shape[1] // n_island
    for shift in range(1, n_island + 1):
        columns = pl.ds(pl.multiple_of(lax.rem(island + shift, n_island) * part, 128), part)
        gathered = jnp.dot(pick, cot_ref[:, columns], preferred_element_type=jnp.float32)
        packed = (gathered * scale).astype(jnp.bfloat16)
        for index in range(experts):
            block = packed[index * CAP : (index + 1) * CAP]
            if shift < n_island:
                outs[index][:, (shift - 1) * part : shift * part] = block
            else:
                outs[experts + index][...] = block


def pack_rows(cotangent, weights, expert_ids, counts, n_island):
    experts = counts.shape[1]
    tokens, width = cotangent.shape
    part = width // n_island
    far = jax.ShapeDtypeStruct((CAP, width - part), jnp.bfloat16)
    near = jax.ShapeDtypeStruct((CAP, part), jnp.bfloat16)
    outs = pl.pallas_call(
        functools.partial(pack_body, experts, n_island),
        out_shape=[far] * experts + [near] * experts,
        in_specs=[HBM] * 4,
        out_specs=[VMEM] * (2 * experts),
        scratch_shapes=[
            pltpu.VMEM(expert_ids.shape[::-1], jnp.int32),
            pltpu.VMEM(weights.shape[::-1], jnp.float32),
            pltpu.VMEM(counts.shape, jnp.int32),
            pltpu.VMEM(cotangent.shape, jnp.bfloat16),
            pltpu.SemaphoreType.DMA((4,)),
        ],
        compiler_params=PARAMS,
        name="pack",
    )(expert_ids.T, weights.T, counts, cotangent)
    return outs[:experts], outs[experts:]


def adam(grad, first, second, theta):
    first_new = beta_one * first.astype(jnp.float32) + (1.0 - beta_one) * grad
    second_new = beta_two * second.astype(jnp.float32) + (1.0 - beta_two) * grad * grad
    wide = theta.astype(jnp.float32)
    step_size = first_new / (jnp.sqrt(second_new) + adam_epsilon) + decay_rate * wide
    return (wide - inner_rate * step_size).astype(jnp.bfloat16)


def stage_body(n_dp, *refs):
    saved = refs[:n_dp]
    states = refs[n_dp : n_dp + 3]
    left_ref = refs[n_dp + 3]
    copied = refs[n_dp + 4 : n_dp + 7]
    scratch, sems = refs[n_dp + 7 :]
    copies = [
        pltpu.make_async_copy(src, dst, sems.at[index])
        for index, (src, dst) in enumerate(zip(states, copied))
    ]
    for copy in copies:
        copy.start()
    data = lax.axis_index("dp")
    units = left_ref.shape[0]
    length = scratch.shape[1]
    for shift in range(n_dp):
        scratch[...] = saved[shift][...].astype(jnp.float32).T
        own = scratch[pl.ds(pl.multiple_of(data * units, 8), units), :]
        column = pl.multiple_of(wrap(data - shift, n_dp) * length, 128)
        left_ref[:, pl.ds(column, length)] = own.astype(jnp.bfloat16)
    for copy in copies:
        copy.wait()


def gather_slots(n_dp, pairs, quarters, slots_ref):
    data, position = lax.axis_index("dp"), lax.axis_index("expert")
    core = lax.rem(position, 2)
    place = lax.div(position, 2)
    length = 2 * pairs * CAP
    for shift in range(n_dp):
        group = wrap(data - shift, n_dp)
        for flip in range(2):
            side = core if flip == 0 else 1 - core
            block = quarters[2 * shift + flip]
            for k in range(pairs):
                row = group * length + (2 * source(place, k, pairs) + side) * CAP
                row = pl.multiple_of(row, CAP)
                slots_ref[pl.ds(row, CAP), :] = block[k * CAP : (k + 1) * CAP, :]


def update(left, slots, state_refs, columns):
    grad = FF ** (-0.5) * jnp.dot(left, slots, preferred_element_type=jnp.float32)
    theta, first, second = (ref[:, columns] for ref in state_refs)
    return adam(grad, first, second, theta)


def far_body(n_dp, n_island, pairs, *refs):
    quarters = refs[: 2 * n_dp]
    left_ref, *state_refs = refs[2 * n_dp : 2 * n_dp + 4]
    *outs, slots_ref = refs[2 * n_dp + 4 :]
    gather_slots(n_dp, pairs, quarters, slots_ref)
    island = lax.axis_index("island")
    part = outs[0].shape[1]
    for shift, out in enumerate(outs):
        column = pl.multiple_of(lax.rem(island + shift + 1, n_island) * part, 128)
        slots = slots_ref[:, shift * part : (shift + 1) * part]
        out[...] = update(left_ref[...], slots, state_refs, pl.ds(column, part))


def hidden_body(n_dp, n_island, pairs, *refs):
    quarters = refs[: 2 * n_dp]
    far_ref, theta_ref, *outs, slots_ref = refs[2 * n_dp :]
    gather_slots(n_dp, pairs, quarters, slots_ref)
    island, data = lax.axis_index("island"), lax.axis_index("dp")
    part = slots_ref.shape[1]
    length = slots_ref.shape[0] // n_dp
    total = None
    for shift in range(1, n_island + 1):
        column = pl.multiple_of(lax.rem(island + shift, n_island) * part, 128)
        slots = slots_ref if shift == n_island else far_ref.at[:, (shift - 1) * part : shift * part]
        value = lax.dot_general(
            theta_ref[:, pl.ds(column, part)],
            slots[...],
            (((1,), (1,)), ((), ())),
            preferred_element_type=jnp.float32,
        )
        total = value if total is None else total + value
    hidden = (FF ** (-0.5) * total).astype(jnp.bfloat16)
    for shift, out in enumerate(outs):
        for group in range(n_dp):

            @pl.when(lax.rem(data + shift, n_dp) == group)
            def _():
                out[...] = hidden[:, group * length : (group + 1) * length]


def near_body(slots_ref, left_ref, *refs):
    *state_refs, own_ref = refs
    part = slots_ref.shape[1]
    columns = pl.ds(pl.multiple_of(lax.axis_index("island") * part, 128), part)
    own_ref[...] = update(left_ref[...], slots_ref[...], state_refs, columns)


def outer_body(n_island, anchor_ref, momentum_ref, *refs):
    thetas = refs[:n_island]
    outs = refs[n_island : n_island + 2]
    *results, sems = refs[n_island + 2 :]
    rows = anchor_ref.shape[0]
    parts = 4 if rows % 32 == 0 else 1
    copies = []
    for part in range(parts):
        at = pl.ds(part * (rows // parts), rows // parts)
        total = thetas[0][at, :].astype(jnp.float32)
        for theta in thetas[1:]:
            total = total + theta[at, :].astype(jnp.float32)
        anchor = anchor_ref[at, :]
        mean_delta = anchor - total * (1.0 / n_island)
        momentum_new = outer_beta * momentum_ref[at, :] + mean_delta
        results[1][at, :] = momentum_new
        results[0][at, :] = anchor - outer_rate * (mean_delta + outer_beta * momentum_new)
        for index in range(2):
            copies.append(
                pltpu.make_async_copy(
                    results[index].at[at, :], outs[index].at[at, :], sems.at[index, part]
                )
            )
            copies[-1].start()
    for copy in copies:
        copy.wait()


def join_body(n_dp, *refs):
    parts, out_ref, scratch = refs[:n_dp], refs[n_dp], refs[n_dp + 1]
    data = lax.axis_index("dp")
    units = parts[0].shape[0]
    for shift, part in enumerate(parts):
        row = pl.multiple_of(wrap(data - shift, n_dp) * units, 8)
        scratch[pl.ds(row, units), :] = part[...].astype(jnp.float32)
    out_ref[...] = scratch[...].T.astype(jnp.bfloat16)


def call(body, out_shape, ins, name, scratch=(), in_specs=None, out_specs=None):
    return pl.pallas_call(
        body,
        out_shape=out_shape,
        in_specs=in_specs or [VMEM] * len(ins),
        out_specs=out_specs or [VMEM] * len(out_shape),
        scratch_shapes=list(scratch),
        compiler_params=PARAMS,
        name=name,
    )(*ins)


def per_device(
    theta,
    first_moment,
    second_moment,
    anchor,
    momentum,
    cotangent,
    weights,
    expert_ids,
    expert_counts,
    hidden_saved,
):
    n_island, n_dp, n_expert = (lax.axis_size(name) for name in ("island", "dp", "expert"))
    pairs = n_expert // 2
    units, width = theta.shape[2:]
    length, full_units = hidden_saved.shape[3:]
    part = width // n_island
    bf16 = functools.partial(jax.ShapeDtypeStruct, dtype=jnp.bfloat16)

    def ring(value, name, size, shift):
        return lax.ppermute(value, name, [(k, (k + shift) % size) for k in range(size)])

    def spread(blocks):
        arrived = {0: blocks[0]}
        for k in reversed(range(1, pairs)):
            perm = [
                (2 * z + c, 2 * target(z, k, pairs) + c) for z in range(pairs) for c in range(2)
            ]
            arrived[k] = lax.ppermute(blocks[k], "expert", perm)
        mine = jnp.concatenate([arrived[k] for k in range(pairs)], axis=0)
        swap = [(j, j ^ 1) for j in range(n_expert)]
        quarters = []
        for shift in range(n_dp):
            value = mine if shift == 0 else ring(mine, "dp", n_dp, shift)
            quarters += [value, lax.ppermute(value, "expert", swap)]
        return quarters

    far_blocks, near_blocks = pack_rows(cotangent, weights, expert_ids, expert_counts, n_island)
    far_quarters = spread(far_blocks)
    near_quarters = spread(near_blocks)

    saved = hidden_saved.reshape(length, full_units)
    saved_all = [saved] + [ring(saved, "dp", n_dp, shift) for shift in range(1, n_dp)]
    states = [value.reshape(units, width) for value in (theta, first_moment, second_moment)]
    left, *states = call(
        functools.partial(stage_body, n_dp),
        [bf16((units, n_dp * length))] + [bf16((units, width))] * 3,
        saved_all + states,
        "stage",
        [pltpu.VMEM((full_units, length), jnp.float32), pltpu.SemaphoreType.DMA((3,))],
        in_specs=[VMEM] * n_dp + [HBM] * 3,
    )
    *far, far_slots = call(
        functools.partial(far_body, n_dp, n_island, pairs),
        [bf16((units, part))] * (n_island - 1) + [bf16((n_dp * length, width - part))],
        far_quarters + [left] + states,
        "far_update",
    )
    arrived = [ring(value, "island", n_island, shift + 1) for shift, value in enumerate(far)]
    *hidden, near_slots = call(
        functools.partial(hidden_body, n_dp, n_island, pairs),
        [bf16((units, length))] * n_dp + [bf16((n_dp * length, part))],
        near_quarters + [far_slots, states[0]],
        "hidden_grad",
    )
    hidden = [hidden[0]] + [ring(hidden[s], "dp", n_dp, s) for s in range(1, n_dp)]
    (own,) = call(near_body, [bf16((units, part))], [near_slots, left] + states, "near_update")
    (d_hidden,) = call(
        functools.partial(join_body, n_dp),
        [bf16((length, full_units))],
        hidden,
        "join_hidden",
        [pltpu.VMEM((full_units, length), jnp.float32)],
    )
    outer_type = jax.ShapeDtypeStruct((units, part), jnp.float32)
    anchor_new, momentum_new = call(
        functools.partial(outer_body, n_island),
        [outer_type, outer_type],
        [anchor.reshape(units, part), momentum.reshape(units, part), own] + arrived,
        "outer_update",
        [pltpu.VMEM((units, part), jnp.float32)] * 2 + [pltpu.SemaphoreType.DMA((2, 4))],
        out_specs=[HBM, HBM],
    )
    return (
        anchor_new.reshape(anchor.shape),
        momentum_new.reshape(momentum.shape),
        d_hidden.reshape(hidden_saved.shape),
    )


def solution(mesh):
    return jax.shard_map(
        per_device,
        mesh=mesh,
        in_specs=(
            P("island", "expert", "dp", None),
            P("island", "expert", "dp", None),
            P("island", "expert", "dp", None),
            P("expert", "dp", "island"),
            P("expert", "dp", "island"),
            P(("island", "dp", "expert"), None),
            P(("island", "dp", "expert"), None),
            P(("island", "dp", "expert"), None),
            P(("island", "dp", "expert"), None),
            P("island", "dp", "expert", None, None),
        ),
        out_specs=(
            P("expert", "dp", "island"),
            P("expert", "dp", "island"),
            P("island", "dp", "expert", None, None),
        ),
        check_vma=False,
    )
```

```python
import functools

import jax
import jax.numpy as jnp
from jax import lax
from jax.experimental import pallas as pl
from jax.experimental.pallas import tpu as pltpu
from jax.sharding import PartitionSpec as P

FF = 768
CAP = 16

beta_one = 0.9
beta_two = 0.95
adam_epsilon = 1e-08
inner_rate = 0.1
decay_rate = 0.1
outer_beta = 0.9
outer_rate = 0.7

VMEM = pl.BlockSpec(memory_space=pltpu.VMEM)
HBM = pl.BlockSpec(memory_space=pltpu.HBM)
PARAMS = pltpu.CompilerParams(vmem_limit_bytes=48 * 1024 * 1024)


def in_hbm(value):
    return pltpu.with_memory_space_constraint(value, pltpu.HBM)


def wrap(value, size):
    return lax.rem(value + size, size)


def target(place, step, size):
    return place ^ step if size & (size - 1) == 0 else (place + step) % size


def source(place, step, size):
    return place ^ step if size & (size - 1) == 0 else (place - step) % size


def pack_body(experts, n_island, ids_hbm, weights_hbm, counts_hbm, cot_hbm, *refs):
    outs = refs[:experts]
    ids_ref, weights_ref, counts_ref, cot_ref, sems = refs[experts:]
    copies = [
        pltpu.make_async_copy(src, dst, sems.at[index])
        for index, (src, dst) in enumerate(
            [
                (ids_hbm, ids_ref),
                (weights_hbm, weights_ref),
                (counts_hbm, counts_ref),
                (cot_hbm, cot_ref),
            ]
        )
    ]
    for copy in copies:
        copy.start()
    width, tokens = ids_ref.shape
    rows = experts * CAP
    island = lax.axis_index("island")
    place = lax.div(lax.axis_index("expert"), 2)
    step = lax.broadcasted_iota(jnp.int32, (experts, CAP, tokens), 0).reshape(rows, tokens)
    expert = target(place, step, experts)
    rank = lax.broadcasted_iota(jnp.int32, (experts, CAP, tokens), 1).reshape(rows, tokens)
    earlier = (
        lax.broadcasted_iota(jnp.int32, (tokens, tokens), 0)
        < lax.broadcasted_iota(jnp.int32, (tokens, tokens), 1)
    )
    earlier = jnp.where(earlier, 1.0, 0.0).astype(jnp.bfloat16)
    for copy in copies[:3]:
        copy.wait()
    named = jnp.zeros((rows, tokens), jnp.float32)
    weight = jnp.zeros((rows, tokens), jnp.float32)
    for slot in range(width):
        hit = ids_ref[slot : slot + 1, :] == expert
        named = jnp.where(hit, 1.0, named)
        weight = jnp.where(hit, weights_ref[slot : slot + 1, :], weight)
    limit = jnp.zeros((rows, tokens), jnp.int32)
    for index in range(experts):
        limit = jnp.where(expert == index, counts_ref[:, index : index + 1], limit)
    found = jnp.dot(named.astype(jnp.bfloat16), earlier, preferred_element_type=jnp.float32)
    found = found.astype(jnp.int32)
    picked = (named > 0.0) & (found < limit) & (found == rank)
    pick = jnp.where(picked, 1.0, 0.0)
    scale = jnp.sum(pick * weight, axis=1, keepdims=True)
    pick = pick.astype(jnp.bfloat16)
    copies[3].wait()
    part = cot_ref.shape[1] // n_island
    for shift in range(1, n_island + 1):
        columns = pl.ds(pl.multiple_of(lax.rem(island + shift, n_island) * part, 128), part)
        gathered = jnp.dot(pick, cot_ref[:, columns], preferred_element_type=jnp.float32)
        packed = (gathered * scale).astype(jnp.bfloat16)
        for index, out in enumerate(outs):
            block = packed[index * CAP : (index + 1) * CAP]
            out[:, (shift - 1) * part : shift * part] = block


def pack_rows(cotangent, weights, expert_ids, counts, n_island):
    experts = counts.shape[1]
    ins = [expert_ids.T, weights.T, counts, cotangent]
    return pl.pallas_call(
        functools.partial(pack_body, experts, n_island),
        out_shape=[jax.ShapeDtypeStruct((CAP, cotangent.shape[1]), jnp.bfloat16)] * experts,
        in_specs=[HBM] * 4,
        out_specs=[VMEM] * experts,
        scratch_shapes=[
            pltpu.VMEM(expert_ids.shape[::-1], jnp.int32),
            pltpu.VMEM(weights.shape[::-1], jnp.float32),
            pltpu.VMEM(counts.shape, jnp.int32),
            pltpu.VMEM(cotangent.shape, jnp.bfloat16),
            pltpu.SemaphoreType.DMA((4,)),
        ],
        compiler_params=PARAMS,
        name="pack",
    )(*[in_hbm(value) for value in ins])


def adam(grad, first, second, theta):
    first_new = beta_one * first.astype(jnp.float32) + (1.0 - beta_one) * grad
    second_new = beta_two * second.astype(jnp.float32) + (1.0 - beta_two) * grad * grad
    wide = theta.astype(jnp.float32)
    step_size = first_new / (jnp.sqrt(second_new) + adam_epsilon) + decay_rate * wide
    return (wide - inner_rate * step_size).astype(jnp.bfloat16)


def assemble_body(pairs, *refs):
    blocks, (far_ref, near_ref, mine_ref) = refs[:pairs], refs[-3:]
    split = far_ref.shape[1]
    for index, block in enumerate(blocks):
        rows = slice(index * CAP, (index + 1) * CAP)
        value = block[...]
        far_ref[rows, :] = value[:, :split]
        near_ref[rows, :] = value[:, split:]
        mine_ref[rows, :] = value


def stage_body(*refs):
    states, copied, sems = refs[:3], refs[4:7], refs[7]
    copies = [
        pltpu.make_async_copy(src, dst, sems.at[index])
        for index, (src, dst) in enumerate(zip(states, copied))
    ]
    for copy in copies:
        copy.start()
    for copy in copies:
        copy.wait()


def left_body(n_dp, *refs):
    saved, left_ref, scratch = refs[:n_dp], refs[n_dp], refs[n_dp + 1]
    data = lax.axis_index("dp")
    units = left_ref.shape[0]
    length = scratch.shape[1]
    for shift in range(n_dp):
        scratch[...] = saved[shift][...].astype(jnp.float32).T
        own = scratch[pl.ds(pl.multiple_of(data * units, 8), units), :]
        column = pl.multiple_of(wrap(data - shift, n_dp) * length, 128)
        left_ref[:, pl.ds(column, length)] = own.astype(jnp.bfloat16)


def gather_slots(n_dp, pairs, quarters, slots_ref, first):
    data, position = lax.axis_index("dp"), lax.axis_index("expert")
    core = lax.rem(position, 2)
    place = lax.div(position, 2)
    length = 2 * pairs * CAP
    for shift in range(n_dp):
        group = wrap(data - shift, n_dp)
        for flip in range(2):
            side = core if flip == 0 else 1 - core
            block = quarters[2 * shift + flip]
            columns = slice(first, first + slots_ref.shape[1]) if shift == 0 else slice(None)
            for k in range(pairs):
                at = (pairs - 1 - k) * CAP
                row = group * length + (2 * source(place, k, pairs) + side) * CAP
                row = pl.multiple_of(row, CAP)
                slots_ref[pl.ds(row, CAP), :] = block[at : at + CAP, columns]


def update(left, slots, state_refs, columns):
    grad = FF ** (-0.5) * jnp.dot(left, slots, preferred_element_type=jnp.float32)
    theta, first, second = (ref[:, columns] for ref in state_refs)
    return adam(grad, first, second, theta)


def far_body(n_dp, n_island, pairs, *refs):
    quarters = refs[: 2 * n_dp]
    left_ref, *state_refs = refs[2 * n_dp : 2 * n_dp + 4]
    *outs, slots_ref = refs[3 * n_dp + 3 :]
    gather_slots(n_dp, pairs, quarters, slots_ref, 0)
    island = lax.axis_index("island")
    part = outs[0].shape[1]
    for shift, out in enumerate(outs):
        column = pl.multiple_of(lax.rem(island + shift + 1, n_island) * part, 128)
        slots = slots_ref[:, shift * part : (shift + 1) * part]
        out[...] = update(left_ref[...], slots, state_refs, pl.ds(column, part))


def hidden_body(n_dp, n_island, pairs, *refs):
    quarters = refs[: 2 * n_dp]
    far_ref, theta_ref, *outs, slots_ref = refs[2 * n_dp :]
    gather_slots(n_dp, pairs, quarters, slots_ref, far_ref.shape[1])
    island, data = lax.axis_index("island"), lax.axis_index("dp")
    part = slots_ref.shape[1]
    length = slots_ref.shape[0] // n_dp
    total = None
    for shift in range(1, n_island + 1):
        column = pl.multiple_of(lax.rem(island + shift, n_island) * part, 128)
        slots = slots_ref if shift == n_island else far_ref.at[:, (shift - 1) * part : shift * part]
        value = lax.dot_general(
            theta_ref[:, pl.ds(column, part)],
            slots[...],
            (((1,), (1,)), ((), ())),
            preferred_element_type=jnp.float32,
        )
        total = value if total is None else total + value
    hidden = (FF ** (-0.5) * total).astype(jnp.bfloat16)
    for shift, out in enumerate(outs):
        for group in range(n_dp):

            @pl.when(lax.rem(data + shift, n_dp) == group)
            def _():
                out[...] = hidden[:, group * length : (group + 1) * length]


def near_body(slots_ref, left_ref, *refs):
    *state_refs, own_ref = refs
    part = slots_ref.shape[1]
    columns = pl.ds(pl.multiple_of(lax.axis_index("island") * part, 128), part)
    own_ref[...] = update(left_ref[...], slots_ref[...], state_refs, columns)


def outer_body(n_island, anchor_ref, momentum_ref, *refs):
    thetas = refs[:n_island]
    outs = refs[n_island : n_island + 2]
    *results, sems = refs[n_island + 2 :]
    rows = anchor_ref.shape[0]
    parts = 4 if rows % 32 == 0 else 1
    copies = []
    for part in range(parts):
        at = pl.ds(part * (rows // parts), rows // parts)
        total = thetas[0][at, :].astype(jnp.float32)
        for theta in thetas[1:]:
            total = total + theta[at, :].astype(jnp.float32)
        anchor = anchor_ref[at, :]
        mean_delta = anchor - total * (1.0 / n_island)
        momentum_new = outer_beta * momentum_ref[at, :] + mean_delta
        results[1][at, :] = momentum_new
        results[0][at, :] = anchor - outer_rate * (mean_delta + outer_beta * momentum_new)
        for index in range(2):
            copies.append(
                pltpu.make_async_copy(
                    results[index].at[at, :], outs[index].at[at, :], sems.at[index, part]
                )
            )
            copies[-1].start()
    for copy in copies:
        copy.wait()


def join_body(n_dp, *refs):
    parts, out_ref, scratch = refs[:n_dp], refs[n_dp], refs[n_dp + 1]
    data = lax.axis_index("dp")
    units = parts[0].shape[0]
    for shift, part in enumerate(parts):
        row = pl.multiple_of(wrap(data - shift, n_dp) * units, 8)
        scratch[pl.ds(row, units), :] = part[...].astype(jnp.float32)
    out_ref[...] = scratch[...].T.astype(jnp.bfloat16)


def call(body, out_shape, ins, name, scratch=(), in_specs=None, out_specs=None):
    return pl.pallas_call(
        body,
        out_shape=out_shape,
        in_specs=in_specs or [VMEM] * len(ins),
        out_specs=out_specs or [VMEM] * len(out_shape),
        scratch_shapes=list(scratch),
        compiler_params=PARAMS,
        name=name,
    )(*ins)


def per_device(
    theta,
    first_moment,
    second_moment,
    anchor,
    momentum,
    cotangent,
    weights,
    expert_ids,
    expert_counts,
    hidden_saved,
):
    n_island, n_dp, n_expert = (lax.axis_size(name) for name in ("island", "dp", "expert"))
    pairs = n_expert // 2
    units, width = theta.shape[2:]
    length, full_units = hidden_saved.shape[3:]
    part = width // n_island
    bf16 = functools.partial(jax.ShapeDtypeStruct, dtype=jnp.bfloat16)

    def ring(value, name, size, shift):
        return lax.ppermute(value, name, [(k, (k + shift) % size) for k in range(size)])

    blocks = list(pack_rows(cotangent, weights, expert_ids, expert_counts, n_island))
    arrived = []
    for k in reversed(range(1, pairs)):
        perm = [(2 * z + c, 2 * target(z, k, pairs) + c) for z in range(pairs) for c in range(2)]
        arrived.append(lax.ppermute(blocks[k], "expert", perm))
    saved = hidden_saved.reshape(length, full_units)
    saved_all = [saved] + [ring(saved, "dp", n_dp, shift) for shift in range(1, n_dp)]
    arrived.append(blocks[0])
    far_mine, near_mine, mine = call(
        functools.partial(assemble_body, pairs),
        [bf16((pairs * CAP, columns)) for columns in (width - part, part, width)],
        arrived + saved_all[1:],
        "assemble",
    )
    swap = [(j, j ^ 1) for j in range(n_expert)]
    other = lax.ppermute(mine, "expert", swap)

    def spread(chunk):
        quarters = [mine, other]
        for shift in range(1, n_dp):
            value = ring(chunk, "dp", n_dp, shift)
            quarters += [value, lax.ppermute(value, "expert", swap)]
        return quarters

    far_quarters = spread(far_mine)
    near_quarters = spread(near_mine)
    near_rows = near_quarters[2::2]

    (left,) = call(
        functools.partial(left_body, n_dp),
        [bf16((units, n_dp * length))],
        saved_all,
        "left",
        [pltpu.VMEM((full_units, length), jnp.float32)],
    )
    states = [in_hbm(value.reshape(units, width)) for value in (theta, first_moment, second_moment)]
    states = call(
        stage_body,
        [bf16((units, width))] * 3,
        states + [blocks[0]],
        "stage",
        [pltpu.SemaphoreType.DMA((3,))],
        in_specs=[HBM] * 3 + [VMEM],
    )
    *far, far_slots = call(
        functools.partial(far_body, n_dp, n_island, pairs),
        [bf16((units, part))] * (n_island - 1) + [bf16((n_dp * length, width - part))],
        far_quarters + [left, *states] + near_rows,
        "far_update",
    )
    arrived = [ring(value, "island", n_island, shift + 1) for shift, value in enumerate(far)]
    *hidden, near_slots = call(
        functools.partial(hidden_body, n_dp, n_island, pairs),
        [bf16((units, length))] * n_dp + [bf16((n_dp * length, part))],
        near_quarters + [far_slots, states[0]],
        "hidden_grad",
    )
    hidden = [hidden[0]] + [ring(hidden[s], "dp", n_dp, s) for s in range(1, n_dp)]
    (own,) = call(near_body, [bf16((units, part))], [near_slots, left, *states], "near_update")
    (d_hidden,) = call(
        functools.partial(join_body, n_dp),
        [bf16((length, full_units))],
        hidden,
        "join_hidden",
        [pltpu.VMEM((full_units, length), jnp.float32)],
    )
    outer_type = jax.ShapeDtypeStruct((units, part), jnp.float32)
    anchor_new, momentum_new = call(
        functools.partial(outer_body, n_island),
        [outer_type, outer_type],
        [anchor.reshape(units, part), momentum.reshape(units, part), own] + arrived,
        "outer_update",
        [pltpu.VMEM((units, part), jnp.float32)] * 2 + [pltpu.SemaphoreType.DMA((2, 4))],
        out_specs=[HBM, HBM],
    )
    return (
        anchor_new.reshape(anchor.shape),
        momentum_new.reshape(momentum.shape),
        d_hidden.reshape(hidden_saved.shape),
    )


def solution(mesh):
    return jax.shard_map(
        per_device,
        mesh=mesh,
        in_specs=(
            P("island", "expert", "dp", None),
            P("island", "expert", "dp", None),
            P("island", "expert", "dp", None),
            P("expert", "dp", "island"),
            P("expert", "dp", "island"),
            P(("island", "dp", "expert"), None),
            P(("island", "dp", "expert"), None),
            P(("island", "dp", "expert"), None),
            P(("island", "dp", "expert"), None),
            P("island", "dp", "expert", None, None),
        ),
        out_specs=(
            P("expert", "dp", "island"),
            P("expert", "dp", "island"),
            P("island", "dp", "expert", None, None),
        ),
        check_vma=False,
    )
```

```python
import functools

import jax
import jax.numpy as jnp
from jax import lax
from jax.experimental import pallas as pl
from jax.experimental.pallas import tpu as pltpu
from jax.sharding import PartitionSpec as P

FF = 768
CAP = 16

beta_one = 0.9
beta_two = 0.95
adam_epsilon = 1e-08
inner_rate = 0.1
decay_rate = 0.1
outer_beta = 0.9
outer_rate = 0.7

VMEM = pl.BlockSpec(memory_space=pltpu.VMEM)
HBM = pl.BlockSpec(memory_space=pltpu.HBM)
PARAMS = pltpu.CompilerParams(vmem_limit_bytes=48 * 1024 * 1024)


def in_hbm(value):
    return pltpu.with_memory_space_constraint(value, pltpu.HBM)


def wrap(value, size):
    return lax.rem(value + size, size)


def target(place, step, size):
    return place ^ step if size & (size - 1) == 0 else (place + step) % size


def source(place, step, size):
    return place ^ step if size & (size - 1) == 0 else (place - step) % size


def pack_body(experts, n_island, ids_hbm, weights_hbm, counts_hbm, cot_hbm, *refs):
    outs = refs[: 2 * experts]
    ids_ref, weights_ref, counts_ref, cot_ref, sems = refs[2 * experts :]
    copies = [
        pltpu.make_async_copy(src, dst, sems.at[index])
        for index, (src, dst) in enumerate(
            [
                (ids_hbm, ids_ref),
                (weights_hbm, weights_ref),
                (counts_hbm, counts_ref),
                (cot_hbm, cot_ref),
            ]
        )
    ]
    for copy in copies:
        copy.start()
    width, tokens = ids_ref.shape
    rows = experts * CAP
    island = lax.axis_index("island")
    place = lax.div(lax.axis_index("expert"), 2)
    step = lax.broadcasted_iota(jnp.int32, (experts, CAP, tokens), 0).reshape(rows, tokens)
    expert = target(place, step, experts)
    rank = lax.broadcasted_iota(jnp.int32, (experts, CAP, tokens), 1).reshape(rows, tokens)
    earlier = (
        lax.broadcasted_iota(jnp.int32, (tokens, tokens), 0)
        < lax.broadcasted_iota(jnp.int32, (tokens, tokens), 1)
    )
    earlier = jnp.where(earlier, 1.0, 0.0).astype(jnp.bfloat16)
    for copy in copies[:3]:
        copy.wait()
    named = jnp.zeros((rows, tokens), jnp.float32)
    weight = jnp.zeros((rows, tokens), jnp.float32)
    for slot in range(width):
        hit = ids_ref[slot : slot + 1, :] == expert
        named = jnp.where(hit, 1.0, named)
        weight = jnp.where(hit, weights_ref[slot : slot + 1, :], weight)
    limit = jnp.zeros((rows, tokens), jnp.int32)
    for index in range(experts):
        limit = jnp.where(expert == index, counts_ref[:, index : index + 1], limit)
    found = jnp.dot(named.astype(jnp.bfloat16), earlier, preferred_element_type=jnp.float32)
    found = found.astype(jnp.int32)
    picked = (named > 0.0) & (found < limit) & (found == rank)
    pick = jnp.where(picked, 1.0, 0.0)
    scale = jnp.sum(pick * weight, axis=1, keepdims=True)
    pick = pick.astype(jnp.bfloat16)
    copies[3].wait()
    part = cot_ref.shape[1] // n_island
    for shift in range(1, n_island + 1):
        columns = pl.ds(pl.multiple_of(lax.rem(island + shift, n_island) * part, 128), part)
        gathered = jnp.dot(pick, cot_ref[:, columns], preferred_element_type=jnp.float32)
        packed = (gathered * scale).astype(jnp.bfloat16)
        for index in range(experts):
            block = packed[index * CAP : (index + 1) * CAP]
            if shift < n_island:
                outs[index][:, (shift - 1) * part : shift * part] = block
            else:
                outs[experts + index][...] = block


def pack_rows(cotangent, weights, expert_ids, counts, n_island):
    experts = counts.shape[1]
    ins = [expert_ids.T, weights.T, counts, cotangent]
    width = cotangent.shape[1]
    part = width // n_island
    outs = [
        jax.ShapeDtypeStruct((CAP, columns), jnp.bfloat16)
        for columns in (width - part, part)
        for _ in range(experts)
    ]
    outs = pl.pallas_call(
        functools.partial(pack_body, experts, n_island),
        out_shape=outs,
        in_specs=[HBM] * 4,
        out_specs=[VMEM] * len(outs),
        scratch_shapes=[
            pltpu.VMEM(expert_ids.shape[::-1], jnp.int32),
            pltpu.VMEM(weights.shape[::-1], jnp.float32),
            pltpu.VMEM(counts.shape, jnp.int32),
            pltpu.VMEM(cotangent.shape, jnp.bfloat16),
            pltpu.SemaphoreType.DMA((4,)),
        ],
        compiler_params=PARAMS,
        name="pack",
    )(*[in_hbm(value) for value in ins])
    return outs[:experts], outs[experts:]


def adam(grad, first, second, theta):
    first_new = beta_one * first.astype(jnp.float32) + (1.0 - beta_one) * grad
    second_new = beta_two * second.astype(jnp.float32) + (1.0 - beta_two) * grad * grad
    wide = theta.astype(jnp.float32)
    step_size = first_new / (jnp.sqrt(second_new) + adam_epsilon) + decay_rate * wide
    return (wide - inner_rate * step_size).astype(jnp.bfloat16)


def assemble_body(pairs, *refs):
    out_ref = refs[-1]
    for index, block in enumerate(refs[:pairs]):
        out_ref[index * CAP : (index + 1) * CAP, :] = block[...]


def stage_body(*refs):
    states, copied, sems = refs[:3], refs[4:7], refs[7]
    copies = [
        pltpu.make_async_copy(src, dst, sems.at[index])
        for index, (src, dst) in enumerate(zip(states, copied))
    ]
    for copy in copies:
        copy.start()
    for copy in copies:
        copy.wait()


def left_body(n_dp, *refs):
    saved, left_ref, scratch = refs[:n_dp], refs[n_dp], refs[n_dp + 1]
    data = lax.axis_index("dp")
    units = left_ref.shape[0]
    length = scratch.shape[1]
    for shift in range(n_dp):
        scratch[...] = saved[shift][...].astype(jnp.float32).T
        own = scratch[pl.ds(pl.multiple_of(data * units, 8), units), :]
        column = pl.multiple_of(wrap(data - shift, n_dp) * length, 128)
        left_ref[:, pl.ds(column, length)] = own.astype(jnp.bfloat16)


def gather_slots(n_dp, pairs, quarters, slots_ref):
    data, position = lax.axis_index("dp"), lax.axis_index("expert")
    core = lax.rem(position, 2)
    place = lax.div(position, 2)
    length = 2 * pairs * CAP
    for shift in range(n_dp):
        group = wrap(data - shift, n_dp)
        for flip in range(2):
            side = core if flip == 0 else 1 - core
            block = quarters[2 * shift + flip]
            for k in range(pairs):
                at = (pairs - 1 - k) * CAP
                row = group * length + (2 * source(place, k, pairs) + side) * CAP
                row = pl.multiple_of(row, CAP)
                slots_ref[pl.ds(row, CAP), :] = block[at : at + CAP, :]


def update(left, slots, state_refs, columns):
    grad = FF ** (-0.5) * jnp.dot(left, slots, preferred_element_type=jnp.float32)
    theta, first, second = (ref[:, columns] for ref in state_refs)
    return adam(grad, first, second, theta)


def far_body(n_dp, n_island, pairs, *refs):
    quarters = refs[: 2 * n_dp]
    left_ref, *state_refs = refs[2 * n_dp : 2 * n_dp + 4]
    *outs, slots_ref = refs[2 * n_dp + 4 :]
    outs = outs[-(n_island - 1) :]
    gather_slots(n_dp, pairs, quarters, slots_ref)
    island = lax.axis_index("island")
    part = outs[0].shape[1]
    for shift, out in enumerate(outs):
        column = pl.multiple_of(lax.rem(island + shift + 1, n_island) * part, 128)
        slots = slots_ref[:, shift * part : (shift + 1) * part]
        out[...] = update(left_ref[...], slots, state_refs, pl.ds(column, part))


def hidden_body(n_dp, n_island, pairs, *refs):
    quarters = refs[: 2 * n_dp]
    far_ref, theta_ref, *outs, slots_ref = refs[2 * n_dp :]
    gather_slots(n_dp, pairs, quarters, slots_ref)
    island, data = lax.axis_index("island"), lax.axis_index("dp")
    part = slots_ref.shape[1]
    length = slots_ref.shape[0] // n_dp
    total = None
    for shift in range(1, n_island + 1):
        column = pl.multiple_of(lax.rem(island + shift, n_island) * part, 128)
        slots = slots_ref if shift == n_island else far_ref.at[:, (shift - 1) * part : shift * part]
        value = lax.dot_general(
            theta_ref[:, pl.ds(column, part)],
            slots[...],
            (((1,), (1,)), ((), ())),
            preferred_element_type=jnp.float32,
        )
        total = value if total is None else total + value
    hidden = (FF ** (-0.5) * total).astype(jnp.bfloat16)
    for shift, out in enumerate(outs):
        for group in range(n_dp):

            @pl.when(lax.rem(data + shift, n_dp) == group)
            def _():
                out[...] = hidden[:, group * length : (group + 1) * length]


def near_body(slots_ref, left_ref, *refs):
    *state_refs, own_ref = refs
    part = slots_ref.shape[1]
    columns = pl.ds(pl.multiple_of(lax.axis_index("island") * part, 128), part)
    own_ref[...] = update(left_ref[...], slots_ref[...], state_refs, columns)


def outer_body(n_island, anchor_ref, momentum_ref, *refs):
    thetas = refs[:n_island]
    outs = refs[n_island : n_island + 2]
    *results, sems = refs[n_island + 2 :]
    rows = anchor_ref.shape[0]
    parts = 4 if rows % 32 == 0 else 1
    copies = []
    for part in range(parts):
        at = pl.ds(part * (rows // parts), rows // parts)
        total = thetas[0][at, :].astype(jnp.float32)
        for theta in thetas[1:]:
            total = total + theta[at, :].astype(jnp.float32)
        anchor = anchor_ref[at, :]
        mean_delta = anchor - total * (1.0 / n_island)
        momentum_new = outer_beta * momentum_ref[at, :] + mean_delta
        results[1][at, :] = momentum_new
        results[0][at, :] = anchor - outer_rate * (mean_delta + outer_beta * momentum_new)
        for index in range(2):
            copies.append(
                pltpu.make_async_copy(
                    results[index].at[at, :], outs[index].at[at, :], sems.at[index, part]
                )
            )
            copies[-1].start()
    for copy in copies:
        copy.wait()


def join_body(n_dp, *refs):
    parts, out_ref, scratch = refs[:n_dp], refs[n_dp], refs[n_dp + 1]
    data = lax.axis_index("dp")
    units = parts[0].shape[0]
    for shift, part in enumerate(parts):
        row = pl.multiple_of(wrap(data - shift, n_dp) * units, 8)
        scratch[pl.ds(row, units), :] = part[...].astype(jnp.float32)
    out_ref[...] = scratch[...].T.astype(jnp.bfloat16)


def call(body, out_shape, ins, name, scratch=(), in_specs=None, out_specs=None):
    return pl.pallas_call(
        body,
        out_shape=out_shape,
        in_specs=in_specs or [VMEM] * len(ins),
        out_specs=out_specs or [VMEM] * len(out_shape),
        scratch_shapes=list(scratch),
        compiler_params=PARAMS,
        name=name,
    )(*ins)


def per_device(
    theta,
    first_moment,
    second_moment,
    anchor,
    momentum,
    cotangent,
    weights,
    expert_ids,
    expert_counts,
    hidden_saved,
):
    n_island, n_dp, n_expert = (lax.axis_size(name) for name in ("island", "dp", "expert"))
    pairs = n_expert // 2
    units, width = theta.shape[2:]
    length, full_units = hidden_saved.shape[3:]
    part = width // n_island
    bf16 = functools.partial(jax.ShapeDtypeStruct, dtype=jnp.bfloat16)

    def ring(value, name, size, shift):
        return lax.ppermute(value, name, [(k, (k + shift) % size) for k in range(size)])

    saved = hidden_saved.reshape(length, full_units)
    saved_all = [saved] + [ring(saved, "dp", n_dp, shift) for shift in range(1, n_dp)]
    far_blocks, near_blocks = pack_rows(cotangent, weights, expert_ids, expert_counts, n_island)
    states = [in_hbm(value.reshape(units, width)) for value in (theta, first_moment, second_moment)]
    states = call(
        stage_body,
        [bf16((units, width))] * 3,
        states + [far_blocks[0]],
        "stage",
        [pltpu.SemaphoreType.DMA((3,))],
        in_specs=[HBM] * 3 + [VMEM],
    )

    def spread(blocks, earlier):
        arrived = []
        for k in reversed(range(1, pairs)):
            perm = [
                (2 * z + c, 2 * target(z, k, pairs) + c) for z in range(pairs) for c in range(2)
            ]
            arrived.append(lax.ppermute(blocks[k], "expert", perm))
        if earlier:
            (mine,) = call(
                functools.partial(assemble_body, pairs),
                [bf16((pairs * CAP, blocks[0].shape[1]))],
                arrived + [blocks[0]] + earlier,
                "assemble",
            )
        else:
            mine = jnp.concatenate(arrived + [blocks[0]], axis=0)
        swap = [(j, j ^ 1) for j in range(n_expert)]
        quarters = []
        for shift in range(n_dp):
            value = mine if shift == 0 else ring(mine, "dp", n_dp, shift)
            quarters += [value, lax.ppermute(value, "expert", swap)]
        return quarters, arrived

    far_quarters, _ = spread(far_blocks, saved_all[1:] + list(states))
    near_quarters, near_arrived = spread(near_blocks, [])

    (left,) = call(
        functools.partial(left_body, n_dp),
        [bf16((units, n_dp * length))],
        saved_all,
        "left",
        [pltpu.VMEM((full_units, length), jnp.float32)],
    )
    *far, far_slots = call(
        functools.partial(far_body, n_dp, n_island, pairs),
        [bf16((units, part))] * (n_island - 1) + [bf16((n_dp * length, width - part))],
        far_quarters + [left, *states],
        "far_update",
    )
    arrived = [ring(value, "island", n_island, shift + 1) for shift, value in enumerate(far)]
    *hidden, near_slots = call(
        functools.partial(hidden_body, n_dp, n_island, pairs),
        [bf16((units, length))] * n_dp + [bf16((n_dp * length, part))],
        near_quarters + [far_slots, states[0]],
        "hidden_grad",
    )
    hidden = [hidden[0]] + [ring(hidden[s], "dp", n_dp, s) for s in range(1, n_dp)]
    (own,) = call(near_body, [bf16((units, part))], [near_slots, left, *states], "near_update")
    (d_hidden,) = call(
        functools.partial(join_body, n_dp),
        [bf16((length, full_units))],
        hidden,
        "join_hidden",
        [pltpu.VMEM((full_units, length), jnp.float32)],
    )
    outer_type = jax.ShapeDtypeStruct((units, part), jnp.float32)
    anchor_new, momentum_new = call(
        functools.partial(outer_body, n_island),
        [outer_type, outer_type],
        [anchor.reshape(units, part), momentum.reshape(units, part), own] + arrived,
        "outer_update",
        [pltpu.VMEM((units, part), jnp.float32)] * 2 + [pltpu.SemaphoreType.DMA((2, 4))],
        out_specs=[HBM, HBM],
    )
    return (
        anchor_new.reshape(anchor.shape),
        momentum_new.reshape(momentum.shape),
        d_hidden.reshape(hidden_saved.shape),
    )


def solution(mesh):
    return jax.shard_map(
        per_device,
        mesh=mesh,
        in_specs=(
            P("island", "expert", "dp", None),
            P("island", "expert", "dp", None),
            P("island", "expert", "dp", None),
            P("expert", "dp", "island"),
            P("expert", "dp", "island"),
            P(("island", "dp", "expert"), None),
            P(("island", "dp", "expert"), None),
            P(("island", "dp", "expert"), None),
            P(("island", "dp", "expert"), None),
            P("island", "dp", "expert", None, None),
        ),
        out_specs=(
            P("expert", "dp", "island"),
            P("expert", "dp", "island"),
            P("island", "dp", "expert", None, None),
        ),
        check_vma=False,
    )
```

```python
import functools

import jax
import jax.numpy as jnp
from jax import lax
from jax.experimental import pallas as pl
from jax.experimental.pallas import tpu as pltpu
from jax.sharding import PartitionSpec as P

FF = 768
CAP = 16

beta_one = 0.9
beta_two = 0.95
adam_epsilon = 1e-08
inner_rate = 0.1
decay_rate = 0.1
outer_beta = 0.9
outer_rate = 0.7

VMEM = pl.BlockSpec(memory_space=pltpu.VMEM)
HBM = pl.BlockSpec(memory_space=pltpu.HBM)
PARAMS = pltpu.CompilerParams(vmem_limit_bytes=48 * 1024 * 1024)


def in_hbm(value):
    return pltpu.with_memory_space_constraint(value, pltpu.HBM)


def wrap(value, size):
    return lax.rem(value + size, size)


def target(place, step, size):
    return place ^ step if size & (size - 1) == 0 else (place + step) % size


def source(place, step, size):
    return place ^ step if size & (size - 1) == 0 else (place - step) % size


def pack_body(experts, n_island, ids_hbm, weights_hbm, counts_hbm, cot_hbm, *refs):
    outs = refs[:experts]
    ids_ref, weights_ref, counts_ref, cot_ref, sems = refs[experts:]
    copies = [
        pltpu.make_async_copy(src, dst, sems.at[index])
        for index, (src, dst) in enumerate(
            [
                (ids_hbm, ids_ref),
                (weights_hbm, weights_ref),
                (counts_hbm, counts_ref),
                (cot_hbm, cot_ref),
            ]
        )
    ]
    for copy in copies:
        copy.start()
    width, tokens = ids_ref.shape
    rows = experts * CAP
    island = lax.axis_index("island")
    place = lax.div(lax.axis_index("expert"), 2)
    step = lax.broadcasted_iota(jnp.int32, (experts, CAP, tokens), 0).reshape(rows, tokens)
    expert = target(place, step, experts)
    rank = lax.broadcasted_iota(jnp.int32, (experts, CAP, tokens), 1).reshape(rows, tokens)
    earlier = (
        lax.broadcasted_iota(jnp.int32, (tokens, tokens), 0)
        < lax.broadcasted_iota(jnp.int32, (tokens, tokens), 1)
    )
    earlier = jnp.where(earlier, 1.0, 0.0).astype(jnp.bfloat16)
    for copy in copies[:3]:
        copy.wait()
    named = jnp.zeros((rows, tokens), jnp.float32)
    weight = jnp.zeros((rows, tokens), jnp.float32)
    for slot in range(width):
        hit = ids_ref[slot : slot + 1, :] == expert
        named = jnp.where(hit, 1.0, named)
        weight = jnp.where(hit, weights_ref[slot : slot + 1, :], weight)
    limit = jnp.zeros((rows, tokens), jnp.int32)
    for index in range(experts):
        limit = jnp.where(expert == index, counts_ref[:, index : index + 1], limit)
    found = jnp.dot(named.astype(jnp.bfloat16), earlier, preferred_element_type=jnp.float32)
    found = found.astype(jnp.int32)
    picked = (named > 0.0) & (found < limit) & (found == rank)
    pick = jnp.where(picked, 1.0, 0.0)
    scale = jnp.sum(pick * weight, axis=1, keepdims=True)
    pick = pick.astype(jnp.bfloat16)
    copies[3].wait()
    part = cot_ref.shape[1] // n_island
    for shift in range(1, n_island + 1):
        columns = pl.ds(pl.multiple_of(lax.rem(island + shift, n_island) * part, 128), part)
        gathered = jnp.dot(pick, cot_ref[:, columns], preferred_element_type=jnp.float32)
        packed = (gathered * scale).astype(jnp.bfloat16)
        for index, out in enumerate(outs):
            block = packed[index * CAP : (index + 1) * CAP]
            out[:, (shift - 1) * part : shift * part] = block


def pack_rows(cotangent, weights, expert_ids, counts, n_island):
    experts = counts.shape[1]
    ins = [expert_ids.T, weights.T, counts, cotangent]
    return pl.pallas_call(
        functools.partial(pack_body, experts, n_island),
        out_shape=[jax.ShapeDtypeStruct((CAP, cotangent.shape[1]), jnp.bfloat16)] * experts,
        in_specs=[HBM] * 4,
        out_specs=[VMEM] * experts,
        scratch_shapes=[
            pltpu.VMEM(expert_ids.shape[::-1], jnp.int32),
            pltpu.VMEM(weights.shape[::-1], jnp.float32),
            pltpu.VMEM(counts.shape, jnp.int32),
            pltpu.VMEM(cotangent.shape, jnp.bfloat16),
            pltpu.SemaphoreType.DMA((4,)),
        ],
        compiler_params=PARAMS,
        name="pack",
    )(*[in_hbm(value) for value in ins])


def adam(grad, first, second, theta):
    first_new = beta_one * first.astype(jnp.float32) + (1.0 - beta_one) * grad
    second_new = beta_two * second.astype(jnp.float32) + (1.0 - beta_two) * grad * grad
    wide = theta.astype(jnp.float32)
    step_size = first_new / (jnp.sqrt(second_new) + adam_epsilon) + decay_rate * wide
    return (wide - inner_rate * step_size).astype(jnp.bfloat16)


def assemble_body(pairs, *refs):
    blocks, (far_ref, near_ref, mine_ref) = refs[:pairs], refs[-3:]
    split = far_ref.shape[1]
    for index, block in enumerate(blocks):
        rows = slice(index * CAP, (index + 1) * CAP)
        value = block[...]
        far_ref[rows, :] = value[:, :split]
        near_ref[rows, :] = value[:, split:]
        mine_ref[rows, :] = value


def stage_body(*refs):
    states, copied, sems = refs[:3], refs[4:7], refs[7]
    copies = [
        pltpu.make_async_copy(src, dst, sems.at[index])
        for index, (src, dst) in enumerate(zip(states, copied))
    ]
    for copy in copies:
        copy.start()
    for copy in copies:
        copy.wait()


def split_body(n_dp, saved_ref, _, *refs):
    *outs, scratch = refs
    units = outs[0].shape[0]
    scratch[...] = saved_ref[...].astype(jnp.float32).T
    for shift, out in enumerate(outs):
        row = pl.multiple_of(lax.rem(lax.axis_index("dp") + shift, n_dp) * units, 8)
        out[...] = scratch[pl.ds(row, units), :].astype(jnp.bfloat16)


def gather_slots(n_dp, pairs, quarters, slots_ref, first):
    data, position = lax.axis_index("dp"), lax.axis_index("expert")
    core = lax.rem(position, 2)
    place = lax.div(position, 2)
    length = 2 * pairs * CAP
    for shift in range(n_dp):
        group = wrap(data - shift, n_dp)
        for flip in range(2):
            side = core if flip == 0 else 1 - core
            block = quarters[2 * shift + flip]
            columns = slice(first, first + slots_ref.shape[1]) if shift == 0 else slice(None)
            for k in range(pairs):
                at = (pairs - 1 - k) * CAP
                row = group * length + (2 * source(place, k, pairs) + side) * CAP
                row = pl.multiple_of(row, CAP)
                slots_ref[pl.ds(row, CAP), :] = block[at : at + CAP, columns]


def update(left, slots, state_refs, columns):
    grad = FF ** (-0.5) * jnp.dot(left, slots, preferred_element_type=jnp.float32)
    theta, first, second = (ref[:, columns] for ref in state_refs)
    return adam(grad, first, second, theta)


def far_body(n_dp, n_island, pairs, *refs):
    quarters = refs[: 2 * n_dp]
    saved = refs[2 * n_dp : 3 * n_dp]
    state_refs = refs[3 * n_dp : 3 * n_dp + 3]
    *outs, slots_ref, left_ref = refs[3 * n_dp + 3 :]
    length = saved[0].shape[1]
    for shift, value in enumerate(saved):
        column = pl.multiple_of(wrap(lax.axis_index("dp") - shift, n_dp) * length, 128)
        left_ref[:, pl.ds(column, length)] = value[...]
    gather_slots(n_dp, pairs, quarters, slots_ref, 0)
    island = lax.axis_index("island")
    part = outs[0].shape[1]
    for shift, out in enumerate(outs):
        column = pl.multiple_of(lax.rem(island + shift + 1, n_island) * part, 128)
        slots = slots_ref[:, shift * part : (shift + 1) * part]
        out[...] = update(left_ref[...], slots, state_refs, pl.ds(column, part))


def hidden_body(n_dp, n_island, pairs, *refs):
    quarters = refs[: 2 * n_dp]
    far_ref, theta_ref, *outs, slots_ref = refs[2 * n_dp :]
    gather_slots(n_dp, pairs, quarters, slots_ref, far_ref.shape[1])
    island, data = lax.axis_index("island"), lax.axis_index("dp")
    part = slots_ref.shape[1]
    length = slots_ref.shape[0] // n_dp
    total = None
    for shift in range(1, n_island + 1):
        column = pl.multiple_of(lax.rem(island + shift, n_island) * part, 128)
        slots = slots_ref if shift == n_island else far_ref.at[:, (shift - 1) * part : shift * part]
        value = lax.dot_general(
            theta_ref[:, pl.ds(column, part)],
            slots[...],
            (((1,), (1,)), ((), ())),
            preferred_element_type=jnp.float32,
        )
        total = value if total is None else total + value
    hidden = (FF ** (-0.5) * total).astype(jnp.bfloat16)
    for shift, out in enumerate(outs):
        for group in range(n_dp):

            @pl.when(lax.rem(data + shift, n_dp) == group)
            def _():
                out[...] = hidden[:, group * length : (group + 1) * length]


def near_body(slots_ref, left_ref, *refs):
    *state_refs, own_ref = refs
    part = slots_ref.shape[1]
    columns = pl.ds(pl.multiple_of(lax.axis_index("island") * part, 128), part)
    own_ref[...] = update(left_ref[...], slots_ref[...], state_refs, columns)


def last_body(n_island, n_dp, *refs):
    anchor_ref, momentum_ref = refs[:2]
    thetas = refs[2 : 2 + n_island]
    hidden = refs[2 + n_island : 2 + n_island + n_dp]
    *outs, hidden_out = refs[2 + n_island + n_dp : 5 + n_island + n_dp]
    *results, hidden_ref, scratch, sems = refs[5 + n_island + n_dp :]
    data = lax.axis_index("dp")
    units = hidden[0].shape[0]
    for shift, value in enumerate(hidden):
        row = pl.multiple_of(wrap(data - shift, n_dp) * units, 8)
        scratch[pl.ds(row, units), :] = value[...].astype(jnp.float32)
    hidden_ref[...] = scratch[...].T.astype(jnp.bfloat16)
    copies = [pltpu.make_async_copy(hidden_ref, hidden_out, sems.at[2, 0])]
    copies[0].start()
    rows = anchor_ref.shape[0]
    parts = 4 if rows % 32 == 0 else 1
    for part in range(parts):
        at = pl.ds(part * (rows // parts), rows // parts)
        total = thetas[0][at, :].astype(jnp.float32)
        for theta in thetas[1:]:
            total = total + theta[at, :].astype(jnp.float32)
        anchor = anchor_ref[at, :]
        mean_delta = anchor - total * (1.0 / n_island)
        momentum_new = outer_beta * momentum_ref[at, :] + mean_delta
        results[1][at, :] = momentum_new
        results[0][at, :] = anchor - outer_rate * (mean_delta + outer_beta * momentum_new)
        for index in range(2):
            copies.append(
                pltpu.make_async_copy(
                    results[index].at[at, :], outs[index].at[at, :], sems.at[index, part]
                )
            )
            copies[-1].start()
    for copy in copies:
        copy.wait()


def call(body, out_shape, ins, name, scratch=(), in_specs=None, out_specs=None):
    return pl.pallas_call(
        body,
        out_shape=out_shape,
        in_specs=in_specs or [VMEM] * len(ins),
        out_specs=out_specs or [VMEM] * len(out_shape),
        scratch_shapes=list(scratch),
        compiler_params=PARAMS,
        name=name,
    )(*ins)


def per_device(
    theta,
    first_moment,
    second_moment,
    anchor,
    momentum,
    cotangent,
    weights,
    expert_ids,
    expert_counts,
    hidden_saved,
):
    n_island, n_dp, n_expert = (lax.axis_size(name) for name in ("island", "dp", "expert"))
    pairs = n_expert // 2
    units, width = theta.shape[2:]
    length, full_units = hidden_saved.shape[3:]
    part = width // n_island
    bf16 = functools.partial(jax.ShapeDtypeStruct, dtype=jnp.bfloat16)

    def ring(value, name, size, shift):
        return lax.ppermute(value, name, [(k, (k + shift) % size) for k in range(size)])

    blocks = list(pack_rows(cotangent, weights, expert_ids, expert_counts, n_island))
    arrived = []
    for k in reversed(range(1, pairs)):
        perm = [(2 * z + c, 2 * target(z, k, pairs) + c) for z in range(pairs) for c in range(2)]
        arrived.append(lax.ppermute(blocks[k], "expert", perm))
    saved = hidden_saved.reshape(length, full_units)
    states = [in_hbm(value.reshape(units, width)) for value in (theta, first_moment, second_moment)]
    states = call(
        stage_body,
        [bf16((units, width))] * 3,
        states + [blocks[0]],
        "stage",
        [pltpu.SemaphoreType.DMA((3,))],
        in_specs=[HBM] * 3 + [VMEM],
    )
    saved_all = call(
        functools.partial(split_body, n_dp),
        [bf16((units, length))] * n_dp,
        [saved, blocks[0]],
        "split",
        [pltpu.VMEM((full_units, length), jnp.float32)],
    )
    saved_all = [ring(saved_all[s], "dp", n_dp, s) if s else saved_all[0] for s in range(n_dp)]
    arrived.append(blocks[0])
    far_mine, near_mine, mine = call(
        functools.partial(assemble_body, pairs),
        [bf16((pairs * CAP, columns)) for columns in (width - part, part, width)],
        arrived + list(states) + saved_all[1:],
        "assemble",
    )
    swap = [(j, j ^ 1) for j in range(n_expert)]
    other = lax.ppermute(mine, "expert", swap)

    def spread(chunk):
        quarters = [mine, other]
        for shift in range(1, n_dp):
            value = ring(chunk, "dp", n_dp, shift)
            quarters += [value, lax.ppermute(value, "expert", swap)]
        return quarters

    far_quarters = spread(far_mine)
    near_quarters = spread(near_mine)
    *far, far_slots, left = call(
        functools.partial(far_body, n_dp, n_island, pairs),
        [bf16((units, part))] * (n_island - 1) + [bf16((n_dp * length, width - part)), bf16((units, n_dp * length))],
        far_quarters + saved_all + list(states),
        "far_update",
    )
    theirs = [ring(value, "island", n_island, shift + 1) for shift, value in enumerate(far)]
    *hidden, near_slots = call(
        functools.partial(hidden_body, n_dp, n_island, pairs),
        [bf16((units, length))] * n_dp + [bf16((n_dp * length, part))],
        near_quarters + [far_slots, states[0]],
        "hidden_grad",
    )
    hidden = [hidden[0]] + [ring(hidden[s], "dp", n_dp, s) for s in range(1, n_dp)]
    (own,) = call(near_body, [bf16((units, part))], [near_slots, left, *states], "near_update")
    outer_type = jax.ShapeDtypeStruct((units, part), jnp.float32)
    anchor_new, momentum_new, d_hidden = call(
        functools.partial(last_body, n_island, n_dp),
        [outer_type, outer_type, bf16((length, full_units))],
        [anchor.reshape(units, part), momentum.reshape(units, part), own] + theirs + hidden,
        "outer_update",
        [pltpu.VMEM((units, part), jnp.float32)] * 2
        + [
            pltpu.VMEM((length, full_units), jnp.bfloat16),
            pltpu.VMEM((full_units, length), jnp.float32),
            pltpu.SemaphoreType.DMA((3, 4)),
        ],
        out_specs=[HBM, HBM, HBM],
    )
    return (
        anchor_new.reshape(anchor.shape),
        momentum_new.reshape(momentum.shape),
        d_hidden.reshape(hidden_saved.shape),
    )


def solution(mesh):
    return jax.shard_map(
        per_device,
        mesh=mesh,
        in_specs=(
            P("island", "expert", "dp", None),
            P("island", "expert", "dp", None),
            P("island", "expert", "dp", None),
            P("expert", "dp", "island"),
            P("expert", "dp", "island"),
            P(("island", "dp", "expert"), None),
            P(("island", "dp", "expert"), None),
            P(("island", "dp", "expert"), None),
            P(("island", "dp", "expert"), None),
            P("island", "dp", "expert", None, None),
        ),
        out_specs=(
            P("expert", "dp", "island"),
            P("expert", "dp", "island"),
            P("island", "dp", "expert", None, None),
        ),
        check_vma=False,
    )
```

```python
import functools

import jax
import jax.numpy as jnp
from jax import lax
from jax.experimental import pallas as pl
from jax.experimental.pallas import tpu as pltpu
from jax.sharding import PartitionSpec as P

FF = 768
CAP = 16

beta_one = 0.9
beta_two = 0.95
adam_epsilon = 1e-08
inner_rate = 0.1
decay_rate = 0.1
outer_beta = 0.9
outer_rate = 0.7

VMEM = pl.BlockSpec(memory_space=pltpu.VMEM)
HBM = pl.BlockSpec(memory_space=pltpu.HBM)
PARAMS = pltpu.CompilerParams(vmem_limit_bytes=48 * 1024 * 1024)


def in_hbm(value):
    return pltpu.with_memory_space_constraint(value, pltpu.HBM)


def wrap(value, size):
    return lax.rem(value + size, size)


def target(place, step, size):
    return place ^ step if size & (size - 1) == 0 else (place + step) % size


def source(place, step, size):
    return place ^ step if size & (size - 1) == 0 else (place - step) % size


def cut(part):
    return part * 3 // 4 // 128 * 128


def pieces(n_island, width):
    part = width // n_island
    first = cut(part)
    island = lax.axis_index("island")
    order = [(shift, 0, first) for shift in range(1, n_island)]
    order += [(shift, first, part - first) for shift in range(1, n_island)]
    order += [(n_island, 0, part)]
    found, at = [], 0
    for shift, skip, size in order:
        column = lax.rem(island + shift, n_island) * part + skip
        found.append((slice(at, at + size), pl.ds(pl.multiple_of(column, 128), size)))
        at += size
    return found


def pack_body(experts, n_island, ids_hbm, weights_hbm, counts_hbm, cot_hbm, *refs):
    outs = refs[:experts]
    ids_ref, weights_ref, counts_ref, cot_ref, sems = refs[experts:]
    copies = [
        pltpu.make_async_copy(src, dst, sems.at[index])
        for index, (src, dst) in enumerate(
            [
                (ids_hbm, ids_ref),
                (weights_hbm, weights_ref),
                (counts_hbm, counts_ref),
                (cot_hbm, cot_ref),
            ]
        )
    ]
    for copy in copies:
        copy.start()
    width, tokens = ids_ref.shape
    rows = experts * CAP
    place = lax.div(lax.axis_index("expert"), 2)
    step = lax.broadcasted_iota(jnp.int32, (experts, CAP, tokens), 0).reshape(rows, tokens)
    expert = target(place, step, experts)
    rank = lax.broadcasted_iota(jnp.int32, (experts, CAP, tokens), 1).reshape(rows, tokens)
    earlier = (
        lax.broadcasted_iota(jnp.int32, (tokens, tokens), 0)
        < lax.broadcasted_iota(jnp.int32, (tokens, tokens), 1)
    )
    earlier = jnp.where(earlier, 1.0, 0.0).astype(jnp.bfloat16)
    for copy in copies[:3]:
        copy.wait()
    named = jnp.zeros((rows, tokens), jnp.float32)
    weight = jnp.zeros((rows, tokens), jnp.float32)
    for slot in range(width):
        hit = ids_ref[slot : slot + 1, :] == expert
        named = jnp.where(hit, 1.0, named)
        weight = jnp.where(hit, weights_ref[slot : slot + 1, :], weight)
    limit = jnp.zeros((rows, tokens), jnp.int32)
    for index in range(experts):
        limit = jnp.where(expert == index, counts_ref[:, index : index + 1], limit)
    found = jnp.dot(named.astype(jnp.bfloat16), earlier, preferred_element_type=jnp.float32)
    found = found.astype(jnp.int32)
    picked = (named > 0.0) & (found < limit) & (found == rank)
    pick = jnp.where(picked, 1.0, 0.0)
    scale = jnp.sum(pick * weight, axis=1, keepdims=True)
    pick = pick.astype(jnp.bfloat16)
    copies[3].wait()
    for at, columns in pieces(n_island, cot_ref.shape[1]):
        gathered = jnp.dot(pick, cot_ref[:, columns], preferred_element_type=jnp.float32)
        packed = (gathered * scale).astype(jnp.bfloat16)
        for index, out in enumerate(outs):
            out[:, at] = packed[index * CAP : (index + 1) * CAP]


def pack_rows(cotangent, weights, expert_ids, counts, n_island):
    experts = counts.shape[1]
    ins = [expert_ids.T, weights.T, counts, cotangent]
    return pl.pallas_call(
        functools.partial(pack_body, experts, n_island),
        out_shape=[jax.ShapeDtypeStruct((CAP, cotangent.shape[1]), jnp.bfloat16)] * experts,
        in_specs=[HBM] * 4,
        out_specs=[VMEM] * experts,
        scratch_shapes=[
            pltpu.VMEM(expert_ids.shape[::-1], jnp.int32),
            pltpu.VMEM(weights.shape[::-1], jnp.float32),
            pltpu.VMEM(counts.shape, jnp.int32),
            pltpu.VMEM(cotangent.shape, jnp.bfloat16),
            pltpu.SemaphoreType.DMA((4,)),
        ],
        compiler_params=PARAMS,
        name="pack",
    )(*[in_hbm(value) for value in ins])


def adam(grad, first, second, theta):
    first_new = beta_one * first.astype(jnp.float32) + (1.0 - beta_one) * grad
    second_new = beta_two * second.astype(jnp.float32) + (1.0 - beta_two) * grad * grad
    wide = theta.astype(jnp.float32)
    step_size = first_new / (jnp.sqrt(second_new) + adam_epsilon) + decay_rate * wide
    return (wide - inner_rate * step_size).astype(jnp.bfloat16)


def assemble_body(pairs, *refs):
    blocks, (one_ref, two_ref, mine_ref) = refs[:pairs], refs[-3:]
    split = one_ref.shape[1]
    for index, block in enumerate(blocks):
        rows = slice(index * CAP, (index + 1) * CAP)
        value = block[...]
        one_ref[rows, :] = value[:, :split]
        two_ref[rows, :] = value[:, split:]
        mine_ref[rows, :] = value


def stage_body(*refs):
    states, copied, sems = refs[:3], refs[4:7], refs[7]
    copies = [
        pltpu.make_async_copy(src, dst, sems.at[index])
        for index, (src, dst) in enumerate(zip(states, copied))
    ]
    for copy in copies:
        copy.start()
    for copy in copies:
        copy.wait()


def split_body(n_dp, saved_ref, _, *refs):
    *outs, scratch = refs
    units = outs[0].shape[0]
    scratch[...] = saved_ref[...].astype(jnp.float32).T
    for shift, out in enumerate(outs):
        row = pl.multiple_of(lax.rem(lax.axis_index("dp") + shift, n_dp) * units, 8)
        out[...] = scratch[pl.ds(row, units), :].astype(jnp.bfloat16)


def gather_slots(n_dp, pairs, quarters, slots_ref, first):
    data, position = lax.axis_index("dp"), lax.axis_index("expert")
    core = lax.rem(position, 2)
    place = lax.div(position, 2)
    length = 2 * pairs * CAP
    for shift in range(n_dp):
        group = wrap(data - shift, n_dp)
        for flip in range(2):
            side = core if flip == 0 else 1 - core
            block = quarters[2 * shift + flip]
            columns = slice(first, first + slots_ref.shape[1]) if shift == 0 else slice(None)
            for k in range(pairs):
                at = (pairs - 1 - k) * CAP
                row = group * length + (2 * source(place, k, pairs) + side) * CAP
                row = pl.multiple_of(row, CAP)
                slots_ref[pl.ds(row, CAP), :] = block[at : at + CAP, columns]


def update(left, slots, state_refs, columns):
    grad = FF ** (-0.5) * jnp.dot(left, slots, preferred_element_type=jnp.float32)
    theta, first, second = (ref[:, columns] for ref in state_refs)
    return adam(grad, first, second, theta)


def one_body(n_dp, n_island, pairs, *refs):
    quarters = refs[: 2 * n_dp]
    saved = refs[2 * n_dp : 3 * n_dp]
    state_refs = refs[3 * n_dp : 3 * n_dp + 3]
    *outs, slots_ref, left_ref = refs[3 * n_dp + 3 :]
    length = saved[0].shape[1]
    for shift, value in enumerate(saved):
        column = pl.multiple_of(wrap(lax.axis_index("dp") - shift, n_dp) * length, 128)
        left_ref[:, pl.ds(column, length)] = value[...]
    gather_slots(n_dp, pairs, quarters, slots_ref, 0)
    places = pieces(n_island, state_refs[0].shape[1])
    for out, (at, columns) in zip(outs, places):
        out[...] = update(left_ref[...], slots_ref[:, at], state_refs, columns)


def two_body(n_dp, n_island, pairs, *refs):
    quarters = refs[: 2 * n_dp]
    left_ref, *state_refs = refs[2 * n_dp : 2 * n_dp + 4]
    *outs, slots_ref = refs[2 * n_dp + 4 :]
    width = state_refs[0].shape[1]
    first = width - slots_ref.shape[1]
    gather_slots(n_dp, pairs, quarters, slots_ref, first)
    places = pieces(n_island, width)[n_island - 1 :]
    for out, (at, columns) in zip(outs, places):
        slots = slots_ref[:, at.start - first : at.stop - first]
        out[...] = update(left_ref[...], slots, state_refs, columns)


def hidden_body(n_dp, n_island, one_ref, two_ref, theta_ref, *outs):
    data = lax.axis_index("dp")
    split = one_ref.shape[1]
    length = one_ref.shape[0] // n_dp
    total = None
    for at, columns in pieces(n_island, theta_ref.shape[1]):
        in_one = at.stop <= split
        slots = one_ref[:, at] if in_one else two_ref[:, at.start - split : at.stop - split]
        value = lax.dot_general(
            theta_ref[:, columns],
            slots,
            (((1,), (1,)), ((), ())),
            preferred_element_type=jnp.float32,
        )
        total = value if total is None else total + value
    hidden = (FF ** (-0.5) * total).astype(jnp.bfloat16)
    for shift, out in enumerate(outs):
        for group in range(n_dp):

            @pl.when(lax.rem(data + shift, n_dp) == group)
            def _():
                out[...] = hidden[:, group * length : (group + 1) * length]


def near_body(slots_ref, left_ref, *refs):
    state_refs, own_ref = refs[:3], refs[-1]
    part = own_ref.shape[1]
    columns = pl.ds(pl.multiple_of(lax.axis_index("island") * part, 128), part)
    slots = slots_ref[:, slots_ref.shape[1] - part :]
    own_ref[...] = update(left_ref[...], slots, state_refs, columns)


def last_body(n_island, n_dp, *refs):
    anchor_ref, momentum_ref = refs[:2]
    own_ref, theirs = refs[2], refs[3 : 1 + 2 * n_island]
    hidden = refs[1 + 2 * n_island : 1 + 2 * n_island + n_dp]
    *outs, hidden_out = refs[1 + 2 * n_island + n_dp : 4 + 2 * n_island + n_dp]
    *results, hidden_ref, scratch, sems = refs[4 + 2 * n_island + n_dp :]
    data = lax.axis_index("dp")
    units = hidden[0].shape[0]
    for shift, value in enumerate(hidden):
        row = pl.multiple_of(wrap(data - shift, n_dp) * units, 8)
        scratch[pl.ds(row, units), :] = value[...].astype(jnp.float32)
    hidden_ref[...] = scratch[...].T.astype(jnp.bfloat16)
    copies = [pltpu.make_async_copy(hidden_ref, hidden_out, sems.at[2, 0])]
    copies[0].start()
    rows, part = anchor_ref.shape
    steps = 2 if rows % 16 == 0 else 1
    for side in range(2):
        columns = slice(0, cut(part)) if side == 0 else slice(cut(part), part)
        for step in range(steps):
            at = slice(step * (rows // steps), (step + 1) * (rows // steps))
            total = own_ref[at, columns].astype(jnp.float32)
            for theta in theirs[side * (n_island - 1) : (side + 1) * (n_island - 1)]:
                total = total + theta[at, :].astype(jnp.float32)
            anchor = anchor_ref[at, columns]
            mean_delta = anchor - total * (1.0 / n_island)
            momentum_new = outer_beta * momentum_ref[at, columns] + mean_delta
            results[1][at, columns] = momentum_new
            results[0][at, columns] = anchor - outer_rate * (mean_delta + outer_beta * momentum_new)
            for index in range(2):
                copies.append(
                    pltpu.make_async_copy(
                        results[index].at[at, columns],
                        outs[index].at[at, columns],
                        sems.at[index, 2 * side + step],
                    )
                )
                copies[-1].start()
    for copy in copies:
        copy.wait()


def call(body, out_shape, ins, name, scratch=(), in_specs=None, out_specs=None):
    return pl.pallas_call(
        body,
        out_shape=out_shape,
        in_specs=in_specs or [VMEM] * len(ins),
        out_specs=out_specs or [VMEM] * len(out_shape),
        scratch_shapes=list(scratch),
        compiler_params=PARAMS,
        name=name,
    )(*ins)


def per_device(
    theta,
    first_moment,
    second_moment,
    anchor,
    momentum,
    cotangent,
    weights,
    expert_ids,
    expert_counts,
    hidden_saved,
):
    n_island, n_dp, n_expert = (lax.axis_size(name) for name in ("island", "dp", "expert"))
    pairs = n_expert // 2
    units, width = theta.shape[2:]
    length, full_units = hidden_saved.shape[3:]
    part = width // n_island
    first = cut(part)
    split = (n_island - 1) * first
    bf16 = functools.partial(jax.ShapeDtypeStruct, dtype=jnp.bfloat16)

    def ring(value, name, size, shift):
        return lax.ppermute(value, name, [(k, (k + shift) % size) for k in range(size)])

    blocks = list(pack_rows(cotangent, weights, expert_ids, expert_counts, n_island))
    arrived = []
    for k in reversed(range(1, pairs)):
        perm = [(2 * z + c, 2 * target(z, k, pairs) + c) for z in range(pairs) for c in range(2)]
        arrived.append(lax.ppermute(blocks[k], "expert", perm))
    saved = hidden_saved.reshape(length, full_units)
    states = [in_hbm(value.reshape(units, width)) for value in (theta, first_moment, second_moment)]
    states = call(
        stage_body,
        [bf16((units, width))] * 3,
        states + [blocks[0]],
        "stage",
        [pltpu.SemaphoreType.DMA((3,))],
        in_specs=[HBM] * 3 + [VMEM],
    )
    saved_all = call(
        functools.partial(split_body, n_dp),
        [bf16((units, length))] * n_dp,
        [saved, blocks[0]],
        "split",
        [pltpu.VMEM((full_units, length), jnp.float32)],
    )
    saved_all = [ring(saved_all[s], "dp", n_dp, s) if s else saved_all[0] for s in range(n_dp)]
    arrived.append(blocks[0])
    one_mine, two_mine, mine = call(
        functools.partial(assemble_body, pairs),
        [bf16((pairs * CAP, columns)) for columns in (split, width - split, width)],
        arrived + list(states) + saved_all[1:],
        "assemble",
    )
    swap = [(j, j ^ 1) for j in range(n_expert)]
    other = lax.ppermute(mine, "expert", swap)

    def spread(chunk, after=None):
        quarters = [mine, other]
        for shift in range(1, n_dp):
            value = ring(chunk, "dp", n_dp, shift)
            if after is not None:
                value, _ = lax.optimization_barrier((value, after))
            quarters += [value, lax.ppermute(value, "expert", swap)]
        return quarters

    one_quarters = spread(one_mine)
    *one, one_slots, left = call(
        functools.partial(one_body, n_dp, n_island, pairs),
        [bf16((units, first))] * (n_island - 1)
        + [bf16((n_dp * length, split)), bf16((units, n_dp * length))],
        one_quarters + saved_all + list(states),
        "far_one",
    )
    theirs = [ring(value, "island", n_island, shift + 1) for shift, value in enumerate(one)]
    two_quarters = spread(two_mine, left)
    *two, two_slots = call(
        functools.partial(two_body, n_dp, n_island, pairs),
        [bf16((units, part - first))] * (n_island - 1)
        + [bf16((n_dp * length, width - split))],
        two_quarters + [left, *states],
        "far_two",
    )
    theirs += [ring(value, "island", n_island, shift + 1) for shift, value in enumerate(two)]
    hidden = call(
        functools.partial(hidden_body, n_dp, n_island),
        [bf16((units, length))] * n_dp,
        [one_slots, two_slots, states[0]],
        "hidden_grad",
    )
    hidden = [hidden[0]] + [ring(hidden[s], "dp", n_dp, s) for s in range(1, n_dp)]
    (own,) = call(
        near_body, [bf16((units, part))], [two_slots, left, *states] + theirs[: n_island - 1], "near_update"
    )
    outer_type = jax.ShapeDtypeStruct((units, part), jnp.float32)
    anchor_new, momentum_new, d_hidden = call(
        functools.partial(last_body, n_island, n_dp),
        [outer_type, outer_type, bf16((length, full_units))],
        [anchor.reshape(units, part), momentum.reshape(units, part), own] + theirs + hidden,
        "outer_update",
        [pltpu.VMEM((units, part), jnp.float32)] * 2
        + [
            pltpu.VMEM((length, full_units), jnp.bfloat16),
            pltpu.VMEM((full_units, length), jnp.float32),
            pltpu.SemaphoreType.DMA((3, 4)),
        ],
        out_specs=[HBM, HBM, HBM],
    )
    return (
        anchor_new.reshape(anchor.shape),
        momentum_new.reshape(momentum.shape),
        d_hidden.reshape(hidden_saved.shape),
    )


def solution(mesh):
    return jax.shard_map(
        per_device,
        mesh=mesh,
        in_specs=(
            P("island", "expert", "dp", None),
            P("island", "expert", "dp", None),
            P("island", "expert", "dp", None),
            P("expert", "dp", "island"),
            P("expert", "dp", "island"),
            P(("island", "dp", "expert"), None),
            P(("island", "dp", "expert"), None),
            P(("island", "dp", "expert"), None),
            P(("island", "dp", "expert"), None),
            P("island", "dp", "expert", None, None),
        ),
        out_specs=(
            P("expert", "dp", "island"),
            P("expert", "dp", "island"),
            P("island", "dp", "expert", None, None),
        ),
        check_vma=False,
    )
```

```python
import functools

import jax
import jax.numpy as jnp
from jax import lax
from jax.experimental import pallas as pl
from jax.experimental.pallas import tpu as pltpu
from jax.sharding import PartitionSpec as P

FF = 768
CAP = 16

beta_one = 0.9
beta_two = 0.95
adam_epsilon = 1e-08
inner_rate = 0.1
decay_rate = 0.1
outer_beta = 0.9
outer_rate = 0.7

VMEM = pl.BlockSpec(memory_space=pltpu.VMEM)
HBM = pl.BlockSpec(memory_space=pltpu.HBM)
PARAMS = pltpu.CompilerParams(vmem_limit_bytes=48 * 1024 * 1024)


def in_hbm(value):
    return pltpu.with_memory_space_constraint(value, pltpu.HBM)


def wrap(value, size):
    return lax.rem(value + size, size)


def target(place, step, size):
    return place ^ step if size & (size - 1) == 0 else (place + step) % size


def source(place, step, size):
    return place ^ step if size & (size - 1) == 0 else (place - step) % size


def cut(part):
    return part * 3 // 4 // 128 * 128


def pieces(n_island, width):
    part = width // n_island
    first = cut(part)
    island = lax.axis_index("island")
    order = [(shift, 0, first) for shift in range(1, n_island)]
    order += [(shift, first, part - first) for shift in range(1, n_island)]
    order += [(n_island, 0, part)]
    found, at = [], 0
    for shift, skip, size in order:
        column = lax.rem(island + shift, n_island) * part + skip
        found.append((slice(at, at + size), pl.ds(pl.multiple_of(column, 128), size)))
        at += size
    return found


def pack_body(experts, n_island, ids_hbm, weights_hbm, counts_hbm, cot_hbm, *refs):
    outs = refs[:experts]
    ids_ref, weights_ref, counts_ref, cot_ref, sems = refs[experts:]
    copies = [
        pltpu.make_async_copy(src, dst, sems.at[index])
        for index, (src, dst) in enumerate(
            [
                (ids_hbm, ids_ref),
                (weights_hbm, weights_ref),
                (counts_hbm, counts_ref),
                (cot_hbm, cot_ref),
            ]
        )
    ]
    for copy in copies:
        copy.start()
    width, tokens = ids_ref.shape
    rows = experts * CAP
    place = lax.div(lax.axis_index("expert"), 2)
    step = lax.broadcasted_iota(jnp.int32, (experts, CAP, tokens), 0).reshape(rows, tokens)
    expert = target(place, step, experts)
    rank = lax.broadcasted_iota(jnp.int32, (experts, CAP, tokens), 1).reshape(rows, tokens)
    earlier = (
        lax.broadcasted_iota(jnp.int32, (tokens, tokens), 0)
        < lax.broadcasted_iota(jnp.int32, (tokens, tokens), 1)
    )
    earlier = jnp.where(earlier, 1.0, 0.0).astype(jnp.bfloat16)
    for copy in copies[:3]:
        copy.wait()
    named = jnp.zeros((rows, tokens), jnp.float32)
    weight = jnp.zeros((rows, tokens), jnp.float32)
    for slot in range(width):
        hit = ids_ref[slot : slot + 1, :] == expert
        named = jnp.where(hit, 1.0, named)
        weight = jnp.where(hit, weights_ref[slot : slot + 1, :], weight)
    limit = jnp.zeros((rows, tokens), jnp.int32)
    for index in range(experts):
        limit = jnp.where(expert == index, counts_ref[:, index : index + 1], limit)
    found = jnp.dot(named.astype(jnp.bfloat16), earlier, preferred_element_type=jnp.float32)
    found = found.astype(jnp.int32)
    picked = (named > 0.0) & (found < limit) & (found == rank)
    pick = jnp.where(picked, 1.0, 0.0)
    scale = jnp.sum(pick * weight, axis=1, keepdims=True)
    pick = pick.astype(jnp.bfloat16)
    copies[3].wait()
    for at, columns in pieces(n_island, cot_ref.shape[1]):
        gathered = jnp.dot(pick, cot_ref[:, columns], preferred_element_type=jnp.float32)
        packed = (gathered * scale).astype(jnp.bfloat16)
        for index, out in enumerate(outs):
            out[:, at] = packed[index * CAP : (index + 1) * CAP]


def pack_rows(cotangent, weights, expert_ids, counts, n_island):
    experts = counts.shape[1]
    ins = [expert_ids.T, weights.T, counts, cotangent]
    return pl.pallas_call(
        functools.partial(pack_body, experts, n_island),
        out_shape=[jax.ShapeDtypeStruct((CAP, cotangent.shape[1]), jnp.bfloat16)] * experts,
        in_specs=[HBM] * 4,
        out_specs=[VMEM] * experts,
        scratch_shapes=[
            pltpu.VMEM(expert_ids.shape[::-1], jnp.int32),
            pltpu.VMEM(weights.shape[::-1], jnp.float32),
            pltpu.VMEM(counts.shape, jnp.int32),
            pltpu.VMEM(cotangent.shape, jnp.bfloat16),
            pltpu.SemaphoreType.DMA((4,)),
        ],
        compiler_params=PARAMS,
        name="pack",
    )(*[in_hbm(value) for value in ins])


def adam(grad, first, second, theta):
    first_new = beta_one * first.astype(jnp.float32) + (1.0 - beta_one) * grad
    second_new = beta_two * second.astype(jnp.float32) + (1.0 - beta_two) * grad * grad
    wide = theta.astype(jnp.float32)
    step_size = first_new / (jnp.sqrt(second_new) + adam_epsilon) + decay_rate * wide
    return (wide - inner_rate * step_size).astype(jnp.bfloat16)


def assemble_body(pairs, *refs):
    blocks, (one_ref, mine_ref) = refs[:pairs], refs[-2:]
    split = one_ref.shape[1]
    for index, block in enumerate(blocks):
        rows = slice(index * CAP, (index + 1) * CAP)
        value = block[...]
        one_ref[rows, :] = value[:, :split]
        mine_ref[rows, :] = value


def rest_body(mine_ref, *refs):
    out_ref = refs[-1]
    out_ref[...] = mine_ref[:, mine_ref.shape[1] - out_ref.shape[1] :]


def stage_body(*refs):
    states, copied, sems = refs[:3], refs[4:7], refs[7]
    copies = [
        pltpu.make_async_copy(src, dst, sems.at[index])
        for index, (src, dst) in enumerate(zip(states, copied))
    ]
    for copy in copies:
        copy.start()
    for copy in copies:
        copy.wait()


def split_body(n_dp, saved_ref, _, *refs):
    *outs, scratch = refs
    units = outs[0].shape[0]
    scratch[...] = saved_ref[...].astype(jnp.float32).T
    for shift, out in enumerate(outs):
        row = pl.multiple_of(lax.rem(lax.axis_index("dp") + shift, n_dp) * units, 8)
        out[...] = scratch[pl.ds(row, units), :].astype(jnp.bfloat16)


def gather_slots(n_dp, pairs, quarters, slots_ref, first):
    data, position = lax.axis_index("dp"), lax.axis_index("expert")
    core = lax.rem(position, 2)
    place = lax.div(position, 2)
    length = 2 * pairs * CAP
    for shift in range(n_dp):
        group = wrap(data - shift, n_dp)
        for flip in range(2):
            side = core if flip == 0 else 1 - core
            block = quarters[2 * shift + flip]
            columns = slice(first, first + slots_ref.shape[1]) if shift == 0 else slice(None)
            for k in range(pairs):
                at = (pairs - 1 - k) * CAP
                row = group * length + (2 * source(place, k, pairs) + side) * CAP
                row = pl.multiple_of(row, CAP)
                slots_ref[pl.ds(row, CAP), :] = block[at : at + CAP, columns]


def update(left, slots, state_refs, columns):
    grad = FF ** (-0.5) * jnp.dot(left, slots, preferred_element_type=jnp.float32)
    theta, first, second = (ref[:, columns] for ref in state_refs)
    return adam(grad, first, second, theta)


def one_body(n_dp, n_island, pairs, *refs):
    quarters = refs[: 2 * n_dp]
    saved = refs[2 * n_dp : 3 * n_dp]
    state_refs = refs[3 * n_dp : 3 * n_dp + 3]
    *outs, slots_ref, left_ref = refs[3 * n_dp + 3 :]
    length = saved[0].shape[1]
    for shift, value in enumerate(saved):
        column = pl.multiple_of(wrap(lax.axis_index("dp") - shift, n_dp) * length, 128)
        left_ref[:, pl.ds(column, length)] = value[...]
    gather_slots(n_dp, pairs, quarters, slots_ref, 0)
    places = pieces(n_island, state_refs[0].shape[1])
    for out, (at, columns) in zip(outs, places):
        out[...] = update(left_ref[...], slots_ref[:, at], state_refs, columns)


def two_body(n_dp, n_island, pairs, *refs):
    quarters = refs[: 2 * n_dp]
    left_ref, *state_refs = refs[2 * n_dp : 2 * n_dp + 4]
    *outs, slots_ref = refs[2 * n_dp + 4 :]
    width = state_refs[0].shape[1]
    first = width - slots_ref.shape[1]
    gather_slots(n_dp, pairs, quarters, slots_ref, first)
    places = pieces(n_island, width)[n_island - 1 :]
    for out, (at, columns) in zip(outs, places):
        slots = slots_ref[:, at.start - first : at.stop - first]
        out[...] = update(left_ref[...], slots, state_refs, columns)


def hidden_body(n_dp, n_island, one_ref, two_ref, theta_ref, *outs):
    data = lax.axis_index("dp")
    split = one_ref.shape[1]
    length = one_ref.shape[0] // n_dp
    total = None
    for at, columns in pieces(n_island, theta_ref.shape[1]):
        in_one = at.stop <= split
        slots = one_ref[:, at] if in_one else two_ref[:, at.start - split : at.stop - split]
        value = lax.dot_general(
            theta_ref[:, columns],
            slots,
            (((1,), (1,)), ((), ())),
            preferred_element_type=jnp.float32,
        )
        total = value if total is None else total + value
    hidden = (FF ** (-0.5) * total).astype(jnp.bfloat16)
    for shift, out in enumerate(outs):
        for group in range(n_dp):

            @pl.when(lax.rem(data + shift, n_dp) == group)
            def _():
                out[...] = hidden[:, group * length : (group + 1) * length]


def near_body(slots_ref, left_ref, *refs):
    *state_refs, own_ref = refs
    part = own_ref.shape[1]
    columns = pl.ds(pl.multiple_of(lax.axis_index("island") * part, 128), part)
    slots = slots_ref[:, slots_ref.shape[1] - part :]
    own_ref[...] = update(left_ref[...], slots, state_refs, columns)


def outer_step(columns, anchor_ref, momentum_ref, own_ref, theirs, results, outs, sems):
    n_island = len(theirs) + 1
    rows = anchor_ref.shape[0]
    steps = 2 if rows % 16 == 0 else 1
    copies = []
    for step in range(steps):
        at = slice(step * (rows // steps), (step + 1) * (rows // steps))
        total = own_ref[at, columns].astype(jnp.float32)
        for theta in theirs:
            total = total + theta[at, :].astype(jnp.float32)
        anchor = anchor_ref[at, columns]
        mean_delta = anchor - total * (1.0 / n_island)
        momentum_new = outer_beta * momentum_ref[at, columns] + mean_delta
        results[1][at, :] = momentum_new
        results[0][at, :] = anchor - outer_rate * (mean_delta + outer_beta * momentum_new)
        for index in range(2):
            copies.append(
                pltpu.make_async_copy(
                    results[index].at[at, :], outs[index].at[at, columns], sems.at[index, step]
                )
            )
            copies[-1].start()
    return copies


def outer_one_body(n_island, anchor_ref, momentum_ref, own_ref, *refs):
    theirs, outs = refs[: n_island - 1], refs[n_island - 1 : n_island + 1]
    *results, sems = refs[n_island + 1 :]
    columns = slice(0, results[0].shape[1])
    for copy in outer_step(columns, anchor_ref, momentum_ref, own_ref, theirs, results, outs, sems):
        copy.wait()


def outer_two_body(n_island, n_dp, _, __, anchor_ref, momentum_ref, own_ref, *refs):
    theirs, refs = refs[: n_island - 1], refs[n_island - 1 :]
    hidden, refs = refs[:n_dp], refs[n_dp:]
    *outs, hidden_out = refs[:3]
    *results, hidden_ref, scratch, sems = refs[3:]
    data = lax.axis_index("dp")
    units = hidden[0].shape[0]
    for shift, value in enumerate(hidden):
        row = pl.multiple_of(wrap(data - shift, n_dp) * units, 8)
        scratch[pl.ds(row, units), :] = value[...].astype(jnp.float32)
    part = anchor_ref.shape[1]
    columns = slice(part - results[0].shape[1], part)
    copies = outer_step(columns, anchor_ref, momentum_ref, own_ref, theirs, results, outs, sems)
    hidden_ref[...] = scratch[...].T.astype(jnp.bfloat16)
    copies.append(pltpu.make_async_copy(hidden_ref, hidden_out, sems.at[2, 0]))
    copies[-1].start()
    for copy in copies:
        copy.wait()


def call(body, out_shape, ins, name, scratch=(), in_specs=None, out_specs=None, aliases=None):
    return pl.pallas_call(
        body,
        out_shape=out_shape,
        in_specs=in_specs or [VMEM] * len(ins),
        out_specs=out_specs or [VMEM] * len(out_shape),
        scratch_shapes=list(scratch),
        input_output_aliases=aliases or {},
        compiler_params=PARAMS,
        name=name,
    )(*ins)


def per_device(
    theta,
    first_moment,
    second_moment,
    anchor,
    momentum,
    cotangent,
    weights,
    expert_ids,
    expert_counts,
    hidden_saved,
):
    n_island, n_dp, n_expert = (lax.axis_size(name) for name in ("island", "dp", "expert"))
    pairs = n_expert // 2
    units, width = theta.shape[2:]
    length, full_units = hidden_saved.shape[3:]
    part = width // n_island
    first = cut(part)
    split = (n_island - 1) * first
    bf16 = functools.partial(jax.ShapeDtypeStruct, dtype=jnp.bfloat16)

    def ring(value, name, size, shift):
        return lax.ppermute(value, name, [(k, (k + shift) % size) for k in range(size)])

    blocks = list(pack_rows(cotangent, weights, expert_ids, expert_counts, n_island))
    arrived = []
    for k in reversed(range(1, pairs)):
        perm = [(2 * z + c, 2 * target(z, k, pairs) + c) for z in range(pairs) for c in range(2)]
        arrived.append(lax.ppermute(blocks[k], "expert", perm))
    saved = hidden_saved.reshape(length, full_units)
    saved_all = call(
        functools.partial(split_body, n_dp),
        [bf16((units, length))] * n_dp,
        [saved, blocks[0]],
        "split",
        [pltpu.VMEM((full_units, length), jnp.float32)],
    )
    saved_all = [ring(saved_all[s], "dp", n_dp, s) if s else saved_all[0] for s in range(n_dp)]
    arrived.append(blocks[0])
    one_mine, mine = call(
        functools.partial(assemble_body, pairs),
        [bf16((pairs * CAP, columns)) for columns in (split, width)],
        arrived + saved_all[1:],
        "assemble",
    )
    swap = [(j, j ^ 1) for j in range(n_expert)]
    other = lax.ppermute(mine, "expert", swap)
    states = [in_hbm(value.reshape(units, width)) for value in (theta, first_moment, second_moment)]
    states = call(
        stage_body,
        [bf16((units, width))] * 3,
        states + [mine],
        "stage",
        [pltpu.SemaphoreType.DMA((3,))],
        in_specs=[HBM] * 3 + [VMEM],
    )
    (two_mine,) = call(
        rest_body, [bf16((pairs * CAP, width - split))], [mine, other, *states], "rest"
    )

    def spread(chunk, after=None):
        quarters = [mine, other]
        for shift in range(1, n_dp):
            value = ring(chunk, "dp", n_dp, shift)
            if after is not None:
                value, _ = lax.optimization_barrier((value, after))
            quarters += [value, lax.ppermute(value, "expert", swap)]
        return quarters

    one_quarters = spread(one_mine)
    *one, one_slots, left = call(
        functools.partial(one_body, n_dp, n_island, pairs),
        [bf16((units, first))] * (n_island - 1)
        + [bf16((n_dp * length, split)), bf16((units, n_dp * length))],
        one_quarters + saved_all + list(states),
        "far_one",
    )
    theirs = [ring(value, "island", n_island, shift + 1) for shift, value in enumerate(one)]
    two_quarters = spread(two_mine, left)
    *two, two_slots = call(
        functools.partial(two_body, n_dp, n_island, pairs),
        [bf16((units, part - first))] * (n_island - 1)
        + [bf16((n_dp * length, width - split))],
        two_quarters + [left, *states],
        "far_two",
    )
    theirs += [ring(value, "island", n_island, shift + 1) for shift, value in enumerate(two)]
    hidden = call(
        functools.partial(hidden_body, n_dp, n_island),
        [bf16((units, length))] * n_dp,
        [one_slots, two_slots, states[0]],
        "hidden_grad",
    )
    hidden = [hidden[0]] + [ring(hidden[s], "dp", n_dp, s) for s in range(1, n_dp)]
    (own,) = call(near_body, [bf16((units, part))], [two_slots, left, *states], "near_update")
    outer = [anchor.reshape(units, part), momentum.reshape(units, part), own]
    outer_type = jax.ShapeDtypeStruct((units, part), jnp.float32)
    begun = call(
        functools.partial(outer_one_body, n_island),
        [outer_type, outer_type],
        outer + theirs[: n_island - 1],
        "outer_one",
        [pltpu.VMEM((units, first), jnp.float32)] * 2 + [pltpu.SemaphoreType.DMA((2, 2))],
        out_specs=[HBM, HBM],
    )
    ins = [*begun, *outer, *theirs[n_island - 1 :], *hidden]
    anchor_new, momentum_new, d_hidden = call(
        functools.partial(outer_two_body, n_island, n_dp),
        [outer_type, outer_type, bf16((length, full_units))],
        ins,
        "outer_two",
        [pltpu.VMEM((units, part - first), jnp.float32)] * 2
        + [
            pltpu.VMEM((length, full_units), jnp.bfloat16),
            pltpu.VMEM((full_units, length), jnp.float32),
            pltpu.SemaphoreType.DMA((3, 2)),
        ],
        in_specs=[HBM, HBM] + [VMEM] * (len(ins) - 2),
        out_specs=[HBM, HBM, HBM],
        aliases={0: 0, 1: 1},
    )
    return (
        anchor_new.reshape(anchor.shape),
        momentum_new.reshape(momentum.shape),
        d_hidden.reshape(hidden_saved.shape),
    )


def solution(mesh):
    return jax.shard_map(
        per_device,
        mesh=mesh,
        in_specs=(
            P("island", "expert", "dp", None),
            P("island", "expert", "dp", None),
            P("island", "expert", "dp", None),
            P("expert", "dp", "island"),
            P("expert", "dp", "island"),
            P(("island", "dp", "expert"), None),
            P(("island", "dp", "expert"), None),
            P(("island", "dp", "expert"), None),
            P(("island", "dp", "expert"), None),
            P("island", "dp", "expert", None, None),
        ),
        out_specs=(
            P("expert", "dp", "island"),
            P("expert", "dp", "island"),
            P("island", "dp", "expert", None, None),
        ),
        check_vma=False,
    )
```

```python
import functools

import jax
import jax.numpy as jnp
from jax import lax
from jax.experimental import pallas as pl
from jax.experimental.pallas import tpu as pltpu
from jax.sharding import PartitionSpec as P

FF = 768
CAP = 16

beta_one = 0.9
beta_two = 0.95
adam_epsilon = 1e-08
inner_rate = 0.1
decay_rate = 0.1
outer_beta = 0.9
outer_rate = 0.7

VMEM = pl.BlockSpec(memory_space=pltpu.VMEM)
HBM = pl.BlockSpec(memory_space=pltpu.HBM)
PARAMS = pltpu.CompilerParams(vmem_limit_bytes=48 * 1024 * 1024)


def in_hbm(value):
    return pltpu.with_memory_space_constraint(value, pltpu.HBM)


def wrap(value, size):
    return lax.rem(value + size, size)


def target(place, step, size):
    return place ^ step if size & (size - 1) == 0 else (place + step) % size


def order(size):
    return sorted(range(size), key=lambda step: (step == 0, step != size // 2, -step))


def source(place, step, size):
    return place ^ step if size & (size - 1) == 0 else (place - step) % size


def cut(part):
    return part * 3 // 4 // 128 * 128


def pieces(n_island, width):
    part = width // n_island
    first = cut(part)
    island = lax.axis_index("island")
    order = [(shift, 0, first) for shift in range(1, n_island)]
    order += [(shift, first, part - first) for shift in range(1, n_island)]
    order += [(n_island, 0, part)]
    found, at = [], 0
    for shift, skip, size in order:
        column = lax.rem(island + shift, n_island) * part + skip
        found.append((slice(at, at + size), pl.ds(pl.multiple_of(column, 128), size)))
        at += size
    return found


def pack_body(experts, n_island, ids_hbm, weights_hbm, counts_hbm, cot_hbm, *refs):
    outs = refs[:experts]
    ids_ref, weights_ref, counts_ref, cot_ref, sems = refs[experts:]
    copies = [
        pltpu.make_async_copy(src, dst, sems.at[index])
        for index, (src, dst) in enumerate(
            [
                (ids_hbm, ids_ref),
                (weights_hbm, weights_ref),
                (counts_hbm, counts_ref),
                (cot_hbm, cot_ref),
            ]
        )
    ]
    for copy in copies:
        copy.start()
    width, tokens = ids_ref.shape
    rows = experts * CAP
    place = lax.div(lax.axis_index("expert"), 2)
    step = lax.broadcasted_iota(jnp.int32, (experts, CAP, tokens), 0).reshape(rows, tokens)
    expert = target(place, step, experts)
    rank = lax.broadcasted_iota(jnp.int32, (experts, CAP, tokens), 1).reshape(rows, tokens)
    earlier = (
        lax.broadcasted_iota(jnp.int32, (tokens, tokens), 0)
        < lax.broadcasted_iota(jnp.int32, (tokens, tokens), 1)
    )
    earlier = jnp.where(earlier, 1.0, 0.0).astype(jnp.bfloat16)
    for copy in copies[:3]:
        copy.wait()
    named = jnp.zeros((rows, tokens), jnp.float32)
    weight = jnp.zeros((rows, tokens), jnp.float32)
    for slot in range(width):
        hit = ids_ref[slot : slot + 1, :] == expert
        named = jnp.where(hit, 1.0, named)
        weight = jnp.where(hit, weights_ref[slot : slot + 1, :], weight)
    limit = jnp.zeros((rows, tokens), jnp.int32)
    for index in range(experts):
        limit = jnp.where(expert == index, counts_ref[:, index : index + 1], limit)
    found = jnp.dot(named.astype(jnp.bfloat16), earlier, preferred_element_type=jnp.float32)
    found = found.astype(jnp.int32)
    picked = (named > 0.0) & (found < limit) & (found == rank)
    pick = jnp.where(picked, 1.0, 0.0)
    scale = jnp.sum(pick * weight, axis=1, keepdims=True)
    pick = pick.astype(jnp.bfloat16)
    copies[3].wait()
    for at, columns in pieces(n_island, cot_ref.shape[1]):
        gathered = jnp.dot(pick, cot_ref[:, columns], preferred_element_type=jnp.float32)
        packed = (gathered * scale).astype(jnp.bfloat16)
        for index, out in enumerate(outs):
            out[:, at] = packed[index * CAP : (index + 1) * CAP]


def pack_rows(cotangent, weights, expert_ids, counts, n_island):
    experts = counts.shape[1]
    ins = [expert_ids.T, weights.T, counts, cotangent]
    return pl.pallas_call(
        functools.partial(pack_body, experts, n_island),
        out_shape=[jax.ShapeDtypeStruct((CAP, cotangent.shape[1]), jnp.bfloat16)] * experts,
        in_specs=[HBM] * 4,
        out_specs=[VMEM] * experts,
        scratch_shapes=[
            pltpu.VMEM(expert_ids.shape[::-1], jnp.int32),
            pltpu.VMEM(weights.shape[::-1], jnp.float32),
            pltpu.VMEM(counts.shape, jnp.int32),
            pltpu.VMEM(cotangent.shape, jnp.bfloat16),
            pltpu.SemaphoreType.DMA((4,)),
        ],
        compiler_params=PARAMS,
        name="pack",
    )(*[in_hbm(value) for value in ins])


def adam(product, first, second, theta):
    scale = FF ** (-0.5)
    wide = theta.astype(jnp.float32)
    first_new = (inner_rate * beta_one) * first.astype(jnp.float32)
    first_new = first_new + (inner_rate * (1.0 - beta_one) * scale) * product
    second_new = beta_two * second.astype(jnp.float32)
    second_new = second_new + ((1.0 - beta_two) * scale * scale) * (product * product)
    step_size = first_new / (jnp.sqrt(second_new) + adam_epsilon)
    return ((1.0 - inner_rate * decay_rate) * wide - step_size).astype(jnp.bfloat16)


def assemble_body(pairs, *refs):
    blocks, (one_ref, two_ref) = refs[:pairs], refs[-2:]
    split = one_ref.shape[1]
    for index, block in enumerate(blocks):
        rows = slice(index * CAP, (index + 1) * CAP)
        one_ref[rows, :] = block[:, :split]
        two_ref[rows, :] = block[:, split:]


def rest_body(two_ref, *refs):
    refs[-1][...] = two_ref[...]


def stage_body(*refs):
    states, copied, sems = refs[:3], refs[4:7], refs[7]
    copies = [
        pltpu.make_async_copy(src, dst, sems.at[index])
        for index, (src, dst) in enumerate(zip(states, copied))
    ]
    for copy in copies:
        copy.start()
    for copy in copies:
        copy.wait()


def split_body(n_dp, saved_ref, _, *refs):
    *outs, scratch = refs
    units = outs[0].shape[0]
    scratch[...] = saved_ref[...].astype(jnp.float32).T
    for shift, out in enumerate(outs):
        row = pl.multiple_of(lax.rem(lax.axis_index("dp") + shift, n_dp) * units, 8)
        out[...] = scratch[pl.ds(row, units), :].astype(jnp.bfloat16)


def gather_slots(n_dp, pairs, quarters, slots_ref):
    data, position = lax.axis_index("dp"), lax.axis_index("expert")
    core = lax.rem(position, 2)
    place = lax.div(position, 2)
    length = 2 * pairs * CAP
    for shift in range(n_dp):
        group = wrap(data - shift, n_dp)
        for flip in range(2):
            side = core if flip == 0 else 1 - core
            block = quarters[2 * shift + flip]
            for k in range(pairs):
                at = order(pairs).index(k) * CAP
                row = group * length + (2 * source(place, k, pairs) + side) * CAP
                row = pl.multiple_of(row, CAP)
                slots_ref[pl.ds(row, CAP), :] = block[at : at + CAP, :]


def update(left, slots, state_refs, columns):
    product = jnp.dot(left, slots, preferred_element_type=jnp.float32)
    theta, first, second = (ref[:, columns] for ref in state_refs)
    return adam(product, first, second, theta)


def one_body(n_dp, n_island, pairs, *refs):
    quarters = refs[: 2 * n_dp]
    saved = refs[2 * n_dp : 3 * n_dp]
    state_refs = refs[3 * n_dp : 3 * n_dp + 3]
    *outs, slots_ref, left_ref = refs[3 * n_dp + 3 :]
    length = saved[0].shape[1]
    for shift, value in enumerate(saved):
        column = pl.multiple_of(wrap(lax.axis_index("dp") - shift, n_dp) * length, 128)
        left_ref[:, pl.ds(column, length)] = value[...]
    gather_slots(n_dp, pairs, quarters, slots_ref)
    places = pieces(n_island, state_refs[0].shape[1])
    for out, (at, columns) in zip(outs, places):
        out[...] = update(left_ref[...], slots_ref[:, at], state_refs, columns)


def two_body(n_dp, n_island, pairs, *refs):
    quarters = refs[: 2 * n_dp]
    left_ref, *state_refs = refs[2 * n_dp : 2 * n_dp + 4]
    *outs, slots_ref = refs[2 * n_dp + 4 :]
    width = state_refs[0].shape[1]
    first = width - slots_ref.shape[1]
    gather_slots(n_dp, pairs, quarters, slots_ref)
    places = pieces(n_island, width)[n_island - 1 :]
    for out, (at, columns) in zip(outs, places):
        slots = slots_ref[:, at.start - first : at.stop - first]
        out[...] = update(left_ref[...], slots, state_refs, columns)


def hidden_body(n_dp, n_island, one_ref, two_ref, theta_ref, *outs):
    data = lax.axis_index("dp")
    split = one_ref.shape[1]
    length = one_ref.shape[0] // n_dp
    total = None
    for at, columns in pieces(n_island, theta_ref.shape[1]):
        in_one = at.stop <= split
        slots = one_ref[:, at] if in_one else two_ref[:, at.start - split : at.stop - split]
        value = lax.dot_general(
            theta_ref[:, columns],
            slots,
            (((1,), (1,)), ((), ())),
            preferred_element_type=jnp.float32,
        )
        total = value if total is None else total + value
    hidden = (FF ** (-0.5) * total).astype(jnp.bfloat16)
    for shift, out in enumerate(outs):
        for group in range(n_dp):

            @pl.when(lax.rem(data + shift, n_dp) == group)
            def _():
                out[...] = hidden[:, group * length : (group + 1) * length]


def near_body(slots_ref, left_ref, *refs):
    *state_refs, own_ref = refs
    part = own_ref.shape[1]
    columns = pl.ds(pl.multiple_of(lax.axis_index("island") * part, 128), part)
    slots = slots_ref[:, slots_ref.shape[1] - part :]
    own_ref[...] = update(left_ref[...], slots, state_refs, columns)


def outer_step(columns, anchor_ref, momentum_ref, own_ref, theirs, results, outs, sems):
    n_island = len(theirs) + 1
    rows = anchor_ref.shape[0]
    steps = 2 if rows % 16 == 0 else 1
    copies = []
    for step in range(steps):
        at = slice(step * (rows // steps), (step + 1) * (rows // steps))
        total = own_ref[at, columns].astype(jnp.float32)
        for theta in theirs:
            total = total + theta[at, :].astype(jnp.float32)
        anchor = anchor_ref[at, columns]
        mean_delta = anchor - total * (1.0 / n_island)
        momentum_new = outer_beta * momentum_ref[at, columns] + mean_delta
        results[1][at, :] = momentum_new
        results[0][at, :] = anchor - outer_rate * (mean_delta + outer_beta * momentum_new)
        for index in range(2):
            copies.append(
                pltpu.make_async_copy(
                    results[index].at[at, :], outs[index].at[at, columns], sems.at[index, step]
                )
            )
            copies[-1].start()
    return copies


def outer_one_body(n_island, anchor_ref, momentum_ref, own_ref, *refs):
    theirs, outs = refs[: n_island - 1], refs[n_island - 1 : n_island + 1]
    *results, sems = refs[n_island + 1 :]
    columns = slice(0, results[0].shape[1])
    for copy in outer_step(columns, anchor_ref, momentum_ref, own_ref, theirs, results, outs, sems):
        copy.wait()


def outer_two_body(n_island, n_dp, _, __, anchor_ref, momentum_ref, own_ref, *refs):
    theirs, refs = refs[: n_island - 1], refs[n_island - 1 :]
    hidden, refs = refs[:n_dp], refs[n_dp:]
    *outs, hidden_out = refs[:3]
    *results, hidden_ref, scratch, sems = refs[3:]
    data = lax.axis_index("dp")
    units = hidden[0].shape[0]
    for shift, value in enumerate(hidden):
        row = pl.multiple_of(wrap(data - shift, n_dp) * units, 8)
        scratch[pl.ds(row, units), :] = value[...].astype(jnp.float32)
    part = anchor_ref.shape[1]
    columns = slice(part - results[0].shape[1], part)
    copies = outer_step(columns, anchor_ref, momentum_ref, own_ref, theirs, results, outs, sems)
    hidden_ref[...] = scratch[...].T.astype(jnp.bfloat16)
    copies.append(pltpu.make_async_copy(hidden_ref, hidden_out, sems.at[2, 0]))
    copies[-1].start()
    for copy in copies:
        copy.wait()


def call(body, out_shape, ins, name, scratch=(), in_specs=None, out_specs=None, aliases=None):
    return pl.pallas_call(
        body,
        out_shape=out_shape,
        in_specs=in_specs or [VMEM] * len(ins),
        out_specs=out_specs or [VMEM] * len(out_shape),
        scratch_shapes=list(scratch),
        input_output_aliases=aliases or {},
        compiler_params=PARAMS,
        name=name,
    )(*ins)


def per_device(
    theta,
    first_moment,
    second_moment,
    anchor,
    momentum,
    cotangent,
    weights,
    expert_ids,
    expert_counts,
    hidden_saved,
):
    n_island, n_dp, n_expert = (lax.axis_size(name) for name in ("island", "dp", "expert"))
    pairs = n_expert // 2
    units, width = theta.shape[2:]
    length, full_units = hidden_saved.shape[3:]
    part = width // n_island
    first = cut(part)
    split = (n_island - 1) * first
    bf16 = functools.partial(jax.ShapeDtypeStruct, dtype=jnp.bfloat16)

    def ring(value, name, size, shift):
        return lax.ppermute(value, name, [(k, (k + shift) % size) for k in range(size)])

    blocks = list(pack_rows(cotangent, weights, expert_ids, expert_counts, n_island))
    arrived = []
    for k in order(pairs)[:-1]:
        perm = [(2 * z + c, 2 * target(z, k, pairs) + c) for z in range(pairs) for c in range(2)]
        arrived.append(lax.ppermute(blocks[k], "expert", perm))
    saved = hidden_saved.reshape(length, full_units)
    saved_all = call(
        functools.partial(split_body, n_dp),
        [bf16((units, length))] * n_dp,
        [saved, blocks[0]],
        "split",
        [pltpu.VMEM((full_units, length), jnp.float32)],
    )
    saved_all = [ring(saved_all[s], "dp", n_dp, s) if s else saved_all[0] for s in range(n_dp)]
    arrived.append(blocks[0])
    one_mine, two_mine = call(
        functools.partial(assemble_body, pairs),
        [bf16((pairs * CAP, columns)) for columns in (split, width - split)],
        arrived + saved_all[1:],
        "assemble",
    )
    swap = [(j, j ^ 1) for j in range(n_expert)]

    def spread(mine, after=None):
        quarters = [mine, lax.ppermute(mine, "expert", swap)]
        for shift in range(1, n_dp):
            value = ring(mine, "dp", n_dp, shift)
            if after is not None:
                value, _ = lax.optimization_barrier((value, after))
            quarters += [value, lax.ppermute(value, "expert", swap)]
        return quarters

    one_quarters = spread(one_mine)
    states = [in_hbm(value.reshape(units, width)) for value in (theta, first_moment, second_moment)]
    states = call(
        stage_body,
        [bf16((units, width))] * 3,
        states + [one_mine],
        "stage",
        [pltpu.SemaphoreType.DMA((3,))],
        in_specs=[HBM] * 3 + [VMEM],
    )
    (two_mine,) = call(
        rest_body,
        [bf16((pairs * CAP, width - split))],
        [two_mine, one_quarters[1], *states],
        "rest",
    )
    *one, one_slots, left = call(
        functools.partial(one_body, n_dp, n_island, pairs),
        [bf16((units, first))] * (n_island - 1)
        + [bf16((n_dp * length, split)), bf16((units, n_dp * length))],
        one_quarters + saved_all + list(states),
        "far_one",
    )
    theirs = [ring(value, "island", n_island, shift + 1) for shift, value in enumerate(one)]
    two_quarters = spread(two_mine, left)
    *two, two_slots = call(
        functools.partial(two_body, n_dp, n_island, pairs),
        [bf16((units, part - first))] * (n_island - 1)
        + [bf16((n_dp * length, width - split))],
        two_quarters + [left, *states],
        "far_two",
    )
    theirs += [ring(value, "island", n_island, shift + 1) for shift, value in enumerate(two)]
    hidden = call(
        functools.partial(hidden_body, n_dp, n_island),
        [bf16((units, length))] * n_dp,
        [one_slots, two_slots, states[0]],
        "hidden_grad",
    )
    hidden = [hidden[0]] + [ring(hidden[s], "dp", n_dp, s) for s in range(1, n_dp)]
    (own,) = call(near_body, [bf16((units, part))], [two_slots, left, *states], "near_update")
    outer = [anchor.reshape(units, part), momentum.reshape(units, part), own]
    outer_type = jax.ShapeDtypeStruct((units, part), jnp.float32)
    begun = call(
        functools.partial(outer_one_body, n_island),
        [outer_type, outer_type],
        outer + theirs[: n_island - 1],
        "outer_one",
        [pltpu.VMEM((units, first), jnp.float32)] * 2 + [pltpu.SemaphoreType.DMA((2, 2))],
        out_specs=[HBM, HBM],
    )
    ins = [*begun, *outer, *theirs[n_island - 1 :], *hidden]
    anchor_new, momentum_new, d_hidden = call(
        functools.partial(outer_two_body, n_island, n_dp),
        [outer_type, outer_type, bf16((length, full_units))],
        ins,
        "outer_two",
        [pltpu.VMEM((units, part - first), jnp.float32)] * 2
        + [
            pltpu.VMEM((length, full_units), jnp.bfloat16),
            pltpu.VMEM((full_units, length), jnp.float32),
            pltpu.SemaphoreType.DMA((3, 2)),
        ],
        in_specs=[HBM, HBM] + [VMEM] * (len(ins) - 2),
        out_specs=[HBM, HBM, HBM],
        aliases={0: 0, 1: 1},
    )
    return (
        anchor_new.reshape(anchor.shape),
        momentum_new.reshape(momentum.shape),
        d_hidden.reshape(hidden_saved.shape),
    )


def solution(mesh):
    return jax.shard_map(
        per_device,
        mesh=mesh,
        in_specs=(
            P("island", "expert", "dp", None),
            P("island", "expert", "dp", None),
            P("island", "expert", "dp", None),
            P("expert", "dp", "island"),
            P("expert", "dp", "island"),
            P(("island", "dp", "expert"), None),
            P(("island", "dp", "expert"), None),
            P(("island", "dp", "expert"), None),
            P(("island", "dp", "expert"), None),
            P("island", "dp", "expert", None, None),
        ),
        out_specs=(
            P("expert", "dp", "island"),
            P("expert", "dp", "island"),
            P("island", "dp", "expert", None, None),
        ),
        check_vma=False,
    )
```

```python
import functools

import jax
import jax.numpy as jnp
from jax import lax
from jax.experimental import pallas as pl
from jax.experimental.pallas import tpu as pltpu
from jax.sharding import PartitionSpec as P

FF = 768
CAP = 16

beta_one = 0.9
beta_two = 0.95
adam_epsilon = 1e-08
inner_rate = 0.1
decay_rate = 0.1
outer_beta = 0.9
outer_rate = 0.7

VMEM = pl.BlockSpec(memory_space=pltpu.VMEM)
HBM = pl.BlockSpec(memory_space=pltpu.HBM)
PARAMS = pltpu.CompilerParams(vmem_limit_bytes=48 * 1024 * 1024)


def in_hbm(value):
    return pltpu.with_memory_space_constraint(value, pltpu.HBM)


def wrap(value, size):
    return lax.rem(value + size, size)


def target(place, step, size):
    return place ^ step if size & (size - 1) == 0 else (place + step) % size


def order(size):
    return sorted(range(size), key=lambda step: (step == 0, step != size // 2, -step))


def source(place, step, size):
    return place ^ step if size & (size - 1) == 0 else (place - step) % size


def cut(part):
    return part * 3 // 4 // 128 * 128


def pieces(n_island, width):
    part = width // n_island
    first = cut(part)
    island = lax.axis_index("island")
    order = [(shift, 0, first) for shift in range(1, n_island)]
    order += [(shift, first, part - first) for shift in range(1, n_island)]
    order += [(n_island, 0, part)]
    found, at = [], 0
    for shift, skip, size in order:
        column = lax.rem(island + shift, n_island) * part + skip
        found.append((slice(at, at + size), pl.ds(pl.multiple_of(column, 128), size)))
        at += size
    return found


def pack_body(experts, n_island, ids_hbm, weights_hbm, counts_hbm, cot_hbm, *refs):
    outs = refs[:experts]
    ids_ref, weights_ref, counts_ref, cot_ref, sems = refs[experts:]
    places = pieces(n_island, cot_ref.shape[1])
    pairs = [(ids_hbm, ids_ref), (weights_hbm, weights_ref), (counts_hbm, counts_ref)]
    pairs += [(cot_hbm.at[:, columns], cot_ref.at[:, at]) for at, columns in places]
    copies = [
        pltpu.make_async_copy(src, dst, sems.at[index]) for index, (src, dst) in enumerate(pairs)
    ]
    for copy in copies:
        copy.start()
    width, tokens = ids_ref.shape
    rows = experts * CAP
    place = lax.div(lax.axis_index("expert"), 2)
    step = lax.broadcasted_iota(jnp.int32, (experts, CAP, tokens), 0).reshape(rows, tokens)
    expert = target(place, step, experts)
    rank = lax.broadcasted_iota(jnp.int32, (experts, CAP, tokens), 1).reshape(rows, tokens)
    earlier = (
        lax.broadcasted_iota(jnp.int32, (tokens, tokens), 0)
        < lax.broadcasted_iota(jnp.int32, (tokens, tokens), 1)
    )
    earlier = jnp.where(earlier, 1.0, 0.0).astype(jnp.bfloat16)
    for copy in copies[:3]:
        copy.wait()
    named = jnp.zeros((rows, tokens), jnp.float32)
    weight = jnp.zeros((rows, tokens), jnp.float32)
    for slot in range(width):
        hit = ids_ref[slot : slot + 1, :] == expert
        named = jnp.where(hit, 1.0, named)
        weight = jnp.where(hit, weights_ref[slot : slot + 1, :], weight)
    limit = jnp.zeros((rows, tokens), jnp.int32)
    for index in range(experts):
        limit = jnp.where(expert == index, counts_ref[:, index : index + 1], limit)
    found = jnp.dot(named.astype(jnp.bfloat16), earlier, preferred_element_type=jnp.float32)
    found = found.astype(jnp.int32)
    picked = (named > 0.0) & (found < limit) & (found == rank)
    pick = jnp.where(picked, 1.0, 0.0)
    scale = jnp.sum(pick * weight, axis=1, keepdims=True)
    pick = pick.astype(jnp.bfloat16)
    for copy, (at, _) in zip(copies[3:], places):
        copy.wait()
        gathered = jnp.dot(pick, cot_ref[:, at], preferred_element_type=jnp.float32)
        packed = (gathered * scale).astype(jnp.bfloat16)
        for index, out in enumerate(outs):
            out[:, at] = packed[index * CAP : (index + 1) * CAP]


def pack_rows(cotangent, weights, expert_ids, counts, n_island):
    experts = counts.shape[1]
    ins = [expert_ids.T, weights.T, counts, cotangent]
    return pl.pallas_call(
        functools.partial(pack_body, experts, n_island),
        out_shape=[jax.ShapeDtypeStruct((CAP, cotangent.shape[1]), jnp.bfloat16)] * experts,
        in_specs=[HBM] * 4,
        out_specs=[VMEM] * experts,
        scratch_shapes=[
            pltpu.VMEM(expert_ids.shape[::-1], jnp.int32),
            pltpu.VMEM(weights.shape[::-1], jnp.float32),
            pltpu.VMEM(counts.shape, jnp.int32),
            pltpu.VMEM(cotangent.shape, jnp.bfloat16),
            pltpu.SemaphoreType.DMA((2 + 2 * n_island,)),
        ],
        compiler_params=PARAMS,
        name="pack",
    )(*[in_hbm(value) for value in ins])


def adam(product, first, second, theta):
    scale = FF ** (-0.5)
    wide = theta.astype(jnp.float32)
    first_new = (inner_rate * beta_one) * first.astype(jnp.float32)
    first_new = first_new + (inner_rate * (1.0 - beta_one) * scale) * product
    second_new = beta_two * second.astype(jnp.float32)
    second_new = second_new + ((1.0 - beta_two) * scale * scale) * (product * product)
    step_size = first_new / (jnp.sqrt(second_new) + adam_epsilon)
    return ((1.0 - inner_rate * decay_rate) * wide - step_size).astype(jnp.bfloat16)


def assemble_body(pairs, *refs):
    blocks, (one_ref, two_ref) = refs[:pairs], refs[-2:]
    split = one_ref.shape[1]
    for index, block in enumerate(blocks):
        rows = slice(index * CAP, (index + 1) * CAP)
        one_ref[rows, :] = block[:, :split]
        two_ref[rows, :] = block[:, split:]


def rest_body(two_ref, *refs):
    refs[-1][...] = two_ref[...]


def stage_body(*refs):
    states, copied, sems = refs[:3], refs[4:7], refs[7]
    copies = [
        pltpu.make_async_copy(src, dst, sems.at[index])
        for index, (src, dst) in enumerate(zip(states, copied))
    ]
    for copy in copies:
        copy.start()
    for copy in copies:
        copy.wait()


def split_body(n_dp, saved_ref, _, *refs):
    *outs, scratch = refs
    units = outs[0].shape[0]
    scratch[...] = saved_ref[...].astype(jnp.float32).T
    for shift, out in enumerate(outs):
        row = pl.multiple_of(lax.rem(lax.axis_index("dp") + shift, n_dp) * units, 8)
        out[...] = scratch[pl.ds(row, units), :].astype(jnp.bfloat16)


def gather_slots(n_dp, pairs, quarters, slots_ref):
    data, position = lax.axis_index("dp"), lax.axis_index("expert")
    core = lax.rem(position, 2)
    place = lax.div(position, 2)
    length = 2 * pairs * CAP
    for shift in range(n_dp):
        group = wrap(data - shift, n_dp)
        for flip in range(2):
            side = core if flip == 0 else 1 - core
            block = quarters[2 * shift + flip]
            for k in range(pairs):
                at = order(pairs).index(k) * CAP
                row = group * length + (2 * source(place, k, pairs) + side) * CAP
                row = pl.multiple_of(row, CAP)
                slots_ref[pl.ds(row, CAP), :] = block[at : at + CAP, :]


def update(left, slots, state_refs, columns):
    product = jnp.dot(left, slots, preferred_element_type=jnp.float32)
    theta, first, second = (ref[:, columns] for ref in state_refs)
    return adam(product, first, second, theta)


def one_body(n_dp, n_island, pairs, *refs):
    quarters = refs[: 2 * n_dp]
    saved = refs[2 * n_dp : 3 * n_dp]
    state_refs = refs[3 * n_dp : 3 * n_dp + 3]
    *outs, slots_ref, left_ref = refs[3 * n_dp + 3 :]
    length = saved[0].shape[1]
    for shift, value in enumerate(saved):
        column = pl.multiple_of(wrap(lax.axis_index("dp") - shift, n_dp) * length, 128)
        left_ref[:, pl.ds(column, length)] = value[...]
    gather_slots(n_dp, pairs, quarters, slots_ref)
    places = pieces(n_island, state_refs[0].shape[1])
    for out, (at, columns) in zip(outs, places):
        out[...] = update(left_ref[...], slots_ref[:, at], state_refs, columns)


def two_body(n_dp, n_island, pairs, *refs):
    quarters = refs[: 2 * n_dp]
    left_ref, *state_refs = refs[2 * n_dp : 2 * n_dp + 4]
    *outs, slots_ref = refs[2 * n_dp + 4 :]
    width = state_refs[0].shape[1]
    first = width - slots_ref.shape[1]
    gather_slots(n_dp, pairs, quarters, slots_ref)
    places = pieces(n_island, width)[n_island - 1 :]
    for out, (at, columns) in zip(outs, places):
        slots = slots_ref[:, at.start - first : at.stop - first]
        out[...] = update(left_ref[...], slots, state_refs, columns)


def hidden_body(n_dp, n_island, one_ref, two_ref, theta_ref, *outs):
    data = lax.axis_index("dp")
    split = one_ref.shape[1]
    length = one_ref.shape[0] // n_dp
    total = None
    for at, columns in pieces(n_island, theta_ref.shape[1]):
        in_one = at.stop <= split
        slots = one_ref[:, at] if in_one else two_ref[:, at.start - split : at.stop - split]
        value = lax.dot_general(
            theta_ref[:, columns],
            slots,
            (((1,), (1,)), ((), ())),
            preferred_element_type=jnp.float32,
        )
        total = value if total is None else total + value
    hidden = (FF ** (-0.5) * total).astype(jnp.bfloat16)
    for shift, out in enumerate(outs):
        for group in range(n_dp):

            @pl.when(lax.rem(data + shift, n_dp) == group)
            def _():
                out[...] = hidden[:, group * length : (group + 1) * length]


def near_body(slots_ref, left_ref, *refs):
    *state_refs, own_ref = refs
    part = own_ref.shape[1]
    columns = pl.ds(pl.multiple_of(lax.axis_index("island") * part, 128), part)
    slots = slots_ref[:, slots_ref.shape[1] - part :]
    own_ref[...] = update(left_ref[...], slots, state_refs, columns)


def outer_step(columns, anchor_ref, momentum_ref, own_ref, theirs, results, outs, sems):
    n_island = len(theirs) + 1
    rows = anchor_ref.shape[0]
    steps = 2 if rows % 16 == 0 else 1
    copies = []
    for step in range(steps):
        at = slice(step * (rows // steps), (step + 1) * (rows // steps))
        total = own_ref[at, columns].astype(jnp.float32)
        for theta in theirs:
            total = total + theta[at, :].astype(jnp.float32)
        anchor = anchor_ref[at, columns]
        mean_delta = anchor - total * (1.0 / n_island)
        momentum_new = outer_beta * momentum_ref[at, columns] + mean_delta
        results[1][at, :] = momentum_new
        results[0][at, :] = anchor - outer_rate * (mean_delta + outer_beta * momentum_new)
        for index in range(2):
            copies.append(
                pltpu.make_async_copy(
                    results[index].at[at, :], outs[index].at[at, columns], sems.at[index, step]
                )
            )
            copies[-1].start()
    return copies


def outer_one_body(n_island, anchor_ref, momentum_ref, own_ref, *refs):
    theirs, outs = refs[: n_island - 1], refs[n_island - 1 : n_island + 1]
    *results, sems = refs[n_island + 1 :]
    columns = slice(0, results[0].shape[1])
    for copy in outer_step(columns, anchor_ref, momentum_ref, own_ref, theirs, results, outs, sems):
        copy.wait()


def outer_two_body(n_island, n_dp, _, __, anchor_ref, momentum_ref, own_ref, *refs):
    theirs, refs = refs[: n_island - 1], refs[n_island - 1 :]
    hidden, refs = refs[:n_dp], refs[n_dp:]
    *outs, hidden_out = refs[:3]
    *results, hidden_ref, scratch, sems = refs[3:]
    data = lax.axis_index("dp")
    units = hidden[0].shape[0]
    for shift, value in enumerate(hidden):
        row = pl.multiple_of(wrap(data - shift, n_dp) * units, 8)
        scratch[pl.ds(row, units), :] = value[...].astype(jnp.float32)
    part = anchor_ref.shape[1]
    columns = slice(part - results[0].shape[1], part)
    copies = outer_step(columns, anchor_ref, momentum_ref, own_ref, theirs, results, outs, sems)
    hidden_ref[...] = scratch[...].T.astype(jnp.bfloat16)
    copies.append(pltpu.make_async_copy(hidden_ref, hidden_out, sems.at[2, 0]))
    copies[-1].start()
    for copy in copies:
        copy.wait()


def call(body, out_shape, ins, name, scratch=(), in_specs=None, out_specs=None, aliases=None):
    return pl.pallas_call(
        body,
        out_shape=out_shape,
        in_specs=in_specs or [VMEM] * len(ins),
        out_specs=out_specs or [VMEM] * len(out_shape),
        scratch_shapes=list(scratch),
        input_output_aliases=aliases or {},
        compiler_params=PARAMS,
        name=name,
    )(*ins)


def per_device(
    theta,
    first_moment,
    second_moment,
    anchor,
    momentum,
    cotangent,
    weights,
    expert_ids,
    expert_counts,
    hidden_saved,
):
    n_island, n_dp, n_expert = (lax.axis_size(name) for name in ("island", "dp", "expert"))
    pairs = n_expert // 2
    units, width = theta.shape[2:]
    length, full_units = hidden_saved.shape[3:]
    part = width // n_island
    first = cut(part)
    split = (n_island - 1) * first
    bf16 = functools.partial(jax.ShapeDtypeStruct, dtype=jnp.bfloat16)

    def ring(value, name, size, shift):
        return lax.ppermute(value, name, [(k, (k + shift) % size) for k in range(size)])

    blocks = list(pack_rows(cotangent, weights, expert_ids, expert_counts, n_island))
    arrived = []
    for k in order(pairs)[:-1]:
        perm = [(2 * z + c, 2 * target(z, k, pairs) + c) for z in range(pairs) for c in range(2)]
        arrived.append(lax.ppermute(blocks[k], "expert", perm))
    saved = hidden_saved.reshape(length, full_units)
    states = [in_hbm(value.reshape(units, width)) for value in (theta, first_moment, second_moment)]
    states = call(
        stage_body,
        [bf16((units, width))] * 3,
        states + [blocks[0]],
        "stage",
        [pltpu.SemaphoreType.DMA((3,))],
        in_specs=[HBM] * 3 + [VMEM],
    )
    saved_all = call(
        functools.partial(split_body, n_dp),
        [bf16((units, length))] * n_dp,
        [saved, blocks[0]],
        "split",
        [pltpu.VMEM((full_units, length), jnp.float32)],
    )
    saved_all = [ring(saved_all[s], "dp", n_dp, s) if s else saved_all[0] for s in range(n_dp)]
    arrived.append(blocks[0])
    one_mine, two_mine = call(
        functools.partial(assemble_body, pairs),
        [bf16((pairs * CAP, columns)) for columns in (split, width - split)],
        arrived + list(states) + saved_all[1:],
        "assemble",
    )
    swap = [(j, j ^ 1) for j in range(n_expert)]

    def spread(mine, after=None):
        quarters = [mine, lax.ppermute(mine, "expert", swap)]
        for shift in range(1, n_dp):
            value = ring(mine, "dp", n_dp, shift)
            if after is not None:
                value, _ = lax.optimization_barrier((value, after))
            quarters += [value, lax.ppermute(value, "expert", swap)]
        return quarters

    one_quarters = spread(one_mine)
    (two_mine,) = call(
        rest_body,
        [bf16((pairs * CAP, width - split))],
        [two_mine, one_quarters[1]],
        "rest",
    )
    *one, one_slots, left = call(
        functools.partial(one_body, n_dp, n_island, pairs),
        [bf16((units, first))] * (n_island - 1)
        + [bf16((n_dp * length, split)), bf16((units, n_dp * length))],
        one_quarters + saved_all + list(states),
        "far_one",
    )
    theirs = [ring(value, "island", n_island, shift + 1) for shift, value in enumerate(one)]
    two_quarters = spread(two_mine, left)
    *two, two_slots = call(
        functools.partial(two_body, n_dp, n_island, pairs),
        [bf16((units, part - first))] * (n_island - 1)
        + [bf16((n_dp * length, width - split))],
        two_quarters + [left, *states],
        "far_two",
    )
    theirs += [ring(value, "island", n_island, shift + 1) for shift, value in enumerate(two)]
    hidden = call(
        functools.partial(hidden_body, n_dp, n_island),
        [bf16((units, length))] * n_dp,
        [one_slots, two_slots, states[0]],
        "hidden_grad",
    )
    hidden = [hidden[0]] + [ring(hidden[s], "dp", n_dp, s) for s in range(1, n_dp)]
    (own,) = call(near_body, [bf16((units, part))], [two_slots, left, *states], "near_update")
    outer = [anchor.reshape(units, part), momentum.reshape(units, part), own]
    outer_type = jax.ShapeDtypeStruct((units, part), jnp.float32)
    begun = call(
        functools.partial(outer_one_body, n_island),
        [outer_type, outer_type],
        outer + theirs[: n_island - 1],
        "outer_one",
        [pltpu.VMEM((units, first), jnp.float32)] * 2 + [pltpu.SemaphoreType.DMA((2, 2))],
        out_specs=[HBM, HBM],
    )
    ins = [*begun, *outer, *theirs[n_island - 1 :], *hidden]
    anchor_new, momentum_new, d_hidden = call(
        functools.partial(outer_two_body, n_island, n_dp),
        [outer_type, outer_type, bf16((length, full_units))],
        ins,
        "outer_two",
        [pltpu.VMEM((units, part - first), jnp.float32)] * 2
        + [
            pltpu.VMEM((length, full_units), jnp.bfloat16),
            pltpu.VMEM((full_units, length), jnp.float32),
            pltpu.SemaphoreType.DMA((3, 2)),
        ],
        in_specs=[HBM, HBM] + [VMEM] * (len(ins) - 2),
        out_specs=[HBM, HBM, HBM],
        aliases={0: 0, 1: 1},
    )
    return (
        anchor_new.reshape(anchor.shape),
        momentum_new.reshape(momentum.shape),
        d_hidden.reshape(hidden_saved.shape),
    )


def solution(mesh):
    return jax.shard_map(
        per_device,
        mesh=mesh,
        in_specs=(
            P("island", "expert", "dp", None),
            P("island", "expert", "dp", None),
            P("island", "expert", "dp", None),
            P("expert", "dp", "island"),
            P("expert", "dp", "island"),
            P(("island", "dp", "expert"), None),
            P(("island", "dp", "expert"), None),
            P(("island", "dp", "expert"), None),
            P(("island", "dp", "expert"), None),
            P("island", "dp", "expert", None, None),
        ),
        out_specs=(
            P("expert", "dp", "island"),
            P("expert", "dp", "island"),
            P("island", "dp", "expert", None, None),
        ),
        check_vma=False,
    )
```

```python
import functools

import jax
import jax.numpy as jnp
from jax import lax
from jax.experimental import pallas as pl
from jax.experimental.pallas import tpu as pltpu
from jax.sharding import PartitionSpec as P

FF = 768
CAP = 16

beta_one = 0.9
beta_two = 0.95
adam_epsilon = 1e-08
inner_rate = 0.1
decay_rate = 0.1
outer_beta = 0.9
outer_rate = 0.7

VMEM = pl.BlockSpec(memory_space=pltpu.VMEM)
HBM = pl.BlockSpec(memory_space=pltpu.HBM)
PARAMS = pltpu.CompilerParams(vmem_limit_bytes=48 * 1024 * 1024)


PEAK = 1.15e15
MICROSECONDS = {
    "stage": 1.6,
    "split": 0.1,
    "assemble": 0.05,
    "rest": 0.05,
    "far_one": 3.0,
    "far_two": 0.01,
    "hidden_grad": 0.01,
    "near_update": 0.01,
    "outer_one": 1.1,
    "outer_two": 0.9,
}


def in_hbm(value):
    return pltpu.with_memory_space_constraint(value, pltpu.HBM)


def wrap(value, size):
    return lax.rem(value + size, size)


def target(place, step, size):
    return place ^ step if size & (size - 1) == 0 else (place + step) % size


def order(size):
    return sorted(range(size), key=lambda step: (step == 0, step != size // 2, -step))


def source(place, step, size):
    return place ^ step if size & (size - 1) == 0 else (place - step) % size


def cut(part):
    return part * 3 // 4 // 128 * 128


def pieces(n_island, width):
    part = width // n_island
    first = cut(part)
    island = lax.axis_index("island")
    order = [(shift, 0, first) for shift in range(1, n_island)]
    order += [(shift, first, part - first) for shift in range(1, n_island)]
    order += [(n_island, 0, part)]
    found, at = [], 0
    for shift, skip, size in order:
        column = lax.rem(island + shift, n_island) * part + skip
        found.append((slice(at, at + size), pl.ds(pl.multiple_of(column, 128), size)))
        at += size
    return found


def pack_body(experts, n_island, ids_hbm, weights_hbm, counts_hbm, cot_hbm, *refs):
    outs = refs[:experts]
    ids_ref, weights_ref, counts_ref, cot_ref, sems = refs[experts:]
    copies = [
        pltpu.make_async_copy(src, dst, sems.at[index])
        for index, (src, dst) in enumerate(
            [
                (ids_hbm, ids_ref),
                (weights_hbm, weights_ref),
                (counts_hbm, counts_ref),
                (cot_hbm, cot_ref),
            ]
        )
    ]
    for copy in copies:
        copy.start()
    width, tokens = ids_ref.shape
    rows = experts * CAP
    place = lax.div(lax.axis_index("expert"), 2)
    step = lax.broadcasted_iota(jnp.int32, (experts, CAP, tokens), 0).reshape(rows, tokens)
    expert = target(place, step, experts)
    rank = lax.broadcasted_iota(jnp.int32, (experts, CAP, tokens), 1).reshape(rows, tokens)
    earlier = (
        lax.broadcasted_iota(jnp.int32, (tokens, tokens), 0)
        < lax.broadcasted_iota(jnp.int32, (tokens, tokens), 1)
    )
    earlier = jnp.where(earlier, 1.0, 0.0).astype(jnp.bfloat16)
    for copy in copies[:3]:
        copy.wait()
    named = jnp.zeros((rows, tokens), jnp.float32)
    weight = jnp.zeros((rows, tokens), jnp.float32)
    for slot in range(width):
        hit = ids_ref[slot : slot + 1, :] == expert
        named = jnp.where(hit, 1.0, named)
        weight = jnp.where(hit, weights_ref[slot : slot + 1, :], weight)
    limit = jnp.zeros((rows, tokens), jnp.int32)
    for index in range(experts):
        limit = jnp.where(expert == index, counts_ref[:, index : index + 1], limit)
    found = jnp.dot(named.astype(jnp.bfloat16), earlier, preferred_element_type=jnp.float32)
    found = found.astype(jnp.int32)
    picked = (named > 0.0) & (found < limit) & (found == rank)
    pick = jnp.where(picked, 1.0, 0.0)
    scale = jnp.sum(pick * weight, axis=1, keepdims=True)
    pick = pick.astype(jnp.bfloat16)
    copies[3].wait()
    for at, columns in pieces(n_island, cot_ref.shape[1]):
        gathered = jnp.dot(pick, cot_ref[:, columns], preferred_element_type=jnp.float32)
        packed = (gathered * scale).astype(jnp.bfloat16)
        for index, out in enumerate(outs):
            out[:, at] = packed[index * CAP : (index + 1) * CAP]


def pack_rows(cotangent, weights, expert_ids, counts, n_island):
    experts = counts.shape[1]
    ins = [expert_ids.T, weights.T, counts, cotangent]
    return pl.pallas_call(
        functools.partial(pack_body, experts, n_island),
        out_shape=[jax.ShapeDtypeStruct((CAP, cotangent.shape[1]), jnp.bfloat16)] * experts,
        in_specs=[HBM] * 4,
        out_specs=[VMEM] * experts,
        scratch_shapes=[
            pltpu.VMEM(expert_ids.shape[::-1], jnp.int32),
            pltpu.VMEM(weights.shape[::-1], jnp.float32),
            pltpu.VMEM(counts.shape, jnp.int32),
            pltpu.VMEM(cotangent.shape, jnp.bfloat16),
            pltpu.SemaphoreType.DMA((4,)),
        ],
        compiler_params=PARAMS,
        name="pack",
    )(*[in_hbm(value) for value in ins])


def adam(product, first, second, theta):
    scale = FF ** (-0.5)
    wide = theta.astype(jnp.float32)
    first_new = (inner_rate * beta_one) * first.astype(jnp.float32)
    first_new = first_new + (inner_rate * (1.0 - beta_one) * scale) * product
    second_new = beta_two * second.astype(jnp.float32)
    second_new = second_new + ((1.0 - beta_two) * scale * scale) * (product * product)
    step_size = first_new / (jnp.sqrt(second_new) + adam_epsilon)
    return ((1.0 - inner_rate * decay_rate) * wide - step_size).astype(jnp.bfloat16)


def assemble_body(pairs, *refs):
    blocks, (one_ref, two_ref) = refs[:pairs], refs[-2:]
    split = one_ref.shape[1]
    for index, block in enumerate(blocks):
        rows = slice(index * CAP, (index + 1) * CAP)
        one_ref[rows, :] = block[:, :split]
        two_ref[rows, :] = block[:, split:]


def rest_body(two_ref, *refs):
    refs[-1][...] = two_ref[...]


def stage_body(*refs):
    states, copied, sems = refs[:3], refs[4:7], refs[7]
    copies = [
        pltpu.make_async_copy(src, dst, sems.at[index])
        for index, (src, dst) in enumerate(zip(states, copied))
    ]
    for copy in copies:
        copy.start()
    for copy in copies:
        copy.wait()


def split_body(n_dp, saved_ref, _, *refs):
    *outs, scratch = refs
    units = outs[0].shape[0]
    scratch[...] = saved_ref[...].astype(jnp.float32).T
    for shift, out in enumerate(outs):
        row = pl.multiple_of(lax.rem(lax.axis_index("dp") + shift, n_dp) * units, 8)
        out[...] = scratch[pl.ds(row, units), :].astype(jnp.bfloat16)


def gather_slots(n_dp, pairs, quarters, slots_ref):
    data, position = lax.axis_index("dp"), lax.axis_index("expert")
    core = lax.rem(position, 2)
    place = lax.div(position, 2)
    length = 2 * pairs * CAP
    for shift in range(n_dp):
        group = wrap(data - shift, n_dp)
        for flip in range(2):
            side = core if flip == 0 else 1 - core
            block = quarters[2 * shift + flip]
            for k in range(pairs):
                at = order(pairs).index(k) * CAP
                row = group * length + (2 * source(place, k, pairs) + side) * CAP
                row = pl.multiple_of(row, CAP)
                slots_ref[pl.ds(row, CAP), :] = block[at : at + CAP, :]


def update(left, slots, state_refs, columns):
    product = jnp.dot(left, slots, preferred_element_type=jnp.float32)
    theta, first, second = (ref[:, columns] for ref in state_refs)
    return adam(product, first, second, theta)


def one_body(n_dp, n_island, pairs, *refs):
    quarters = refs[: 2 * n_dp]
    saved = refs[2 * n_dp : 3 * n_dp]
    state_refs = refs[3 * n_dp : 3 * n_dp + 3]
    *outs, slots_ref, left_ref = refs[3 * n_dp + 3 :]
    length = saved[0].shape[1]
    for shift, value in enumerate(saved):
        column = pl.multiple_of(wrap(lax.axis_index("dp") - shift, n_dp) * length, 128)
        left_ref[:, pl.ds(column, length)] = value[...]
    gather_slots(n_dp, pairs, quarters, slots_ref)
    places = pieces(n_island, state_refs[0].shape[1])
    for out, (at, columns) in zip(outs, places):
        out[...] = update(left_ref[...], slots_ref[:, at], state_refs, columns)


def two_body(n_dp, n_island, pairs, *refs):
    quarters = refs[: 2 * n_dp]
    left_ref, *state_refs = refs[2 * n_dp : 2 * n_dp + 4]
    *outs, slots_ref = refs[2 * n_dp + 4 :]
    width = state_refs[0].shape[1]
    first = width - slots_ref.shape[1]
    gather_slots(n_dp, pairs, quarters, slots_ref)
    places = pieces(n_island, width)[n_island - 1 :]
    for out, (at, columns) in zip(outs, places):
        slots = slots_ref[:, at.start - first : at.stop - first]
        out[...] = update(left_ref[...], slots, state_refs, columns)


def hidden_body(n_dp, n_island, one_ref, two_ref, theta_ref, *outs):
    data = lax.axis_index("dp")
    split = one_ref.shape[1]
    length = one_ref.shape[0] // n_dp
    total = None
    for at, columns in pieces(n_island, theta_ref.shape[1]):
        in_one = at.stop <= split
        slots = one_ref[:, at] if in_one else two_ref[:, at.start - split : at.stop - split]
        value = lax.dot_general(
            theta_ref[:, columns],
            slots,
            (((1,), (1,)), ((), ())),
            preferred_element_type=jnp.float32,
        )
        total = value if total is None else total + value
    hidden = (FF ** (-0.5) * total).astype(jnp.bfloat16)
    for shift, out in enumerate(outs):
        for group in range(n_dp):

            @pl.when(lax.rem(data + shift, n_dp) == group)
            def _():
                out[...] = hidden[:, group * length : (group + 1) * length]


def near_body(slots_ref, left_ref, *refs):
    *state_refs, own_ref = refs
    part = own_ref.shape[1]
    columns = pl.ds(pl.multiple_of(lax.axis_index("island") * part, 128), part)
    slots = slots_ref[:, slots_ref.shape[1] - part :]
    own_ref[...] = update(left_ref[...], slots, state_refs, columns)


def outer_step(columns, anchor_ref, momentum_ref, own_ref, theirs, results, outs, sems):
    n_island = len(theirs) + 1
    rows = anchor_ref.shape[0]
    steps = 2 if rows % 16 == 0 else 1
    copies = []
    for step in range(steps):
        at = slice(step * (rows // steps), (step + 1) * (rows // steps))
        total = own_ref[at, columns].astype(jnp.float32)
        for theta in theirs:
            total = total + theta[at, :].astype(jnp.float32)
        anchor = anchor_ref[at, columns]
        mean_delta = anchor - total * (1.0 / n_island)
        momentum_new = outer_beta * momentum_ref[at, columns] + mean_delta
        results[1][at, :] = momentum_new
        results[0][at, :] = anchor - outer_rate * (mean_delta + outer_beta * momentum_new)
        for index in range(2):
            copies.append(
                pltpu.make_async_copy(
                    results[index].at[at, :], outs[index].at[at, columns], sems.at[index, step]
                )
            )
            copies[-1].start()
    return copies


def outer_one_body(n_island, anchor_ref, momentum_ref, own_ref, *refs):
    theirs, outs = refs[: n_island - 1], refs[n_island - 1 : n_island + 1]
    *results, sems = refs[n_island + 1 :]
    columns = slice(0, results[0].shape[1])
    for copy in outer_step(columns, anchor_ref, momentum_ref, own_ref, theirs, results, outs, sems):
        copy.wait()


def outer_two_body(n_island, n_dp, _, __, anchor_ref, momentum_ref, own_ref, *refs):
    theirs, refs = refs[: n_island - 1], refs[n_island - 1 :]
    hidden, refs = refs[:n_dp], refs[n_dp:]
    *outs, hidden_out = refs[:3]
    *results, hidden_ref, scratch, sems = refs[3:]
    data = lax.axis_index("dp")
    units = hidden[0].shape[0]
    for shift, value in enumerate(hidden):
        row = pl.multiple_of(wrap(data - shift, n_dp) * units, 8)
        scratch[pl.ds(row, units), :] = value[...].astype(jnp.float32)
    part = anchor_ref.shape[1]
    columns = slice(part - results[0].shape[1], part)
    copies = outer_step(columns, anchor_ref, momentum_ref, own_ref, theirs, results, outs, sems)
    hidden_ref[...] = scratch[...].T.astype(jnp.bfloat16)
    copies.append(pltpu.make_async_copy(hidden_ref, hidden_out, sems.at[2, 0]))
    copies[-1].start()
    for copy in copies:
        copy.wait()


def call(body, out_shape, ins, name, scratch=(), in_specs=None, out_specs=None, aliases=None):
    cost = int(MICROSECONDS[name] * PEAK / 1e6)
    return pl.pallas_call(
        body,
        out_shape=out_shape,
        in_specs=in_specs or [VMEM] * len(ins),
        out_specs=out_specs or [VMEM] * len(out_shape),
        scratch_shapes=list(scratch),
        input_output_aliases=aliases or {},
        cost_estimate=pl.CostEstimate(flops=cost, transcendentals=0, bytes_accessed=0),
        compiler_params=PARAMS,
        name=name,
    )(*ins)


def per_device(
    theta,
    first_moment,
    second_moment,
    anchor,
    momentum,
    cotangent,
    weights,
    expert_ids,
    expert_counts,
    hidden_saved,
):
    n_island, n_dp, n_expert = (lax.axis_size(name) for name in ("island", "dp", "expert"))
    pairs = n_expert // 2
    units, width = theta.shape[2:]
    length, full_units = hidden_saved.shape[3:]
    part = width // n_island
    first = cut(part)
    split = (n_island - 1) * first
    bf16 = functools.partial(jax.ShapeDtypeStruct, dtype=jnp.bfloat16)

    def ring(value, name, size, shift):
        return lax.ppermute(value, name, [(k, (k + shift) % size) for k in range(size)])

    blocks = list(pack_rows(cotangent, weights, expert_ids, expert_counts, n_island))
    arrived = []
    for k in order(pairs)[:-1]:
        perm = [(2 * z + c, 2 * target(z, k, pairs) + c) for z in range(pairs) for c in range(2)]
        arrived.append(lax.ppermute(blocks[k], "expert", perm))
    saved = hidden_saved.reshape(length, full_units)
    states = [in_hbm(value.reshape(units, width)) for value in (theta, first_moment, second_moment)]
    states = call(
        stage_body,
        [bf16((units, width))] * 3,
        states + [blocks[0]],
        "stage",
        [pltpu.SemaphoreType.DMA((3,))],
        in_specs=[HBM] * 3 + [VMEM],
    )
    saved_all = call(
        functools.partial(split_body, n_dp),
        [bf16((units, length))] * n_dp,
        [saved, blocks[0]],
        "split",
        [pltpu.VMEM((full_units, length), jnp.float32)],
    )
    saved_all = [ring(saved_all[s], "dp", n_dp, s) if s else saved_all[0] for s in range(n_dp)]
    arrived.append(blocks[0])
    one_mine, two_mine = call(
        functools.partial(assemble_body, pairs),
        [bf16((pairs * CAP, columns)) for columns in (split, width - split)],
        arrived + list(states) + saved_all[1:],
        "assemble",
    )
    swap = [(j, j ^ 1) for j in range(n_expert)]

    def spread(mine, other, after=None):
        quarters = [mine, other]
        for shift in range(1, n_dp):
            value = ring(mine, "dp", n_dp, shift)
            if after is not None:
                value, _ = lax.optimization_barrier((value, after))
            quarters += [value, lax.ppermute(value, "expert", swap)]
        return quarters

    one_other = lax.ppermute(one_mine, "expert", swap)
    one_quarters = spread(one_mine, one_other)
    two_other = lax.ppermute(two_mine, "expert", swap)
    (two_mine,) = call(
        rest_body,
        [bf16((pairs * CAP, width - split))],
        [two_mine, two_other, one_other],
        "rest",
    )
    *one, one_slots, left = call(
        functools.partial(one_body, n_dp, n_island, pairs),
        [bf16((units, first))] * (n_island - 1)
        + [bf16((n_dp * length, split)), bf16((units, n_dp * length))],
        one_quarters + saved_all + list(states),
        "far_one",
    )
    theirs = [ring(value, "island", n_island, shift + 1) for shift, value in enumerate(one)]
    two_quarters = spread(two_mine, two_other, left)
    *two, two_slots = call(
        functools.partial(two_body, n_dp, n_island, pairs),
        [bf16((units, part - first))] * (n_island - 1)
        + [bf16((n_dp * length, width - split))],
        two_quarters + [left, *states],
        "far_two",
    )
    theirs += [ring(value, "island", n_island, shift + 1) for shift, value in enumerate(two)]
    hidden = call(
        functools.partial(hidden_body, n_dp, n_island),
        [bf16((units, length))] * n_dp,
        [one_slots, two_slots, states[0]],
        "hidden_grad",
    )
    hidden = [hidden[0]] + [ring(hidden[s], "dp", n_dp, s) for s in range(1, n_dp)]
    (own,) = call(near_body, [bf16((units, part))], [two_slots, left, *states], "near_update")
    outer = [anchor.reshape(units, part), momentum.reshape(units, part), own]
    outer_type = jax.ShapeDtypeStruct((units, part), jnp.float32)
    begun = call(
        functools.partial(outer_one_body, n_island),
        [outer_type, outer_type],
        outer + theirs[: n_island - 1],
        "outer_one",
        [pltpu.VMEM((units, first), jnp.float32)] * 2 + [pltpu.SemaphoreType.DMA((2, 2))],
        out_specs=[HBM, HBM],
    )
    ins = [*begun, *outer, *theirs[n_island - 1 :], *hidden]
    anchor_new, momentum_new, d_hidden = call(
        functools.partial(outer_two_body, n_island, n_dp),
        [outer_type, outer_type, bf16((length, full_units))],
        ins,
        "outer_two",
        [pltpu.VMEM((units, part - first), jnp.float32)] * 2
        + [
            pltpu.VMEM((length, full_units), jnp.bfloat16),
            pltpu.VMEM((full_units, length), jnp.float32),
            pltpu.SemaphoreType.DMA((3, 2)),
        ],
        in_specs=[HBM, HBM] + [VMEM] * (len(ins) - 2),
        out_specs=[HBM, HBM, HBM],
        aliases={0: 0, 1: 1},
    )
    return (
        anchor_new.reshape(anchor.shape),
        momentum_new.reshape(momentum.shape),
        d_hidden.reshape(hidden_saved.shape),
    )


def solution(mesh):
    return jax.shard_map(
        per_device,
        mesh=mesh,
        in_specs=(
            P("island", "expert", "dp", None),
            P("island", "expert", "dp", None),
            P("island", "expert", "dp", None),
            P("expert", "dp", "island"),
            P("expert", "dp", "island"),
            P(("island", "dp", "expert"), None),
            P(("island", "dp", "expert"), None),
            P(("island", "dp", "expert"), None),
            P(("island", "dp", "expert"), None),
            P("island", "dp", "expert", None, None),
        ),
        out_specs=(
            P("expert", "dp", "island"),
            P("expert", "dp", "island"),
            P("island", "dp", "expert", None, None),
        ),
        check_vma=False,
    )
```

```python
import functools

import jax
import jax.numpy as jnp
from jax import lax
from jax.experimental import pallas as pl
from jax.experimental.pallas import tpu as pltpu
from jax.sharding import PartitionSpec as P

FF = 768
CAP = 16

beta_one = 0.9
beta_two = 0.95
adam_epsilon = 1e-08
inner_rate = 0.1
decay_rate = 0.1
outer_beta = 0.9
outer_rate = 0.7

VMEM = pl.BlockSpec(memory_space=pltpu.VMEM)
HBM = pl.BlockSpec(memory_space=pltpu.HBM)
PARAMS = pltpu.CompilerParams(vmem_limit_bytes=48 * 1024 * 1024)


PEAK = 1.15e15
MICROSECONDS = {
    "stage": 1.6,
    "split": 0.1,
    "assemble": 0.05,
    "rest": 0.05,
    "far_one": 0.3,
    "far_two": 0.01,
    "hidden_grad": 0.01,
    "near_update": 0.01,
    "outer_one": 1.1,
    "outer_two": 0.9,
}


def in_hbm(value):
    return pltpu.with_memory_space_constraint(value, pltpu.HBM)


def wrap(value, size):
    return lax.rem(value + size, size)


def target(place, step, size):
    return place ^ step if size & (size - 1) == 0 else (place + step) % size


def order(size):
    return sorted(range(size), key=lambda step: (step == 0, step != size // 2, -step))


def source(place, step, size):
    return place ^ step if size & (size - 1) == 0 else (place - step) % size


def cut(part):
    return part * 5 // 8 // 128 * 128


def pieces(n_island, width):
    part = width // n_island
    first = cut(part)
    island = lax.axis_index("island")
    order = [(shift, 0, first) for shift in range(1, n_island)]
    order += [(shift, first, part - first) for shift in range(1, n_island)]
    order += [(n_island, 0, part)]
    found, at = [], 0
    for shift, skip, size in order:
        column = lax.rem(island + shift, n_island) * part + skip
        found.append((slice(at, at + size), pl.ds(pl.multiple_of(column, 128), size)))
        at += size
    return found


def pack_body(experts, n_island, ids_hbm, weights_hbm, counts_hbm, cot_hbm, *refs):
    outs = refs[:experts]
    ids_ref, weights_ref, counts_ref, cot_ref, sems = refs[experts:]
    copies = [
        pltpu.make_async_copy(src, dst, sems.at[index])
        for index, (src, dst) in enumerate(
            [
                (ids_hbm, ids_ref),
                (weights_hbm, weights_ref),
                (counts_hbm, counts_ref),
                (cot_hbm, cot_ref),
            ]
        )
    ]
    for copy in copies:
        copy.start()
    width, tokens = ids_ref.shape
    rows = experts * CAP
    place = lax.div(lax.axis_index("expert"), 2)
    step = lax.broadcasted_iota(jnp.int32, (experts, CAP, tokens), 0).reshape(rows, tokens)
    expert = target(place, step, experts)
    rank = lax.broadcasted_iota(jnp.int32, (experts, CAP, tokens), 1).reshape(rows, tokens)
    earlier = (
        lax.broadcasted_iota(jnp.int32, (tokens, tokens), 0)
        < lax.broadcasted_iota(jnp.int32, (tokens, tokens), 1)
    )
    earlier = jnp.where(earlier, 1.0, 0.0).astype(jnp.bfloat16)
    for copy in copies[:3]:
        copy.wait()
    named = jnp.zeros((rows, tokens), jnp.float32)
    weight = jnp.zeros((rows, tokens), jnp.float32)
    for slot in range(width):
        hit = ids_ref[slot : slot + 1, :] == expert
        named = jnp.where(hit, 1.0, named)
        weight = jnp.where(hit, weights_ref[slot : slot + 1, :], weight)
    limit = jnp.zeros((rows, tokens), jnp.int32)
    for index in range(experts):
        limit = jnp.where(expert == index, counts_ref[:, index : index + 1], limit)
    found = jnp.dot(named.astype(jnp.bfloat16), earlier, preferred_element_type=jnp.float32)
    found = found.astype(jnp.int32)
    picked = (named > 0.0) & (found < limit) & (found == rank)
    pick = jnp.where(picked, 1.0, 0.0)
    scale = jnp.sum(pick * weight, axis=1, keepdims=True)
    pick = pick.astype(jnp.bfloat16)
    copies[3].wait()
    for at, columns in pieces(n_island, cot_ref.shape[1]):
        gathered = jnp.dot(pick, cot_ref[:, columns], preferred_element_type=jnp.float32)
        packed = (gathered * scale).astype(jnp.bfloat16)
        for index, out in enumerate(outs):
            out[:, at] = packed[index * CAP : (index + 1) * CAP]


def pack_rows(cotangent, weights, expert_ids, counts, n_island):
    experts = counts.shape[1]
    ins = [expert_ids.T, weights.T, counts, cotangent]
    return pl.pallas_call(
        functools.partial(pack_body, experts, n_island),
        out_shape=[jax.ShapeDtypeStruct((CAP, cotangent.shape[1]), jnp.bfloat16)] * experts,
        in_specs=[HBM] * 4,
        out_specs=[VMEM] * experts,
        scratch_shapes=[
            pltpu.VMEM(expert_ids.shape[::-1], jnp.int32),
            pltpu.VMEM(weights.shape[::-1], jnp.float32),
            pltpu.VMEM(counts.shape, jnp.int32),
            pltpu.VMEM(cotangent.shape, jnp.bfloat16),
            pltpu.SemaphoreType.DMA((4,)),
        ],
        compiler_params=PARAMS,
        name="pack",
    )(*[in_hbm(value) for value in ins])


def adam(product, first, second, theta):
    scale = FF ** (-0.5)
    wide = theta.astype(jnp.float32)
    first_new = (inner_rate * beta_one) * first.astype(jnp.float32)
    first_new = first_new + (inner_rate * (1.0 - beta_one) * scale) * product
    second_new = beta_two * second.astype(jnp.float32)
    second_new = second_new + ((1.0 - beta_two) * scale * scale) * (product * product)
    step_size = first_new / (jnp.sqrt(second_new) + adam_epsilon)
    return ((1.0 - inner_rate * decay_rate) * wide - step_size).astype(jnp.bfloat16)


def assemble_body(pairs, *refs):
    blocks, (one_ref, two_ref) = refs[:pairs], refs[-2:]
    split = one_ref.shape[1]
    for index, block in enumerate(blocks):
        rows = slice(index * CAP, (index + 1) * CAP)
        one_ref[rows, :] = block[:, :split]
        two_ref[rows, :] = block[:, split:]


def rest_body(two_ref, *refs):
    refs[-1][...] = two_ref[...]


def stage_body(*refs):
    states, copied, sems = refs[:3], refs[4:7], refs[7]
    copies = [
        pltpu.make_async_copy(src, dst, sems.at[index])
        for index, (src, dst) in enumerate(zip(states, copied))
    ]
    for copy in copies:
        copy.start()
    for copy in copies:
        copy.wait()


def split_body(n_dp, saved_ref, _, *refs):
    *outs, scratch = refs
    units = outs[0].shape[0]
    scratch[...] = saved_ref[...].astype(jnp.float32).T
    for shift, out in enumerate(outs):
        row = pl.multiple_of(lax.rem(lax.axis_index("dp") + shift, n_dp) * units, 8)
        out[...] = scratch[pl.ds(row, units), :].astype(jnp.bfloat16)


def gather_slots(n_dp, pairs, quarters, slots_ref):
    data, position = lax.axis_index("dp"), lax.axis_index("expert")
    core = lax.rem(position, 2)
    place = lax.div(position, 2)
    length = 2 * pairs * CAP
    for shift in range(n_dp):
        group = wrap(data - shift, n_dp)
        for flip in range(2):
            side = core if flip == 0 else 1 - core
            block = quarters[2 * shift + flip]
            for k in range(pairs):
                at = order(pairs).index(k) * CAP
                row = group * length + (2 * source(place, k, pairs) + side) * CAP
                row = pl.multiple_of(row, CAP)
                slots_ref[pl.ds(row, CAP), :] = block[at : at + CAP, :]


def update(left, slots, state_refs, columns):
    product = jnp.dot(left, slots, preferred_element_type=jnp.float32)
    theta, first, second = (ref[:, columns] for ref in state_refs)
    return adam(product, first, second, theta)


def one_body(n_dp, n_island, pairs, *refs):
    quarters = refs[: 2 * n_dp]
    saved = refs[2 * n_dp : 3 * n_dp]
    state_refs = refs[3 * n_dp : 3 * n_dp + 3]
    *outs, slots_ref, left_ref = refs[3 * n_dp + 3 :]
    length = saved[0].shape[1]
    for shift, value in enumerate(saved):
        column = pl.multiple_of(wrap(lax.axis_index("dp") - shift, n_dp) * length, 128)
        left_ref[:, pl.ds(column, length)] = value[...]
    gather_slots(n_dp, pairs, quarters, slots_ref)
    places = pieces(n_island, state_refs[0].shape[1])
    for out, (at, columns) in zip(outs, places):
        out[...] = update(left_ref[...], slots_ref[:, at], state_refs, columns)


def two_body(n_dp, n_island, pairs, *refs):
    quarters = refs[: 2 * n_dp]
    left_ref, *state_refs = refs[2 * n_dp : 2 * n_dp + 4]
    *outs, slots_ref = refs[2 * n_dp + 4 :]
    width = state_refs[0].shape[1]
    first = width - slots_ref.shape[1]
    gather_slots(n_dp, pairs, quarters, slots_ref)
    places = pieces(n_island, width)[n_island - 1 :]
    for out, (at, columns) in zip(outs, places):
        slots = slots_ref[:, at.start - first : at.stop - first]
        out[...] = update(left_ref[...], slots, state_refs, columns)


def hidden_body(n_dp, n_island, one_ref, two_ref, theta_ref, *outs):
    data = lax.axis_index("dp")
    split = one_ref.shape[1]
    length = one_ref.shape[0] // n_dp
    total = None
    for at, columns in pieces(n_island, theta_ref.shape[1]):
        in_one = at.stop <= split
        slots = one_ref[:, at] if in_one else two_ref[:, at.start - split : at.stop - split]
        value = lax.dot_general(
            theta_ref[:, columns],
            slots,
            (((1,), (1,)), ((), ())),
            preferred_element_type=jnp.float32,
        )
        total = value if total is None else total + value
    hidden = (FF ** (-0.5) * total).astype(jnp.bfloat16)
    for shift, out in enumerate(outs):
        for group in range(n_dp):

            @pl.when(lax.rem(data + shift, n_dp) == group)
            def _():
                out[...] = hidden[:, group * length : (group + 1) * length]


def near_body(slots_ref, left_ref, *refs):
    *state_refs, own_ref = refs
    part = own_ref.shape[1]
    columns = pl.ds(pl.multiple_of(lax.axis_index("island") * part, 128), part)
    slots = slots_ref[:, slots_ref.shape[1] - part :]
    own_ref[...] = update(left_ref[...], slots, state_refs, columns)


def outer_step(columns, anchor_ref, momentum_ref, own_ref, theirs, results, outs, sems):
    n_island = len(theirs) + 1
    rows = anchor_ref.shape[0]
    steps = 2 if rows % 16 == 0 else 1
    copies = []
    for step in range(steps):
        at = slice(step * (rows // steps), (step + 1) * (rows // steps))
        total = own_ref[at, columns].astype(jnp.float32)
        for theta in theirs:
            total = total + theta[at, :].astype(jnp.float32)
        anchor = anchor_ref[at, columns]
        mean_delta = anchor - total * (1.0 / n_island)
        momentum_new = outer_beta * momentum_ref[at, columns] + mean_delta
        results[1][at, :] = momentum_new
        results[0][at, :] = anchor - outer_rate * (mean_delta + outer_beta * momentum_new)
        for index in range(2):
            copies.append(
                pltpu.make_async_copy(
                    results[index].at[at, :], outs[index].at[at, columns], sems.at[index, step]
                )
            )
            copies[-1].start()
    return copies


def outer_one_body(n_island, anchor_ref, momentum_ref, own_ref, *refs):
    theirs, outs = refs[: n_island - 1], refs[n_island - 1 : n_island + 1]
    *results, sems = refs[n_island + 1 :]
    columns = slice(0, results[0].shape[1])
    for copy in outer_step(columns, anchor_ref, momentum_ref, own_ref, theirs, results, outs, sems):
        copy.wait()


def outer_two_body(n_island, n_dp, _, __, anchor_ref, momentum_ref, own_ref, *refs):
    theirs, refs = refs[: n_island - 1], refs[n_island - 1 :]
    hidden, refs = refs[:n_dp], refs[n_dp:]
    *outs, hidden_out = refs[:3]
    *results, hidden_ref, scratch, sems = refs[3:]
    data = lax.axis_index("dp")
    units = hidden[0].shape[0]
    for shift, value in enumerate(hidden):
        row = pl.multiple_of(wrap(data - shift, n_dp) * units, 8)
        scratch[pl.ds(row, units), :] = value[...].astype(jnp.float32)
    part = anchor_ref.shape[1]
    columns = slice(part - results[0].shape[1], part)
    copies = outer_step(columns, anchor_ref, momentum_ref, own_ref, theirs, results, outs, sems)
    hidden_ref[...] = scratch[...].T.astype(jnp.bfloat16)
    copies.append(pltpu.make_async_copy(hidden_ref, hidden_out, sems.at[2, 0]))
    copies[-1].start()
    for copy in copies:
        copy.wait()


def call(body, out_shape, ins, name, scratch=(), in_specs=None, out_specs=None, aliases=None):
    cost = int(MICROSECONDS[name] * PEAK / 1e6)
    return pl.pallas_call(
        body,
        out_shape=out_shape,
        in_specs=in_specs or [VMEM] * len(ins),
        out_specs=out_specs or [VMEM] * len(out_shape),
        scratch_shapes=list(scratch),
        input_output_aliases=aliases or {},
        cost_estimate=pl.CostEstimate(flops=cost, transcendentals=0, bytes_accessed=0),
        compiler_params=PARAMS,
        name=name,
    )(*ins)


def per_device(
    theta,
    first_moment,
    second_moment,
    anchor,
    momentum,
    cotangent,
    weights,
    expert_ids,
    expert_counts,
    hidden_saved,
):
    n_island, n_dp, n_expert = (lax.axis_size(name) for name in ("island", "dp", "expert"))
    pairs = n_expert // 2
    units, width = theta.shape[2:]
    length, full_units = hidden_saved.shape[3:]
    part = width // n_island
    first = cut(part)
    split = (n_island - 1) * first
    bf16 = functools.partial(jax.ShapeDtypeStruct, dtype=jnp.bfloat16)

    def ring(value, name, size, shift):
        return lax.ppermute(value, name, [(k, (k + shift) % size) for k in range(size)])

    blocks = list(pack_rows(cotangent, weights, expert_ids, expert_counts, n_island))
    arrived = []
    for k in order(pairs)[:-1]:
        perm = [(2 * z + c, 2 * target(z, k, pairs) + c) for z in range(pairs) for c in range(2)]
        arrived.append(lax.ppermute(blocks[k], "expert", perm))
    saved = hidden_saved.reshape(length, full_units)
    saved_all = call(
        functools.partial(split_body, n_dp),
        [bf16((units, length))] * n_dp,
        [saved, blocks[0]],
        "split",
        [pltpu.VMEM((full_units, length), jnp.float32)],
    )
    saved_all = [ring(saved_all[s], "dp", n_dp, s) if s else saved_all[0] for s in range(n_dp)]
    arrived.append(blocks[0])
    one_mine, two_mine = call(
        functools.partial(assemble_body, pairs),
        [bf16((pairs * CAP, columns)) for columns in (split, width - split)],
        arrived + saved_all[1:],
        "assemble",
    )
    swap = [(j, j ^ 1) for j in range(n_expert)]

    def spread(mine, other, after=None):
        quarters = [mine, other]
        for shift in range(1, n_dp):
            value = ring(mine, "dp", n_dp, shift)
            if after is not None:
                value, _ = lax.optimization_barrier((value, after))
            quarters += [value, lax.ppermute(value, "expert", swap)]
        return quarters

    one_other = lax.ppermute(one_mine, "expert", swap)
    one_quarters = spread(one_mine, one_other)
    two_other = lax.ppermute(two_mine, "expert", swap)
    states = [in_hbm(value.reshape(units, width)) for value in (theta, first_moment, second_moment)]
    states = call(
        stage_body,
        [bf16((units, width))] * 3,
        states + [one_mine],
        "stage",
        [pltpu.SemaphoreType.DMA((3,))],
        in_specs=[HBM] * 3 + [VMEM],
    )
    (two_mine,) = call(
        rest_body,
        [bf16((pairs * CAP, width - split))],
        [two_mine, two_other, one_other, *states],
        "rest",
    )
    *one, one_slots, left = call(
        functools.partial(one_body, n_dp, n_island, pairs),
        [bf16((units, first))] * (n_island - 1)
        + [bf16((n_dp * length, split)), bf16((units, n_dp * length))],
        one_quarters + saved_all + list(states),
        "far_one",
    )
    theirs = [ring(value, "island", n_island, shift + 1) for shift, value in enumerate(one)]
    two_quarters = spread(two_mine, two_other, left)
    *two, two_slots = call(
        functools.partial(two_body, n_dp, n_island, pairs),
        [bf16((units, part - first))] * (n_island - 1)
        + [bf16((n_dp * length, width - split))],
        two_quarters + [left, *states],
        "far_two",
    )
    theirs += [ring(value, "island", n_island, shift + 1) for shift, value in enumerate(two)]
    hidden = call(
        functools.partial(hidden_body, n_dp, n_island),
        [bf16((units, length))] * n_dp,
        [one_slots, two_slots, states[0]],
        "hidden_grad",
    )
    hidden = [hidden[0]] + [ring(hidden[s], "dp", n_dp, s) for s in range(1, n_dp)]
    (own,) = call(near_body, [bf16((units, part))], [two_slots, left, *states], "near_update")
    outer = [anchor.reshape(units, part), momentum.reshape(units, part), own]
    outer_type = jax.ShapeDtypeStruct((units, part), jnp.float32)
    begun = call(
        functools.partial(outer_one_body, n_island),
        [outer_type, outer_type],
        outer + theirs[: n_island - 1],
        "outer_one",
        [pltpu.VMEM((units, first), jnp.float32)] * 2 + [pltpu.SemaphoreType.DMA((2, 2))],
        out_specs=[HBM, HBM],
    )
    ins = [*begun, *outer, *theirs[n_island - 1 :], *hidden]
    anchor_new, momentum_new, d_hidden = call(
        functools.partial(outer_two_body, n_island, n_dp),
        [outer_type, outer_type, bf16((length, full_units))],
        ins,
        "outer_two",
        [pltpu.VMEM((units, part - first), jnp.float32)] * 2
        + [
            pltpu.VMEM((length, full_units), jnp.bfloat16),
            pltpu.VMEM((full_units, length), jnp.float32),
            pltpu.SemaphoreType.DMA((3, 2)),
        ],
        in_specs=[HBM, HBM] + [VMEM] * (len(ins) - 2),
        out_specs=[HBM, HBM, HBM],
        aliases={0: 0, 1: 1},
    )
    return (
        anchor_new.reshape(anchor.shape),
        momentum_new.reshape(momentum.shape),
        d_hidden.reshape(hidden_saved.shape),
    )


def solution(mesh):
    return jax.shard_map(
        per_device,
        mesh=mesh,
        in_specs=(
            P("island", "expert", "dp", None),
            P("island", "expert", "dp", None),
            P("island", "expert", "dp", None),
            P("expert", "dp", "island"),
            P("expert", "dp", "island"),
            P(("island", "dp", "expert"), None),
            P(("island", "dp", "expert"), None),
            P(("island", "dp", "expert"), None),
            P(("island", "dp", "expert"), None),
            P("island", "dp", "expert", None, None),
        ),
        out_specs=(
            P("expert", "dp", "island"),
            P("expert", "dp", "island"),
            P("island", "dp", "expert", None, None),
        ),
        check_vma=False,
    )
```

```python
import functools

import jax
import jax.numpy as jnp
from jax import lax
from jax.experimental import pallas as pl
from jax.experimental.pallas import tpu as pltpu
from jax.sharding import PartitionSpec as P

FF = 768
CAP = 16

beta_one = 0.9
beta_two = 0.95
adam_epsilon = 1e-08
inner_rate = 0.1
decay_rate = 0.1
outer_beta = 0.9
outer_rate = 0.7

VMEM = pl.BlockSpec(memory_space=pltpu.VMEM)
HBM = pl.BlockSpec(memory_space=pltpu.HBM)
PARAMS = pltpu.CompilerParams(vmem_limit_bytes=48 * 1024 * 1024)


PEAK = 1.15e15
MICROSECONDS = {
    "stage": 1.6,
    "split": 0.1,
    "deal": 0.05,
    "assemble_one": 0.05,
    "assemble_two": 0.05,
    "far_one": 0.3,
    "far_two": 0.01,
    "hidden_grad": 0.01,
    "near_update": 0.01,
    "outer_one": 1.1,
    "outer_two": 0.9,
}


def in_hbm(value):
    return pltpu.with_memory_space_constraint(value, pltpu.HBM)


def wrap(value, size):
    return lax.rem(value + size, size)


def target(place, step, size):
    return place ^ step if size & (size - 1) == 0 else (place + step) % size


def order(size):
    return sorted(range(size), key=lambda step: (step == 0, step != size // 2, -step))


def source(place, step, size):
    return place ^ step if size & (size - 1) == 0 else (place - step) % size


def cut(part):
    return part * 5 // 8 // 128 * 128


def pieces(n_island, width):
    part = width // n_island
    first = cut(part)
    island = lax.axis_index("island")
    order = [(shift, 0, first) for shift in range(1, n_island)]
    order += [(shift, first, part - first) for shift in range(1, n_island)]
    order += [(n_island, 0, part)]
    found, at = [], 0
    for shift, skip, size in order:
        column = lax.rem(island + shift, n_island) * part + skip
        found.append((slice(at, at + size), pl.ds(pl.multiple_of(column, 128), size)))
        at += size
    return found


def pack_body(experts, n_island, ids_hbm, weights_hbm, counts_hbm, cot_hbm, *refs):
    *outs, first_ref = refs[: experts + 1]
    ids_ref, weights_ref, counts_ref, cot_ref, sems = refs[experts + 1 :]
    copies = [
        pltpu.make_async_copy(src, dst, sems.at[index])
        for index, (src, dst) in enumerate(
            [
                (ids_hbm, ids_ref),
                (weights_hbm, weights_ref),
                (counts_hbm, counts_ref),
                (cot_hbm, cot_ref),
            ]
        )
    ]
    for copy in copies:
        copy.start()
    width, tokens = ids_ref.shape
    rows = experts * CAP
    place = lax.div(lax.axis_index("expert"), 2)
    step = lax.broadcasted_iota(jnp.int32, (experts, CAP, tokens), 0).reshape(rows, tokens)
    expert = target(place, step, experts)
    rank = lax.broadcasted_iota(jnp.int32, (experts, CAP, tokens), 1).reshape(rows, tokens)
    earlier = (
        lax.broadcasted_iota(jnp.int32, (tokens, tokens), 0)
        < lax.broadcasted_iota(jnp.int32, (tokens, tokens), 1)
    )
    earlier = jnp.where(earlier, 1.0, 0.0).astype(jnp.bfloat16)
    for copy in copies[:3]:
        copy.wait()
    named = jnp.zeros((rows, tokens), jnp.float32)
    weight = jnp.zeros((rows, tokens), jnp.float32)
    for slot in range(width):
        hit = ids_ref[slot : slot + 1, :] == expert
        named = jnp.where(hit, 1.0, named)
        weight = jnp.where(hit, weights_ref[slot : slot + 1, :], weight)
    limit = jnp.zeros((rows, tokens), jnp.int32)
    for index in range(experts):
        limit = jnp.where(expert == index, counts_ref[:, index : index + 1], limit)
    found = jnp.dot(named.astype(jnp.bfloat16), earlier, preferred_element_type=jnp.float32)
    found = found.astype(jnp.int32)
    picked = (named > 0.0) & (found < limit) & (found == rank)
    pick = jnp.where(picked, 1.0, 0.0)
    scale = jnp.sum(pick * weight, axis=1, keepdims=True)
    pick = pick.astype(jnp.bfloat16)
    copies[3].wait()
    for at, columns in pieces(n_island, cot_ref.shape[1]):
        gathered = jnp.dot(pick, cot_ref[:, columns], preferred_element_type=jnp.float32)
        packed = (gathered * scale).astype(jnp.bfloat16)
        for index, out in enumerate(outs):
            out[:, at] = packed[index * CAP : (index + 1) * CAP]
        if at.stop <= first_ref.shape[1]:
            first_ref[:, at] = packed


def pack_rows(cotangent, weights, expert_ids, counts, n_island):
    experts = counts.shape[1]
    width = cotangent.shape[1]
    split = (n_island - 1) * cut(width // n_island)
    ins = [expert_ids.T, weights.T, counts, cotangent]
    return pl.pallas_call(
        functools.partial(pack_body, experts, n_island),
        out_shape=[jax.ShapeDtypeStruct((CAP, width), jnp.bfloat16)] * experts
        + [jax.ShapeDtypeStruct((experts * CAP, split), jnp.bfloat16)],
        in_specs=[HBM] * 4,
        out_specs=[VMEM] * (experts + 1),
        scratch_shapes=[
            pltpu.VMEM(expert_ids.shape[::-1], jnp.int32),
            pltpu.VMEM(weights.shape[::-1], jnp.float32),
            pltpu.VMEM(counts.shape, jnp.int32),
            pltpu.VMEM(cotangent.shape, jnp.bfloat16),
            pltpu.SemaphoreType.DMA((4,)),
        ],
        compiler_params=PARAMS,
        name="pack",
    )(*[in_hbm(value) for value in ins])


def adam(product, first, second, theta):
    scale = FF ** (-0.5)
    wide = theta.astype(jnp.float32)
    first_new = (inner_rate * beta_one) * first.astype(jnp.float32)
    first_new = first_new + (inner_rate * (1.0 - beta_one) * scale) * product
    second_new = beta_two * second.astype(jnp.float32)
    second_new = second_new + ((1.0 - beta_two) * scale * scale) * (product * product)
    step_size = first_new / (jnp.sqrt(second_new) + adam_epsilon)
    return ((1.0 - inner_rate * decay_rate) * wide - step_size).astype(jnp.bfloat16)


def deal_body(first_ref, *outs):
    for index, out in enumerate(outs):
        out[...] = first_ref[(index + 1) * CAP : (index + 2) * CAP, :]


def assemble_one_body(n_dp, pairs, *refs):
    out_ref = refs[-1]
    split = out_ref.shape[1]
    for index in range(n_dp * pairs):
        value = refs[index][:CAP, :split]
        out_ref[index * CAP : (index + 1) * CAP, :] = value


def assemble_two_body(pairs, *refs):
    out_ref = refs[-1]
    for index, block in enumerate(refs[:pairs]):
        rows = slice(index * CAP, (index + 1) * CAP)
        out_ref[rows, :] = block[:, block.shape[1] - out_ref.shape[1] :]


def stage_body(*refs):
    states, copied, sems = refs[:3], refs[4:7], refs[7]
    copies = [
        pltpu.make_async_copy(src, dst, sems.at[index])
        for index, (src, dst) in enumerate(zip(states, copied))
    ]
    for copy in copies:
        copy.start()
    for copy in copies:
        copy.wait()


def split_body(n_dp, saved_ref, _, *refs):
    *outs, scratch = refs
    units = outs[0].shape[0]
    scratch[...] = saved_ref[...].astype(jnp.float32).T
    for shift, out in enumerate(outs):
        row = pl.multiple_of(lax.rem(lax.axis_index("dp") + shift, n_dp) * units, 8)
        out[...] = scratch[pl.ds(row, units), :].astype(jnp.bfloat16)


def gather_slots(n_dp, pairs, quarters, slots_ref):
    data, position = lax.axis_index("dp"), lax.axis_index("expert")
    core = lax.rem(position, 2)
    place = lax.div(position, 2)
    length = 2 * pairs * CAP
    for shift in range(n_dp):
        group = wrap(data - shift, n_dp)
        for flip in range(2):
            side = core if flip == 0 else 1 - core
            if len(quarters) == 2:
                block, skip = quarters[flip], shift * pairs * CAP
            else:
                block, skip = quarters[2 * shift + flip], 0
            for k in range(pairs):
                at = skip + order(pairs).index(k) * CAP
                row = group * length + (2 * source(place, k, pairs) + side) * CAP
                row = pl.multiple_of(row, CAP)
                slots_ref[pl.ds(row, CAP), :] = block[at : at + CAP, :]


def update(left, slots, state_refs, columns):
    product = jnp.dot(left, slots, preferred_element_type=jnp.float32)
    theta, first, second = (ref[:, columns] for ref in state_refs)
    return adam(product, first, second, theta)


def one_body(n_dp, n_island, pairs, *refs):
    quarters, refs = refs[:2], refs[2:]
    saved, state_refs = refs[:n_dp], refs[n_dp : n_dp + 3]
    *outs, slots_ref, left_ref = refs[n_dp + 3 :]
    length = saved[0].shape[1]
    for shift, value in enumerate(saved):
        column = pl.multiple_of(wrap(lax.axis_index("dp") - shift, n_dp) * length, 128)
        left_ref[:, pl.ds(column, length)] = value[...]
    gather_slots(n_dp, pairs, quarters, slots_ref)
    places = pieces(n_island, state_refs[0].shape[1])
    for out, (at, columns) in zip(outs, places):
        out[...] = update(left_ref[...], slots_ref[:, at], state_refs, columns)


def two_body(n_dp, n_island, pairs, *refs):
    quarters = refs[: 2 * n_dp]
    left_ref, *state_refs = refs[2 * n_dp : 2 * n_dp + 4]
    *outs, slots_ref = refs[2 * n_dp + 4 :]
    width = state_refs[0].shape[1]
    first = width - slots_ref.shape[1]
    gather_slots(n_dp, pairs, quarters, slots_ref)
    places = pieces(n_island, width)[n_island - 1 :]
    for out, (at, columns) in zip(outs, places):
        slots = slots_ref[:, at.start - first : at.stop - first]
        out[...] = update(left_ref[...], slots, state_refs, columns)


def hidden_body(n_dp, n_island, one_ref, two_ref, theta_ref, *outs):
    data = lax.axis_index("dp")
    split = one_ref.shape[1]
    length = one_ref.shape[0] // n_dp
    total = None
    for at, columns in pieces(n_island, theta_ref.shape[1]):
        in_one = at.stop <= split
        slots = one_ref[:, at] if in_one else two_ref[:, at.start - split : at.stop - split]
        value = lax.dot_general(
            theta_ref[:, columns],
            slots,
            (((1,), (1,)), ((), ())),
            preferred_element_type=jnp.float32,
        )
        total = value if total is None else total + value
    hidden = (FF ** (-0.5) * total).astype(jnp.bfloat16)
    for shift, out in enumerate(outs):
        for group in range(n_dp):

            @pl.when(lax.rem(data + shift, n_dp) == group)
            def _():
                out[...] = hidden[:, group * length : (group + 1) * length]


def near_body(slots_ref, left_ref, *refs):
    *state_refs, own_ref = refs
    part = own_ref.shape[1]
    columns = pl.ds(pl.multiple_of(lax.axis_index("island") * part, 128), part)
    slots = slots_ref[:, slots_ref.shape[1] - part :]
    own_ref[...] = update(left_ref[...], slots, state_refs, columns)


def outer_step(columns, anchor_ref, momentum_ref, own_ref, theirs, results, outs, sems):
    n_island = len(theirs) + 1
    rows = anchor_ref.shape[0]
    steps = 2 if rows % 16 == 0 else 1
    copies = []
    for step in range(steps):
        at = slice(step * (rows // steps), (step + 1) * (rows // steps))
        total = own_ref[at, columns].astype(jnp.float32)
        for theta in theirs:
            total = total + theta[at, :].astype(jnp.float32)
        anchor = anchor_ref[at, columns]
        mean_delta = anchor - total * (1.0 / n_island)
        momentum_new = outer_beta * momentum_ref[at, columns] + mean_delta
        results[1][at, :] = momentum_new
        results[0][at, :] = anchor - outer_rate * (mean_delta + outer_beta * momentum_new)
        for index in range(2):
            copies.append(
                pltpu.make_async_copy(
                    results[index].at[at, :], outs[index].at[at, columns], sems.at[index, step]
                )
            )
            copies[-1].start()
    return copies


def outer_one_body(n_island, anchor_ref, momentum_ref, own_ref, *refs):
    theirs, outs = refs[: n_island - 1], refs[n_island - 1 : n_island + 1]
    *results, sems = refs[n_island + 1 :]
    columns = slice(0, results[0].shape[1])
    for copy in outer_step(columns, anchor_ref, momentum_ref, own_ref, theirs, results, outs, sems):
        copy.wait()


def outer_two_body(n_island, n_dp, _, __, anchor_ref, momentum_ref, own_ref, *refs):
    theirs, refs = refs[: n_island - 1], refs[n_island - 1 :]
    hidden, refs = refs[:n_dp], refs[n_dp:]
    *outs, hidden_out = refs[:3]
    *results, hidden_ref, scratch, sems = refs[3:]
    data = lax.axis_index("dp")
    units = hidden[0].shape[0]
    for shift, value in enumerate(hidden):
        row = pl.multiple_of(wrap(data - shift, n_dp) * units, 8)
        scratch[pl.ds(row, units), :] = value[...].astype(jnp.float32)
    part = anchor_ref.shape[1]
    columns = slice(part - results[0].shape[1], part)
    copies = outer_step(columns, anchor_ref, momentum_ref, own_ref, theirs, results, outs, sems)
    hidden_ref[...] = scratch[...].T.astype(jnp.bfloat16)
    copies.append(pltpu.make_async_copy(hidden_ref, hidden_out, sems.at[2, 0]))
    copies[-1].start()
    for copy in copies:
        copy.wait()


def call(body, out_shape, ins, name, scratch=(), in_specs=None, out_specs=None, aliases=None):
    cost = int(MICROSECONDS[name] * PEAK / 1e6)
    return pl.pallas_call(
        body,
        out_shape=out_shape,
        in_specs=in_specs or [VMEM] * len(ins),
        out_specs=out_specs or [VMEM] * len(out_shape),
        scratch_shapes=list(scratch),
        input_output_aliases=aliases or {},
        cost_estimate=pl.CostEstimate(flops=cost, transcendentals=0, bytes_accessed=0),
        compiler_params=PARAMS,
        name=name,
    )(*ins)


def per_device(
    theta,
    first_moment,
    second_moment,
    anchor,
    momentum,
    cotangent,
    weights,
    expert_ids,
    expert_counts,
    hidden_saved,
):
    n_island, n_dp, n_expert = (lax.axis_size(name) for name in ("island", "dp", "expert"))
    pairs = n_expert // 2
    units, width = theta.shape[2:]
    length, full_units = hidden_saved.shape[3:]
    part = width // n_island
    first = cut(part)
    split = (n_island - 1) * first
    bf16 = functools.partial(jax.ShapeDtypeStruct, dtype=jnp.bfloat16)

    def ring(value, name, size, shift):
        return lax.ppermute(value, name, [(k, (k + shift) % size) for k in range(size)])

    *blocks, first_all = pack_rows(cotangent, weights, expert_ids, expert_counts, n_island)

    def over_z(value, k):
        perm = [(2 * z + c, 2 * target(z, k, pairs) + c) for z in range(pairs) for c in range(2)]
        return lax.ppermute(value, "expert", perm)

    groups = []
    for shift in range(1, n_dp):
        theirs = ring(first_all, "dp", n_dp, shift)
        dealt = call(deal_body, [bf16((CAP, split))] * (pairs - 1), [theirs], "deal")
        groups += [over_z(dealt[k - 1], k) if k else theirs for k in order(pairs)]
    arrived = [over_z(blocks[k], k) if k else blocks[k] for k in order(pairs)]
    states = [in_hbm(value.reshape(units, width)) for value in (theta, first_moment, second_moment)]
    states = call(
        stage_body,
        [bf16((units, width))] * 3,
        states + [blocks[0]],
        "stage",
        [pltpu.SemaphoreType.DMA((3,))],
        in_specs=[HBM] * 3 + [VMEM],
    )
    saved = hidden_saved.reshape(length, full_units)
    saved_all = call(
        functools.partial(split_body, n_dp),
        [bf16((units, length))] * n_dp,
        [saved, blocks[0]],
        "split",
        [pltpu.VMEM((full_units, length), jnp.float32)],
    )
    saved_all = [ring(saved_all[s], "dp", n_dp, s) if s else saved_all[0] for s in range(n_dp)]
    swap = [(j, j ^ 1) for j in range(n_expert)]
    (two_mine,) = call(
        functools.partial(assemble_two_body, pairs),
        [bf16((pairs * CAP, width - split))],
        arrived + saved_all[1:],
        "assemble_two",
    )
    (one_mine,) = call(
        functools.partial(assemble_one_body, n_dp, pairs),
        [bf16((n_dp * pairs * CAP, split))],
        arrived + groups + list(states),
        "assemble_one",
    )
    one_quarters = [one_mine, lax.ppermute(one_mine, "expert", swap)]
    two_other = lax.ppermute(two_mine, "expert", swap)

    def spread(mine, other, after):
        quarters = [mine, other]
        for shift in range(1, n_dp):
            value = ring(mine, "dp", n_dp, shift)
            value, _ = lax.optimization_barrier((value, after))
            quarters += [value, lax.ppermute(value, "expert", swap)]
        return quarters

    *one, one_slots, left = call(
        functools.partial(one_body, n_dp, n_island, pairs),
        [bf16((units, first))] * (n_island - 1)
        + [bf16((n_dp * length, split)), bf16((units, n_dp * length))],
        one_quarters + saved_all + list(states),
        "far_one",
    )
    theirs = [ring(value, "island", n_island, shift + 1) for shift, value in enumerate(one)]
    two_quarters = spread(two_mine, two_other, left)
    *two, two_slots = call(
        functools.partial(two_body, n_dp, n_island, pairs),
        [bf16((units, part - first))] * (n_island - 1)
        + [bf16((n_dp * length, width - split))],
        two_quarters + [left, *states],
        "far_two",
    )
    theirs += [ring(value, "island", n_island, shift + 1) for shift, value in enumerate(two)]
    hidden = call(
        functools.partial(hidden_body, n_dp, n_island),
        [bf16((units, length))] * n_dp,
        [one_slots, two_slots, states[0]],
        "hidden_grad",
    )
    hidden = [hidden[0]] + [ring(hidden[s], "dp", n_dp, s) for s in range(1, n_dp)]
    (own,) = call(near_body, [bf16((units, part))], [two_slots, left, *states], "near_update")
    outer = [anchor.reshape(units, part), momentum.reshape(units, part), own]
    outer_type = jax.ShapeDtypeStruct((units, part), jnp.float32)
    begun = call(
        functools.partial(outer_one_body, n_island),
        [outer_type, outer_type],
        outer + theirs[: n_island - 1],
        "outer_one",
        [pltpu.VMEM((units, first), jnp.float32)] * 2 + [pltpu.SemaphoreType.DMA((2, 2))],
        out_specs=[HBM, HBM],
    )
    ins = [*begun, *outer, *theirs[n_island - 1 :], *hidden]
    anchor_new, momentum_new, d_hidden = call(
        functools.partial(outer_two_body, n_island, n_dp),
        [outer_type, outer_type, bf16((length, full_units))],
        ins,
        "outer_two",
        [pltpu.VMEM((units, part - first), jnp.float32)] * 2
        + [
            pltpu.VMEM((length, full_units), jnp.bfloat16),
            pltpu.VMEM((full_units, length), jnp.float32),
            pltpu.SemaphoreType.DMA((3, 2)),
        ],
        in_specs=[HBM, HBM] + [VMEM] * (len(ins) - 2),
        out_specs=[HBM, HBM, HBM],
        aliases={0: 0, 1: 1},
    )
    return (
        anchor_new.reshape(anchor.shape),
        momentum_new.reshape(momentum.shape),
        d_hidden.reshape(hidden_saved.shape),
    )


def solution(mesh):
    return jax.shard_map(
        per_device,
        mesh=mesh,
        in_specs=(
            P("island", "expert", "dp", None),
            P("island", "expert", "dp", None),
            P("island", "expert", "dp", None),
            P("expert", "dp", "island"),
            P("expert", "dp", "island"),
            P(("island", "dp", "expert"), None),
            P(("island", "dp", "expert"), None),
            P(("island", "dp", "expert"), None),
            P(("island", "dp", "expert"), None),
            P("island", "dp", "expert", None, None),
        ),
        out_specs=(
            P("expert", "dp", "island"),
            P("expert", "dp", "island"),
            P("island", "dp", "expert", None, None),
        ),
        check_vma=False,
    )
```

```python
import functools

import jax
import jax.numpy as jnp
from jax import lax
from jax.experimental import pallas as pl
from jax.experimental.pallas import tpu as pltpu
from jax.sharding import PartitionSpec as P

FF = 768
CAP = 16

beta_one = 0.9
beta_two = 0.95
adam_epsilon = 1e-08
inner_rate = 0.1
decay_rate = 0.1
outer_beta = 0.9
outer_rate = 0.7

VMEM = pl.BlockSpec(memory_space=pltpu.VMEM)
HBM = pl.BlockSpec(memory_space=pltpu.HBM)
PARAMS = pltpu.CompilerParams(vmem_limit_bytes=48 * 1024 * 1024)


PEAK = 1.15e15
MICROSECONDS = {
    "stage": 1.6,
    "deal": 0.05,
    "assemble_one": 0.05,
    "assemble_two": 0.05,
    "far_one": 0.01,
    "far_two": 0.01,
    "hidden_grad": 0.01,
    "near_update": 0.01,
    "outer_one": 1.1,
    "outer_two": 0.9,
}


def in_hbm(value):
    return pltpu.with_memory_space_constraint(value, pltpu.HBM)


def wrap(value, size):
    return lax.rem(value + size, size)


def target(place, step, size):
    return place ^ step if size & (size - 1) == 0 else (place + step) % size


def order(size):
    return sorted(range(size), key=lambda step: (step == 0, step != size // 2, -step))


def source(place, step, size):
    return place ^ step if size & (size - 1) == 0 else (place - step) % size


def cut(part):
    return part * 5 // 8 // 128 * 128


def pieces(n_island, width):
    part = width // n_island
    first = cut(part)
    island = lax.axis_index("island")
    order = [(shift, 0, first) for shift in range(1, n_island)]
    order += [(shift, first, part - first) for shift in range(1, n_island)]
    order += [(n_island, 0, part)]
    found, at = [], 0
    for shift, skip, size in order:
        column = lax.rem(island + shift, n_island) * part + skip
        found.append((slice(at, at + size), pl.ds(pl.multiple_of(column, 128), size)))
        at += size
    return found


def tiles(units, length, width):
    places = [(row, column) for row in range(0, units, 16) for column in range(0, length, 128)]
    across = width // 128
    return [
        (row, column, index // across * 16, index % across * 128)
        for index, (row, column) in enumerate(places)
    ]


def pack_body(
    experts, n_island, n_dp, ids_hbm, weights_hbm, counts_hbm, cot_hbm, saved_hbm, *refs
):
    outs, refs = refs[:experts], refs[experts:]
    own_ref, firsts, refs = refs[0], refs[1:n_dp], refs[n_dp:]
    ids_ref, weights_ref, counts_ref, cot_ref, saved_ref, turned, sems = refs
    copies = [
        pltpu.make_async_copy(src, dst, sems.at[index])
        for index, (src, dst) in enumerate(
            [
                (ids_hbm, ids_ref),
                (weights_hbm, weights_ref),
                (counts_hbm, counts_ref),
                (cot_hbm, cot_ref),
                (saved_hbm, saved_ref),
            ]
        )
    ]
    for copy in copies:
        copy.start()
    width, tokens = ids_ref.shape
    rows = experts * CAP
    place = lax.div(lax.axis_index("expert"), 2)
    step = lax.broadcasted_iota(jnp.int32, (experts, CAP, tokens), 0).reshape(rows, tokens)
    expert = target(place, step, experts)
    rank = lax.broadcasted_iota(jnp.int32, (experts, CAP, tokens), 1).reshape(rows, tokens)
    earlier = (
        lax.broadcasted_iota(jnp.int32, (tokens, tokens), 0)
        < lax.broadcasted_iota(jnp.int32, (tokens, tokens), 1)
    )
    earlier = jnp.where(earlier, 1.0, 0.0).astype(jnp.bfloat16)
    for copy in copies[:3]:
        copy.wait()
    named = jnp.zeros((rows, tokens), jnp.float32)
    weight = jnp.zeros((rows, tokens), jnp.float32)
    for slot in range(width):
        hit = ids_ref[slot : slot + 1, :] == expert
        named = jnp.where(hit, 1.0, named)
        weight = jnp.where(hit, weights_ref[slot : slot + 1, :], weight)
    limit = jnp.zeros((rows, tokens), jnp.int32)
    for index in range(experts):
        limit = jnp.where(expert == index, counts_ref[:, index : index + 1], limit)
    found = jnp.dot(named.astype(jnp.bfloat16), earlier, preferred_element_type=jnp.float32)
    found = found.astype(jnp.int32)
    picked = (named > 0.0) & (found < limit) & (found == rank)
    pick = jnp.where(picked, 1.0, 0.0)
    scale = jnp.sum(pick * weight, axis=1, keepdims=True)
    pick = pick.astype(jnp.bfloat16)
    copies[4].wait()
    turned[...] = saved_ref[...].astype(jnp.float32).T
    units, length = own_ref.shape
    for shift in range(n_dp):
        row = pl.multiple_of(lax.rem(lax.axis_index("dp") + shift, n_dp) * units, 8)
        value = turned[pl.ds(row, units), :].astype(jnp.bfloat16)
        if shift == 0:
            own_ref[...] = value
            continue
        first = firsts[shift - 1]
        first[rows:, :] = jnp.zeros((first.shape[0] - rows, first.shape[1]), jnp.bfloat16)
        for at_row, at_column, to_row, to_column in tiles(units, length, first.shape[1]):
            first[rows + to_row : rows + to_row + 16, to_column : to_column + 128] = value[
                at_row : at_row + 16, at_column : at_column + 128
            ]
    copies[3].wait()
    for at, columns in pieces(n_island, cot_ref.shape[1]):
        gathered = jnp.dot(pick, cot_ref[:, columns], preferred_element_type=jnp.float32)
        packed = (gathered * scale).astype(jnp.bfloat16)
        for index, out in enumerate(outs):
            out[:, at] = packed[index * CAP : (index + 1) * CAP]
        for first in firsts:
            if at.stop <= first.shape[1]:
                first[:rows, at] = packed


def pack_rows(cotangent, weights, expert_ids, counts, saved, n_island, n_dp):
    experts = counts.shape[1]
    width = cotangent.shape[1]
    split = (n_island - 1) * cut(width // n_island)
    length, full_units = saved.shape
    units = full_units // n_dp
    below = tiles(units, length, split)[-1][2] + 16
    bf16 = functools.partial(jax.ShapeDtypeStruct, dtype=jnp.bfloat16)
    outs = [bf16((CAP, width))] * experts + [bf16((units, length))]
    outs += [bf16((experts * CAP + below, split))] * (n_dp - 1)
    ins = [expert_ids.T, weights.T, counts, cotangent, saved]
    return pl.pallas_call(
        functools.partial(pack_body, experts, n_island, n_dp),
        out_shape=outs,
        in_specs=[HBM] * len(ins),
        out_specs=[VMEM] * len(outs),
        scratch_shapes=[
            pltpu.VMEM(expert_ids.shape[::-1], jnp.int32),
            pltpu.VMEM(weights.shape[::-1], jnp.float32),
            pltpu.VMEM(counts.shape, jnp.int32),
            pltpu.VMEM(cotangent.shape, jnp.bfloat16),
            pltpu.VMEM(saved.shape, jnp.bfloat16),
            pltpu.VMEM(saved.shape[::-1], jnp.float32),
            pltpu.SemaphoreType.DMA((len(ins),)),
        ],
        compiler_params=PARAMS,
        name="pack",
    )(*[in_hbm(value) for value in ins])


def adam(product, first, second, theta):
    scale = FF ** (-0.5)
    wide = theta.astype(jnp.float32)
    first_new = (inner_rate * beta_one) * first.astype(jnp.float32)
    first_new = first_new + (inner_rate * (1.0 - beta_one) * scale) * product
    second_new = beta_two * second.astype(jnp.float32)
    second_new = second_new + ((1.0 - beta_two) * scale * scale) * (product * product)
    step_size = first_new / (jnp.sqrt(second_new) + adam_epsilon)
    return ((1.0 - inner_rate * decay_rate) * wide - step_size).astype(jnp.bfloat16)


def deal_body(first_ref, *outs):
    for index, out in enumerate(outs):
        out[...] = first_ref[(index + 1) * CAP : (index + 2) * CAP, :]


def assemble_one_body(n_dp, pairs, *refs):
    out_ref = refs[-1]
    split = out_ref.shape[1]
    for index in range(n_dp * pairs):
        value = refs[index][:CAP, :split]
        out_ref[index * CAP : (index + 1) * CAP, :] = value


def assemble_two_body(pairs, *refs):
    out_ref = refs[-1]
    for index, block in enumerate(refs[:pairs]):
        rows = slice(index * CAP, (index + 1) * CAP)
        out_ref[rows, :] = block[:, block.shape[1] - out_ref.shape[1] :]


def stage_body(*refs):
    states, copied, sems = refs[:3], refs[4:7], refs[7]
    copies = [
        pltpu.make_async_copy(src, dst, sems.at[index])
        for index, (src, dst) in enumerate(zip(states, copied))
    ]
    for copy in copies:
        copy.start()
    for copy in copies:
        copy.wait()


def gather_slots(n_dp, pairs, quarters, slots_ref):
    data, position = lax.axis_index("dp"), lax.axis_index("expert")
    core = lax.rem(position, 2)
    place = lax.div(position, 2)
    length = 2 * pairs * CAP
    for shift in range(n_dp):
        group = wrap(data - shift, n_dp)
        for flip in range(2):
            side = core if flip == 0 else 1 - core
            if len(quarters) == 2:
                block, skip = quarters[flip], shift * pairs * CAP
            else:
                block, skip = quarters[2 * shift + flip], 0
            for k in range(pairs):
                at = skip + order(pairs).index(k) * CAP
                row = group * length + (2 * source(place, k, pairs) + side) * CAP
                row = pl.multiple_of(row, CAP)
                slots_ref[pl.ds(row, CAP), :] = block[at : at + CAP, :]


def update(left, slots, state_refs, columns):
    product = jnp.dot(left, slots, preferred_element_type=jnp.float32)
    theta, first, second = (ref[:, columns] for ref in state_refs)
    return adam(product, first, second, theta)


def one_body(n_dp, n_island, pairs, *refs):
    quarters, refs = refs[:2], refs[2:]
    saved, state_refs = refs[:n_dp], refs[n_dp : n_dp + 3]
    *outs, slots_ref, left_ref = refs[n_dp + 3 :]
    length = saved[0].shape[1]
    units = left_ref.shape[0]
    for shift, value in enumerate(saved):
        group = pl.multiple_of(wrap(lax.axis_index("dp") - shift, n_dp) * length, 128)
        if shift == 0:
            left_ref[:, pl.ds(group, length)] = value[...]
            continue
        for row, column, to_row, to_column in tiles(units, length, value.shape[1]):
            to_row += pairs * CAP
            left_ref[row : row + 16, pl.ds(pl.multiple_of(group + column, 128), 128)] = value[
                to_row : to_row + 16, to_column : to_column + 128
            ]
    gather_slots(n_dp, pairs, quarters, slots_ref)
    places = pieces(n_island, state_refs[0].shape[1])
    for out, (at, columns) in zip(outs, places):
        out[...] = update(left_ref[...], slots_ref[:, at], state_refs, columns)


def two_body(n_dp, n_island, pairs, *refs):
    quarters = refs[: 2 * n_dp]
    left_ref, *state_refs = refs[2 * n_dp : 2 * n_dp + 4]
    *outs, slots_ref = refs[2 * n_dp + 4 :]
    width = state_refs[0].shape[1]
    first = width - slots_ref.shape[1]
    gather_slots(n_dp, pairs, quarters, slots_ref)
    places = pieces(n_island, width)[n_island - 1 :]
    for out, (at, columns) in zip(outs, places):
        slots = slots_ref[:, at.start - first : at.stop - first]
        out[...] = update(left_ref[...], slots, state_refs, columns)


def hidden_body(n_dp, n_island, one_ref, two_ref, theta_ref, *outs):
    data = lax.axis_index("dp")
    split = one_ref.shape[1]
    length = one_ref.shape[0] // n_dp
    total = None
    for at, columns in pieces(n_island, theta_ref.shape[1]):
        in_one = at.stop <= split
        slots = one_ref[:, at] if in_one else two_ref[:, at.start - split : at.stop - split]
        value = lax.dot_general(
            theta_ref[:, columns],
            slots,
            (((1,), (1,)), ((), ())),
            preferred_element_type=jnp.float32,
        )
        total = value if total is None else total + value
    hidden = (FF ** (-0.5) * total).astype(jnp.bfloat16)
    for shift, out in enumerate(outs):
        for group in range(n_dp):

            @pl.when(lax.rem(data + shift, n_dp) == group)
            def _():
                out[...] = hidden[:, group * length : (group + 1) * length]


def near_body(slots_ref, left_ref, *refs):
    *state_refs, own_ref = refs
    part = own_ref.shape[1]
    columns = pl.ds(pl.multiple_of(lax.axis_index("island") * part, 128), part)
    slots = slots_ref[:, slots_ref.shape[1] - part :]
    own_ref[...] = update(left_ref[...], slots, state_refs, columns)


def outer_step(columns, anchor_ref, momentum_ref, own_ref, theirs, results, outs, sems):
    n_island = len(theirs) + 1
    rows = anchor_ref.shape[0]
    steps = 2 if rows % 16 == 0 else 1
    copies = []
    for step in range(steps):
        at = slice(step * (rows // steps), (step + 1) * (rows // steps))
        total = own_ref[at, columns].astype(jnp.float32)
        for theta in theirs:
            total = total + theta[at, :].astype(jnp.float32)
        anchor = anchor_ref[at, columns]
        mean_delta = anchor - total * (1.0 / n_island)
        momentum_new = outer_beta * momentum_ref[at, columns] + mean_delta
        results[1][at, :] = momentum_new
        results[0][at, :] = anchor - outer_rate * (mean_delta + outer_beta * momentum_new)
        for index in range(2):
            copies.append(
                pltpu.make_async_copy(
                    results[index].at[at, :], outs[index].at[at, columns], sems.at[index, step]
                )
            )
            copies[-1].start()
    return copies


def outer_one_body(n_island, anchor_ref, momentum_ref, own_ref, *refs):
    theirs, outs = refs[: n_island - 1], refs[n_island - 1 : n_island + 1]
    *results, sems = refs[n_island + 1 :]
    columns = slice(0, results[0].shape[1])
    for copy in outer_step(columns, anchor_ref, momentum_ref, own_ref, theirs, results, outs, sems):
        copy.wait()


def outer_two_body(n_island, n_dp, _, __, anchor_ref, momentum_ref, own_ref, *refs):
    theirs, refs = refs[: n_island - 1], refs[n_island - 1 :]
    hidden, refs = refs[:n_dp], refs[n_dp:]
    *outs, hidden_out = refs[:3]
    *results, hidden_ref, scratch, sems = refs[3:]
    data = lax.axis_index("dp")
    units = hidden[0].shape[0]
    for shift, value in enumerate(hidden):
        row = pl.multiple_of(wrap(data - shift, n_dp) * units, 8)
        scratch[pl.ds(row, units), :] = value[...].astype(jnp.float32)
    part = anchor_ref.shape[1]
    columns = slice(part - results[0].shape[1], part)
    copies = outer_step(columns, anchor_ref, momentum_ref, own_ref, theirs, results, outs, sems)
    hidden_ref[...] = scratch[...].T.astype(jnp.bfloat16)
    copies.append(pltpu.make_async_copy(hidden_ref, hidden_out, sems.at[2, 0]))
    copies[-1].start()
    for copy in copies:
        copy.wait()


def call(body, out_shape, ins, name, scratch=(), in_specs=None, out_specs=None, aliases=None):
    cost = int(MICROSECONDS[name] * PEAK / 1e6)
    return pl.pallas_call(
        body,
        out_shape=out_shape,
        in_specs=in_specs or [VMEM] * len(ins),
        out_specs=out_specs or [VMEM] * len(out_shape),
        scratch_shapes=list(scratch),
        input_output_aliases=aliases or {},
        cost_estimate=pl.CostEstimate(flops=cost, transcendentals=0, bytes_accessed=0),
        compiler_params=PARAMS,
        name=name,
    )(*ins)


def per_device(
    theta,
    first_moment,
    second_moment,
    anchor,
    momentum,
    cotangent,
    weights,
    expert_ids,
    expert_counts,
    hidden_saved,
):
    n_island, n_dp, n_expert = (lax.axis_size(name) for name in ("island", "dp", "expert"))
    pairs = n_expert // 2
    units, width = theta.shape[2:]
    length, full_units = hidden_saved.shape[3:]
    part = width // n_island
    first = cut(part)
    split = (n_island - 1) * first
    bf16 = functools.partial(jax.ShapeDtypeStruct, dtype=jnp.bfloat16)

    def ring(value, name, size, shift):
        return lax.ppermute(value, name, [(k, (k + shift) % size) for k in range(size)])

    saved = hidden_saved.reshape(length, full_units)
    packed = pack_rows(cotangent, weights, expert_ids, expert_counts, saved, n_island, n_dp)
    blocks, saved_own, firsts = packed[:pairs], packed[pairs], packed[pairs + 1 :]

    def over_z(value, k):
        perm = [(2 * z + c, 2 * target(z, k, pairs) + c) for z in range(pairs) for c in range(2)]
        return lax.ppermute(value, "expert", perm)

    groups, saved_all = [], [saved_own]
    for shift in range(1, n_dp):
        theirs = ring(firsts[shift - 1], "dp", n_dp, shift)
        saved_all.append(theirs)
        dealt = call(deal_body, [bf16((CAP, split))] * (pairs - 1), [theirs], "deal")
        groups += [over_z(dealt[k - 1], k) if k else theirs for k in order(pairs)]
    arrived = [over_z(blocks[k], k) if k else blocks[k] for k in order(pairs)]
    states = [in_hbm(value.reshape(units, width)) for value in (theta, first_moment, second_moment)]
    states = call(
        stage_body,
        [bf16((units, width))] * 3,
        states + [blocks[0]],
        "stage",
        [pltpu.SemaphoreType.DMA((3,))],
        in_specs=[HBM] * 3 + [VMEM],
    )
    swap = [(j, j ^ 1) for j in range(n_expert)]
    (two_mine,) = call(
        functools.partial(assemble_two_body, pairs),
        [bf16((pairs * CAP, width - split))],
        arrived,
        "assemble_two",
    )
    (one_mine,) = call(
        functools.partial(assemble_one_body, n_dp, pairs),
        [bf16((n_dp * pairs * CAP, split))],
        arrived + groups + list(states),
        "assemble_one",
    )
    one_quarters = [one_mine, lax.ppermute(one_mine, "expert", swap)]
    two_other = lax.ppermute(two_mine, "expert", swap)

    def spread(mine, other, after):
        quarters = [mine, other]
        for shift in range(1, n_dp):
            value = ring(mine, "dp", n_dp, shift)
            value, _ = lax.optimization_barrier((value, after))
            quarters += [value, lax.ppermute(value, "expert", swap)]
        return quarters

    *one, one_slots, left = call(
        functools.partial(one_body, n_dp, n_island, pairs),
        [bf16((units, first))] * (n_island - 1)
        + [bf16((n_dp * length, split)), bf16((units, n_dp * length))],
        one_quarters + saved_all + list(states),
        "far_one",
    )
    theirs = [ring(value, "island", n_island, shift + 1) for shift, value in enumerate(one)]
    two_quarters = spread(two_mine, two_other, left)
    *two, two_slots = call(
        functools.partial(two_body, n_dp, n_island, pairs),
        [bf16((units, part - first))] * (n_island - 1)
        + [bf16((n_dp * length, width - split))],
        two_quarters + [left, *states],
        "far_two",
    )
    theirs += [ring(value, "island", n_island, shift + 1) for shift, value in enumerate(two)]
    hidden = call(
        functools.partial(hidden_body, n_dp, n_island),
        [bf16((units, length))] * n_dp,
        [one_slots, two_slots, states[0]],
        "hidden_grad",
    )
    hidden = [hidden[0]] + [ring(hidden[s], "dp", n_dp, s) for s in range(1, n_dp)]
    (own,) = call(near_body, [bf16((units, part))], [two_slots, left, *states], "near_update")
    outer = [anchor.reshape(units, part), momentum.reshape(units, part), own]
    outer_type = jax.ShapeDtypeStruct((units, part), jnp.float32)
    begun = call(
        functools.partial(outer_one_body, n_island),
        [outer_type, outer_type],
        outer + theirs[: n_island - 1],
        "outer_one",
        [pltpu.VMEM((units, first), jnp.float32)] * 2 + [pltpu.SemaphoreType.DMA((2, 2))],
        out_specs=[HBM, HBM],
    )
    ins = [*begun, *outer, *theirs[n_island - 1 :], *hidden]
    anchor_new, momentum_new, d_hidden = call(
        functools.partial(outer_two_body, n_island, n_dp),
        [outer_type, outer_type, bf16((length, full_units))],
        ins,
        "outer_two",
        [pltpu.VMEM((units, part - first), jnp.float32)] * 2
        + [
            pltpu.VMEM((length, full_units), jnp.bfloat16),
            pltpu.VMEM((full_units, length), jnp.float32),
            pltpu.SemaphoreType.DMA((3, 2)),
        ],
        in_specs=[HBM, HBM] + [VMEM] * (len(ins) - 2),
        out_specs=[HBM, HBM, HBM],
        aliases={0: 0, 1: 1},
    )
    return (
        anchor_new.reshape(anchor.shape),
        momentum_new.reshape(momentum.shape),
        d_hidden.reshape(hidden_saved.shape),
    )


def solution(mesh):
    return jax.shard_map(
        per_device,
        mesh=mesh,
        in_specs=(
            P("island", "expert", "dp", None),
            P("island", "expert", "dp", None),
            P("island", "expert", "dp", None),
            P("expert", "dp", "island"),
            P("expert", "dp", "island"),
            P(("island", "dp", "expert"), None),
            P(("island", "dp", "expert"), None),
            P(("island", "dp", "expert"), None),
            P(("island", "dp", "expert"), None),
            P("island", "dp", "expert", None, None),
        ),
        out_specs=(
            P("expert", "dp", "island"),
            P("expert", "dp", "island"),
            P("island", "dp", "expert", None, None),
        ),
        check_vma=False,
    )
```

```python
import functools

import jax
import jax.numpy as jnp
from jax import lax
from jax.experimental import pallas as pl
from jax.experimental.pallas import tpu as pltpu
from jax.sharding import PartitionSpec as P

FF = 768
CAP = 16

beta_one = 0.9
beta_two = 0.95
adam_epsilon = 1e-08
inner_rate = 0.1
decay_rate = 0.1
outer_beta = 0.9
outer_rate = 0.7

VMEM = pl.BlockSpec(memory_space=pltpu.VMEM)
HBM = pl.BlockSpec(memory_space=pltpu.HBM)
PARAMS = pltpu.CompilerParams(vmem_limit_bytes=48 * 1024 * 1024)


def in_hbm(value):
    return pltpu.with_memory_space_constraint(value, pltpu.HBM)


def wrap(value, size):
    return lax.rem(value + size, size)


def target(place, step, size):
    return place ^ step if size & (size - 1) == 0 else (place + step) % size


def order(size):
    return sorted(range(size), key=lambda step: (step == 0, step != size // 2, -step))


def source(place, step, size):
    return place ^ step if size & (size - 1) == 0 else (place - step) % size


def cut(part):
    return part * 3 // 4 // 128 * 128


def pieces(n_island, width):
    part = width // n_island
    first = cut(part)
    island = lax.axis_index("island")
    order = [(shift, 0, first) for shift in range(1, n_island)]
    order += [(shift, first, part - first) for shift in range(1, n_island)]
    order += [(n_island, 0, part)]
    found, at = [], 0
    for shift, skip, size in order:
        column = lax.rem(island + shift, n_island) * part + skip
        found.append((slice(at, at + size), pl.ds(pl.multiple_of(column, 128), size)))
        at += size
    return found


def row_blocks(rows):
    size = rows // 4 if rows % 64 == 0 else rows
    return [pl.ds(first, size) for first in range(0, rows, size)]


def pack_body(experts, n_island, ids_hbm, weights_hbm, counts_hbm, cot_hbm, *refs):
    outs = refs[:experts]
    ids_ref, weights_ref, counts_ref, cot_ref, sems = refs[experts:]
    copies = [
        pltpu.make_async_copy(src, dst, sems.at[index])
        for index, (src, dst) in enumerate(
            [
                (ids_hbm, ids_ref),
                (weights_hbm, weights_ref),
                (counts_hbm, counts_ref),
            ]
            + [(cot_hbm.at[rows, :], cot_ref.at[rows, :]) for rows in row_blocks(cot_hbm.shape[0])]
        )
    ]
    for copy in copies:
        copy.start()
    width, tokens = ids_ref.shape
    rows = experts * CAP
    place = lax.div(lax.axis_index("expert"), 2)
    step = lax.broadcasted_iota(jnp.int32, (experts, CAP, tokens), 0).reshape(rows, tokens)
    expert = target(place, step, experts)
    rank = lax.broadcasted_iota(jnp.int32, (experts, CAP, tokens), 1).reshape(rows, tokens)
    earlier = (
        lax.broadcasted_iota(jnp.int32, (tokens, tokens), 0)
        < lax.broadcasted_iota(jnp.int32, (tokens, tokens), 1)
    )
    earlier = jnp.where(earlier, 1.0, 0.0).astype(jnp.bfloat16)
    for copy in copies[:3]:
        copy.wait()
    named = jnp.zeros((rows, tokens), jnp.float32)
    weight = jnp.zeros((rows, tokens), jnp.float32)
    for slot in range(width):
        hit = ids_ref[slot : slot + 1, :] == expert
        named = jnp.where(hit, 1.0, named)
        weight = jnp.where(hit, weights_ref[slot : slot + 1, :], weight)
    limit = jnp.zeros((rows, tokens), jnp.int32)
    for index in range(experts):
        limit = jnp.where(expert == index, counts_ref[:, index : index + 1], limit)
    found = jnp.dot(named.astype(jnp.bfloat16), earlier, preferred_element_type=jnp.float32)
    found = found.astype(jnp.int32)
    picked = (named > 0.0) & (found < limit) & (found == rank)
    pick = jnp.where(picked, 1.0, 0.0)
    scale = jnp.sum(pick * weight, axis=1, keepdims=True)
    pick = pick.astype(jnp.bfloat16)
    for copy in copies[3:]:
        copy.wait()
    for at, columns in pieces(n_island, cot_ref.shape[1]):
        gathered = jnp.dot(pick, cot_ref[:, columns], preferred_element_type=jnp.float32)
        packed = (gathered * scale).astype(jnp.bfloat16)
        for index, out in enumerate(outs):
            out[:, at] = packed[index * CAP : (index + 1) * CAP]


def pack_rows(cotangent, weights, expert_ids, counts, n_island):
    experts = counts.shape[1]
    ins = [expert_ids.T, weights.T, counts, cotangent]
    return pl.pallas_call(
        functools.partial(pack_body, experts, n_island),
        out_shape=[jax.ShapeDtypeStruct((CAP, cotangent.shape[1]), jnp.bfloat16)] * experts,
        in_specs=[HBM] * 4,
        out_specs=[VMEM] * experts,
        scratch_shapes=[
            pltpu.VMEM(expert_ids.shape[::-1], jnp.int32),
            pltpu.VMEM(weights.shape[::-1], jnp.float32),
            pltpu.VMEM(counts.shape, jnp.int32),
            pltpu.VMEM(cotangent.shape, jnp.bfloat16),
            pltpu.SemaphoreType.DMA((3 + len(row_blocks(cotangent.shape[0])),)),
        ],
        compiler_params=PARAMS,
        name="pack",
    )(*[in_hbm(value) for value in ins])


def adam(product, first, second, theta):
    scale = FF ** (-0.5)
    wide = theta.astype(jnp.float32)
    first_new = (inner_rate * beta_one) * first.astype(jnp.float32)
    first_new = first_new + (inner_rate * (1.0 - beta_one) * scale) * product
    second_new = beta_two * second.astype(jnp.float32)
    second_new = second_new + ((1.0 - beta_two) * scale * scale) * (product * product)
    step_size = first_new / (jnp.sqrt(second_new) + adam_epsilon)
    return ((1.0 - inner_rate * decay_rate) * wide - step_size).astype(jnp.bfloat16)


def assemble_body(pairs, *refs):
    blocks, (one_ref, two_ref) = refs[:pairs], refs[-2:]
    split = one_ref.shape[1]
    for index, block in enumerate(blocks):
        rows = slice(index * CAP, (index + 1) * CAP)
        one_ref[rows, :] = block[:, :split]
        two_ref[rows, :] = block[:, split:]


def rest_body(two_ref, *refs):
    refs[-1][...] = two_ref[...]


def stage_body(*refs):
    states, copied, sems = refs[:3], refs[4:7], refs[7]
    copies = [
        pltpu.make_async_copy(src, dst, sems.at[index])
        for index, (src, dst) in enumerate(zip(states, copied))
    ]
    for copy in copies:
        copy.start()
    for copy in copies:
        copy.wait()


def split_body(n_dp, saved_ref, _, *refs):
    *outs, scratch = refs
    units = outs[0].shape[0]
    scratch[...] = saved_ref[...].astype(jnp.float32).T
    for shift, out in enumerate(outs):
        row = pl.multiple_of(lax.rem(lax.axis_index("dp") + shift, n_dp) * units, 8)
        out[...] = scratch[pl.ds(row, units), :].astype(jnp.bfloat16)


def gather_slots(n_dp, pairs, quarters, slots_ref):
    data, position = lax.axis_index("dp"), lax.axis_index("expert")
    core = lax.rem(position, 2)
    place = lax.div(position, 2)
    length = 2 * pairs * CAP
    for shift in range(n_dp):
        group = wrap(data - shift, n_dp)
        for flip in range(2):
            side = core if flip == 0 else 1 - core
            block = quarters[2 * shift + flip]
            for k in range(pairs):
                at = order(pairs).index(k) * CAP
                row = group * length + (2 * source(place, k, pairs) + side) * CAP
                row = pl.multiple_of(row, CAP)
                slots_ref[pl.ds(row, CAP), :] = block[at : at + CAP, :]


def update(left, slots, state_refs, columns):
    product = jnp.dot(left, slots, preferred_element_type=jnp.float32)
    theta, first, second = (ref[:, columns] for ref in state_refs)
    return adam(product, first, second, theta)


def one_body(n_dp, n_island, pairs, *refs):
    quarters = refs[: 2 * n_dp]
    saved = refs[2 * n_dp : 3 * n_dp]
    state_refs = refs[3 * n_dp : 3 * n_dp + 3]
    *outs, slots_ref, left_ref = refs[3 * n_dp + 3 :]
    length = saved[0].shape[1]
    for shift, value in enumerate(saved):
        column = pl.multiple_of(wrap(lax.axis_index("dp") - shift, n_dp) * length, 128)
        left_ref[:, pl.ds(column, length)] = value[...]
    gather_slots(n_dp, pairs, quarters, slots_ref)
    places = pieces(n_island, state_refs[0].shape[1])
    for out, (at, columns) in zip(outs, places):
        out[...] = update(left_ref[...], slots_ref[:, at], state_refs, columns)


def two_body(n_dp, n_island, pairs, *refs):
    quarters = refs[: 2 * n_dp]
    left_ref, *state_refs = refs[2 * n_dp : 2 * n_dp + 4]
    *outs, slots_ref = refs[2 * n_dp + 4 :]
    width = state_refs[0].shape[1]
    first = width - slots_ref.shape[1]
    gather_slots(n_dp, pairs, quarters, slots_ref)
    places = pieces(n_island, width)[n_island - 1 :]
    for out, (at, columns) in zip(outs, places):
        slots = slots_ref[:, at.start - first : at.stop - first]
        out[...] = update(left_ref[...], slots, state_refs, columns)


def hidden_body(n_dp, n_island, one_ref, two_ref, theta_ref, *outs):
    data = lax.axis_index("dp")
    split = one_ref.shape[1]
    length = one_ref.shape[0] // n_dp
    total = None
    for at, columns in pieces(n_island, theta_ref.shape[1]):
        in_one = at.stop <= split
        slots = one_ref[:, at] if in_one else two_ref[:, at.start - split : at.stop - split]
        value = lax.dot_general(
            theta_ref[:, columns],
            slots,
            (((1,), (1,)), ((), ())),
            preferred_element_type=jnp.float32,
        )
        total = value if total is None else total + value
    hidden = (FF ** (-0.5) * total).astype(jnp.bfloat16)
    for shift, out in enumerate(outs):
        for group in range(n_dp):

            @pl.when(lax.rem(data + shift, n_dp) == group)
            def _():
                out[...] = hidden[:, group * length : (group + 1) * length]


def near_body(slots_ref, left_ref, *refs):
    *state_refs, own_ref = refs
    part = own_ref.shape[1]
    columns = pl.ds(pl.multiple_of(lax.axis_index("island") * part, 128), part)
    slots = slots_ref[:, slots_ref.shape[1] - part :]
    own_ref[...] = update(left_ref[...], slots, state_refs, columns)


def outer_step(columns, anchor_ref, momentum_ref, own_ref, theirs, results, outs, sems):
    n_island = len(theirs) + 1
    rows = anchor_ref.shape[0]
    steps = 2 if rows % 16 == 0 else 1
    copies = []
    for step in range(steps):
        at = slice(step * (rows // steps), (step + 1) * (rows // steps))
        total = own_ref[at, columns].astype(jnp.float32)
        for theta in theirs:
            total = total + theta[at, :].astype(jnp.float32)
        anchor = anchor_ref[at, columns]
        mean_delta = anchor - total * (1.0 / n_island)
        momentum_new = outer_beta * momentum_ref[at, columns] + mean_delta
        results[1][at, :] = momentum_new
        results[0][at, :] = anchor - outer_rate * (mean_delta + outer_beta * momentum_new)
        for index in range(2):
            copies.append(
                pltpu.make_async_copy(
                    results[index].at[at, :], outs[index].at[at, columns], sems.at[index, step]
                )
            )
            copies[-1].start()
    return copies


def outer_one_body(n_island, anchor_ref, momentum_ref, own_ref, *refs):
    theirs, outs = refs[: n_island - 1], refs[n_island - 1 : n_island + 1]
    *results, sems = refs[n_island + 1 :]
    columns = slice(0, results[0].shape[1])
    for copy in outer_step(columns, anchor_ref, momentum_ref, own_ref, theirs, results, outs, sems):
        copy.wait()


def outer_two_body(n_island, n_dp, _, __, anchor_ref, momentum_ref, own_ref, *refs):
    theirs, refs = refs[: n_island - 1], refs[n_island - 1 :]
    hidden, refs = refs[:n_dp], refs[n_dp:]
    *outs, hidden_out = refs[:3]
    *results, hidden_ref, scratch, sems = refs[3:]
    data = lax.axis_index("dp")
    units = hidden[0].shape[0]
    for shift, value in enumerate(hidden):
        row = pl.multiple_of(wrap(data - shift, n_dp) * units, 8)
        scratch[pl.ds(row, units), :] = value[...].astype(jnp.float32)
    part = anchor_ref.shape[1]
    columns = slice(part - results[0].shape[1], part)
    copies = outer_step(columns, anchor_ref, momentum_ref, own_ref, theirs, results, outs, sems)
    hidden_ref[...] = scratch[...].T.astype(jnp.bfloat16)
    copies.append(pltpu.make_async_copy(hidden_ref, hidden_out, sems.at[2, 0]))
    copies[-1].start()
    for copy in copies:
        copy.wait()


def call(body, out_shape, ins, name, scratch=(), in_specs=None, out_specs=None, aliases=None):
    return pl.pallas_call(
        body,
        out_shape=out_shape,
        in_specs=in_specs or [VMEM] * len(ins),
        out_specs=out_specs or [VMEM] * len(out_shape),
        scratch_shapes=list(scratch),
        input_output_aliases=aliases or {},
        compiler_params=PARAMS,
        name=name,
    )(*ins)


def per_device(
    theta,
    first_moment,
    second_moment,
    anchor,
    momentum,
    cotangent,
    weights,
    expert_ids,
    expert_counts,
    hidden_saved,
):
    n_island, n_dp, n_expert = (lax.axis_size(name) for name in ("island", "dp", "expert"))
    pairs = n_expert // 2
    units, width = theta.shape[2:]
    length, full_units = hidden_saved.shape[3:]
    part = width // n_island
    first = cut(part)
    split = (n_island - 1) * first
    bf16 = functools.partial(jax.ShapeDtypeStruct, dtype=jnp.bfloat16)

    def ring(value, name, size, shift):
        return lax.ppermute(value, name, [(k, (k + shift) % size) for k in range(size)])

    blocks = list(pack_rows(cotangent, weights, expert_ids, expert_counts, n_island))
    arrived = []
    for k in order(pairs)[:-1]:
        perm = [(2 * z + c, 2 * target(z, k, pairs) + c) for z in range(pairs) for c in range(2)]
        arrived.append(lax.ppermute(blocks[k], "expert", perm))
    saved = hidden_saved.reshape(length, full_units)
    saved_all = call(
        functools.partial(split_body, n_dp),
        [bf16((units, length))] * n_dp,
        [saved, blocks[0]],
        "split",
        [pltpu.VMEM((full_units, length), jnp.float32)],
    )
    saved_all = [ring(saved_all[s], "dp", n_dp, s) if s else saved_all[0] for s in range(n_dp)]
    arrived.append(blocks[0])
    one_mine, two_mine = call(
        functools.partial(assemble_body, pairs),
        [bf16((pairs * CAP, columns)) for columns in (split, width - split)],
        arrived + saved_all[1:],
        "assemble",
    )
    swap = [(j, j ^ 1) for j in range(n_expert)]

    def spread(mine, after=None):
        quarters = [mine, lax.ppermute(mine, "expert", swap)]
        for shift in range(1, n_dp):
            value = ring(mine, "dp", n_dp, shift)
            if after is not None:
                value, _ = lax.optimization_barrier((value, after))
            quarters += [value, lax.ppermute(value, "expert", swap)]
        return quarters

    one_quarters = spread(one_mine)
    states = [in_hbm(value.reshape(units, width)) for value in (theta, first_moment, second_moment)]
    states = call(
        stage_body,
        [bf16((units, width))] * 3,
        states + [one_mine],
        "stage",
        [pltpu.SemaphoreType.DMA((3,))],
        in_specs=[HBM] * 3 + [VMEM],
    )
    (two_mine,) = call(
        rest_body,
        [bf16((pairs * CAP, width - split))],
        [two_mine, one_quarters[1], *states],
        "rest",
    )
    *one, one_slots, left = call(
        functools.partial(one_body, n_dp, n_island, pairs),
        [bf16((units, first))] * (n_island - 1)
        + [bf16((n_dp * length, split)), bf16((units, n_dp * length))],
        one_quarters + saved_all + list(states),
        "far_one",
    )
    theirs = [ring(value, "island", n_island, shift + 1) for shift, value in enumerate(one)]
    two_quarters = spread(two_mine, left)
    *two, two_slots = call(
        functools.partial(two_body, n_dp, n_island, pairs),
        [bf16((units, part - first))] * (n_island - 1)
        + [bf16((n_dp * length, width - split))],
        two_quarters + [left, *states],
        "far_two",
    )
    theirs += [ring(value, "island", n_island, shift + 1) for shift, value in enumerate(two)]
    hidden = call(
        functools.partial(hidden_body, n_dp, n_island),
        [bf16((units, length))] * n_dp,
        [one_slots, two_slots, states[0]],
        "hidden_grad",
    )
    hidden = [hidden[0]] + [ring(hidden[s], "dp", n_dp, s) for s in range(1, n_dp)]
    (own,) = call(near_body, [bf16((units, part))], [two_slots, left, *states], "near_update")
    outer = [anchor.reshape(units, part), momentum.reshape(units, part), own]
    outer_type = jax.ShapeDtypeStruct((units, part), jnp.float32)
    begun = call(
        functools.partial(outer_one_body, n_island),
        [outer_type, outer_type],
        outer + theirs[: n_island - 1],
        "outer_one",
        [pltpu.VMEM((units, first), jnp.float32)] * 2 + [pltpu.SemaphoreType.DMA((2, 2))],
        out_specs=[HBM, HBM],
    )
    ins = [*begun, *outer, *theirs[n_island - 1 :], *hidden]
    anchor_new, momentum_new, d_hidden = call(
        functools.partial(outer_two_body, n_island, n_dp),
        [outer_type, outer_type, bf16((length, full_units))],
        ins,
        "outer_two",
        [pltpu.VMEM((units, part - first), jnp.float32)] * 2
        + [
            pltpu.VMEM((length, full_units), jnp.bfloat16),
            pltpu.VMEM((full_units, length), jnp.float32),
            pltpu.SemaphoreType.DMA((3, 2)),
        ],
        in_specs=[HBM, HBM] + [VMEM] * (len(ins) - 2),
        out_specs=[HBM, HBM, HBM],
        aliases={0: 0, 1: 1},
    )
    return (
        anchor_new.reshape(anchor.shape),
        momentum_new.reshape(momentum.shape),
        d_hidden.reshape(hidden_saved.shape),
    )


def solution(mesh):
    return jax.shard_map(
        per_device,
        mesh=mesh,
        in_specs=(
            P("island", "expert", "dp", None),
            P("island", "expert", "dp", None),
            P("island", "expert", "dp", None),
            P("expert", "dp", "island"),
            P("expert", "dp", "island"),
            P(("island", "dp", "expert"), None),
            P(("island", "dp", "expert"), None),
            P(("island", "dp", "expert"), None),
            P(("island", "dp", "expert"), None),
            P("island", "dp", "expert", None, None),
        ),
        out_specs=(
            P("expert", "dp", "island"),
            P("expert", "dp", "island"),
            P("island", "dp", "expert", None, None),
        ),
        check_vma=False,
    )
```

```python
import functools

import jax
import jax.numpy as jnp
from jax import lax
from jax.experimental import pallas as pl
from jax.experimental.pallas import tpu as pltpu
from jax.sharding import PartitionSpec as P

FF = 768
CAP = 16

beta_one = 0.9
beta_two = 0.95
adam_epsilon = 1e-08
inner_rate = 0.1
decay_rate = 0.1
outer_beta = 0.9
outer_rate = 0.7

VMEM = pl.BlockSpec(memory_space=pltpu.VMEM)
HBM = pl.BlockSpec(memory_space=pltpu.HBM)
PARAMS = pltpu.CompilerParams(vmem_limit_bytes=48 * 1024 * 1024)


PEAK = 1.15e15
MICROSECONDS = {
    "stage": 1.6,
    "split": 0.1,
    "assemble": 0.05,
    "rest": 0.05,
    "far_one": 0.3,
    "far_two": 0.01,
    "hidden_grad": 0.01,
    "near_update": 0.01,
    "outer_one": 1.7,
    "outer_two": 0.9,
}


def in_hbm(value):
    return pltpu.with_memory_space_constraint(value, pltpu.HBM)


def wrap(value, size):
    return lax.rem(value + size, size)


def target(place, step, size):
    return place ^ step if size & (size - 1) == 0 else (place + step) % size


def order(size):
    return sorted(range(size), key=lambda step: (step == 0, step != size // 2, -step))


def source(place, step, size):
    return place ^ step if size & (size - 1) == 0 else (place - step) % size


def cut(part):
    return part * 5 // 8 // 128 * 128


def pieces(n_island, width):
    part = width // n_island
    first = cut(part)
    island = lax.axis_index("island")
    order = [(shift, 0, first) for shift in range(1, n_island)]
    order += [(shift, first, part - first) for shift in range(1, n_island)]
    order += [(n_island, 0, part)]
    found, at = [], 0
    for shift, skip, size in order:
        column = lax.rem(island + shift, n_island) * part + skip
        found.append((slice(at, at + size), pl.ds(pl.multiple_of(column, 128), size)))
        at += size
    return found


def pack_body(experts, n_island, ids_hbm, weights_hbm, counts_hbm, cot_hbm, *refs):
    outs = refs[:experts]
    ids_ref, weights_ref, counts_ref, cot_ref, sems = refs[experts:]
    copies = [
        pltpu.make_async_copy(src, dst, sems.at[index])
        for index, (src, dst) in enumerate(
            [
                (ids_hbm, ids_ref),
                (weights_hbm, weights_ref),
                (counts_hbm, counts_ref),
                (cot_hbm, cot_ref),
            ]
        )
    ]
    for copy in copies:
        copy.start()
    width, tokens = ids_ref.shape
    rows = experts * CAP
    place = lax.div(lax.axis_index("expert"), 2)
    step = lax.broadcasted_iota(jnp.int32, (experts, CAP, tokens), 0).reshape(rows, tokens)
    expert = target(place, step, experts)
    rank = lax.broadcasted_iota(jnp.int32, (experts, CAP, tokens), 1).reshape(rows, tokens)
    earlier = (
        lax.broadcasted_iota(jnp.int32, (tokens, tokens), 0)
        < lax.broadcasted_iota(jnp.int32, (tokens, tokens), 1)
    )
    earlier = jnp.where(earlier, 1.0, 0.0).astype(jnp.bfloat16)
    for copy in copies[:3]:
        copy.wait()
    named = jnp.zeros((rows, tokens), jnp.float32)
    weight = jnp.zeros((rows, tokens), jnp.float32)
    for slot in range(width):
        hit = ids_ref[slot : slot + 1, :] == expert
        named = jnp.where(hit, 1.0, named)
        weight = jnp.where(hit, weights_ref[slot : slot + 1, :], weight)
    limit = jnp.zeros((rows, tokens), jnp.int32)
    for index in range(experts):
        limit = jnp.where(expert == index, counts_ref[:, index : index + 1], limit)
    found = jnp.dot(named.astype(jnp.bfloat16), earlier, preferred_element_type=jnp.float32)
    found = found.astype(jnp.int32)
    picked = (named > 0.0) & (found < limit) & (found == rank)
    pick = jnp.where(picked, 1.0, 0.0)
    scale = jnp.sum(pick * weight, axis=1, keepdims=True)
    pick = pick.astype(jnp.bfloat16)
    copies[3].wait()
    for at, columns in pieces(n_island, cot_ref.shape[1]):
        gathered = jnp.dot(pick, cot_ref[:, columns], preferred_element_type=jnp.float32)
        packed = (gathered * scale).astype(jnp.bfloat16)
        for index, out in enumerate(outs):
            out[:, at] = packed[index * CAP : (index + 1) * CAP]


def pack_rows(cotangent, weights, expert_ids, counts, n_island):
    experts = counts.shape[1]
    ins = [expert_ids.T, weights.T, counts, cotangent]
    return pl.pallas_call(
        functools.partial(pack_body, experts, n_island),
        out_shape=[jax.ShapeDtypeStruct((CAP, cotangent.shape[1]), jnp.bfloat16)] * experts,
        in_specs=[HBM] * 4,
        out_specs=[VMEM] * experts,
        scratch_shapes=[
            pltpu.VMEM(expert_ids.shape[::-1], jnp.int32),
            pltpu.VMEM(weights.shape[::-1], jnp.float32),
            pltpu.VMEM(counts.shape, jnp.int32),
            pltpu.VMEM(cotangent.shape, jnp.bfloat16),
            pltpu.SemaphoreType.DMA((4,)),
        ],
        compiler_params=PARAMS,
        name="pack",
    )(*[in_hbm(value) for value in ins])


def adam(product, first, second, theta):
    scale = FF ** (-0.5)
    wide = theta.astype(jnp.float32)
    first_new = (inner_rate * beta_one) * first.astype(jnp.float32)
    first_new = first_new + (inner_rate * (1.0 - beta_one) * scale) * product
    second_new = beta_two * second.astype(jnp.float32)
    second_new = second_new + ((1.0 - beta_two) * scale * scale) * (product * product)
    step_size = first_new / (jnp.sqrt(second_new) + adam_epsilon)
    return ((1.0 - inner_rate * decay_rate) * wide - step_size).astype(jnp.bfloat16)


def assemble_body(pairs, *refs):
    blocks, (one_ref, two_ref) = refs[:pairs], refs[-2:]
    split = one_ref.shape[1]
    for index, block in enumerate(blocks):
        rows = slice(index * CAP, (index + 1) * CAP)
        one_ref[rows, :] = block[:, :split]
        two_ref[rows, :] = block[:, split:]


def rest_body(two_ref, *refs):
    refs[-1][...] = two_ref[...]


def stage_body(*refs):
    states, copied, sems = refs[:3], refs[4:7], refs[7]
    copies = [
        pltpu.make_async_copy(src, dst, sems.at[index])
        for index, (src, dst) in enumerate(zip(states, copied))
    ]
    for copy in copies:
        copy.start()
    for copy in copies:
        copy.wait()


def split_body(n_dp, saved_ref, _, *refs):
    *outs, scratch = refs
    units = outs[0].shape[0]
    scratch[...] = saved_ref[...].astype(jnp.float32).T
    for shift, out in enumerate(outs):
        row = pl.multiple_of(lax.rem(lax.axis_index("dp") + shift, n_dp) * units, 8)
        out[...] = scratch[pl.ds(row, units), :].astype(jnp.bfloat16)


def gather_slots(n_dp, pairs, quarters, slots_ref):
    data, position = lax.axis_index("dp"), lax.axis_index("expert")
    core = lax.rem(position, 2)
    place = lax.div(position, 2)
    length = 2 * pairs * CAP
    for shift in range(n_dp):
        group = wrap(data - shift, n_dp)
        for flip in range(2):
            side = core if flip == 0 else 1 - core
            block = quarters[2 * shift + flip]
            for k in range(pairs):
                at = order(pairs).index(k) * CAP
                row = group * length + (2 * source(place, k, pairs) + side) * CAP
                row = pl.multiple_of(row, CAP)
                slots_ref[pl.ds(row, CAP), :] = block[at : at + CAP, :]


def update(left, slots, state_refs, columns):
    product = jnp.dot(left, slots, preferred_element_type=jnp.float32)
    theta, first, second = (ref[:, columns] for ref in state_refs)
    return adam(product, first, second, theta)


def one_body(n_dp, n_island, pairs, *refs):
    quarters = refs[: 2 * n_dp]
    saved = refs[2 * n_dp : 3 * n_dp]
    state_refs = refs[3 * n_dp : 3 * n_dp + 3]
    *outs, slots_ref, left_ref = refs[3 * n_dp + 3 :]
    length = saved[0].shape[1]
    for shift, value in enumerate(saved):
        column = pl.multiple_of(wrap(lax.axis_index("dp") - shift, n_dp) * length, 128)
        left_ref[:, pl.ds(column, length)] = value[...]
    gather_slots(n_dp, pairs, quarters, slots_ref)
    places = pieces(n_island, state_refs[0].shape[1])
    for out, (at, columns) in zip(outs, places):
        out[...] = update(left_ref[...], slots_ref[:, at], state_refs, columns)


def two_body(n_dp, n_island, pairs, *refs):
    quarters = refs[: 2 * n_dp]
    left_ref, *state_refs = refs[2 * n_dp : 2 * n_dp + 4]
    *outs, slots_ref = refs[2 * n_dp + 4 :]
    width = state_refs[0].shape[1]
    first = width - slots_ref.shape[1]
    gather_slots(n_dp, pairs, quarters, slots_ref)
    places = pieces(n_island, width)[n_island - 1 :]
    for out, (at, columns) in zip(outs, places):
        slots = slots_ref[:, at.start - first : at.stop - first]
        out[...] = update(left_ref[...], slots, state_refs, columns)


def hidden_body(n_dp, n_island, one_ref, two_ref, theta_ref, *outs):
    data = lax.axis_index("dp")
    split = one_ref.shape[1]
    length = one_ref.shape[0] // n_dp
    total = None
    for at, columns in pieces(n_island, theta_ref.shape[1]):
        in_one = at.stop <= split
        slots = one_ref[:, at] if in_one else two_ref[:, at.start - split : at.stop - split]
        value = lax.dot_general(
            theta_ref[:, columns],
            slots,
            (((1,), (1,)), ((), ())),
            preferred_element_type=jnp.float32,
        )
        total = value if total is None else total + value
    hidden = (FF ** (-0.5) * total).astype(jnp.bfloat16)
    for shift, out in enumerate(outs):
        for group in range(n_dp):

            @pl.when(lax.rem(data + shift, n_dp) == group)
            def _():
                out[...] = hidden[:, group * length : (group + 1) * length]


def near_body(slots_ref, left_ref, *refs):
    *state_refs, own_ref = refs
    part = own_ref.shape[1]
    columns = pl.ds(pl.multiple_of(lax.axis_index("island") * part, 128), part)
    slots = slots_ref[:, slots_ref.shape[1] - part :]
    own_ref[...] = update(left_ref[...], slots, state_refs, columns)


def outer_step(columns, anchor_ref, momentum_ref, own_ref, theirs, results, outs, sems):
    n_island = len(theirs) + 1
    rows = anchor_ref.shape[0]
    steps = 2 if rows % 16 == 0 else 1
    copies = []
    for step in range(steps):
        at = slice(step * (rows // steps), (step + 1) * (rows // steps))
        total = own_ref[at, columns].astype(jnp.float32)
        for theta in theirs:
            total = total + theta[at, :].astype(jnp.float32)
        anchor = anchor_ref[at, columns]
        mean_delta = anchor - total * (1.0 / n_island)
        momentum_new = outer_beta * momentum_ref[at, columns] + mean_delta
        results[1][at, :] = momentum_new
        results[0][at, :] = anchor - outer_rate * (mean_delta + outer_beta * momentum_new)
        for index in range(2):
            copies.append(
                pltpu.make_async_copy(
                    results[index].at[at, :], outs[index].at[at, columns], sems.at[index, step]
                )
            )
            copies[-1].start()
    return copies


def outer_one_body(n_island, anchor_ref, momentum_ref, own_ref, *refs):
    theirs, outs = refs[: n_island - 1], refs[n_island - 1 : n_island + 1]
    *results, sems = refs[n_island + 1 :]
    columns = slice(0, results[0].shape[1])
    for copy in outer_step(columns, anchor_ref, momentum_ref, own_ref, theirs, results, outs, sems):
        copy.wait()


def outer_two_body(n_island, n_dp, _, __, anchor_ref, momentum_ref, own_ref, *refs):
    theirs, refs = refs[: n_island - 1], refs[n_island - 1 :]
    hidden, refs = refs[:n_dp], refs[n_dp:]
    *outs, hidden_out = refs[:3]
    *results, hidden_ref, scratch, sems = refs[3:]
    data = lax.axis_index("dp")
    units = hidden[0].shape[0]
    for shift, value in enumerate(hidden):
        row = pl.multiple_of(wrap(data - shift, n_dp) * units, 8)
        scratch[pl.ds(row, units), :] = value[...].astype(jnp.float32)
    part = anchor_ref.shape[1]
    columns = slice(part - results[0].shape[1], part)
    copies = outer_step(columns, anchor_ref, momentum_ref, own_ref, theirs, results, outs, sems)
    hidden_ref[...] = scratch[...].T.astype(jnp.bfloat16)
    copies.append(pltpu.make_async_copy(hidden_ref, hidden_out, sems.at[2, 0]))
    copies[-1].start()
    for copy in copies:
        copy.wait()


def call(body, out_shape, ins, name, scratch=(), in_specs=None, out_specs=None, aliases=None):
    cost = int(MICROSECONDS[name] * PEAK / 1e6)
    return pl.pallas_call(
        body,
        out_shape=out_shape,
        in_specs=in_specs or [VMEM] * len(ins),
        out_specs=out_specs or [VMEM] * len(out_shape),
        scratch_shapes=list(scratch),
        input_output_aliases=aliases or {},
        cost_estimate=pl.CostEstimate(flops=cost, transcendentals=0, bytes_accessed=0),
        compiler_params=PARAMS,
        name=name,
    )(*ins)


def per_device(
    theta,
    first_moment,
    second_moment,
    anchor,
    momentum,
    cotangent,
    weights,
    expert_ids,
    expert_counts,
    hidden_saved,
):
    n_island, n_dp, n_expert = (lax.axis_size(name) for name in ("island", "dp", "expert"))
    pairs = n_expert // 2
    units, width = theta.shape[2:]
    length, full_units = hidden_saved.shape[3:]
    part = width // n_island
    first = cut(part)
    split = (n_island - 1) * first
    bf16 = functools.partial(jax.ShapeDtypeStruct, dtype=jnp.bfloat16)

    def ring(value, name, size, shift):
        return lax.ppermute(value, name, [(k, (k + shift) % size) for k in range(size)])

    blocks = list(pack_rows(cotangent, weights, expert_ids, expert_counts, n_island))
    arrived = []
    for k in order(pairs)[:-1]:
        perm = [(2 * z + c, 2 * target(z, k, pairs) + c) for z in range(pairs) for c in range(2)]
        arrived.append(lax.ppermute(blocks[k], "expert", perm))
    saved = hidden_saved.reshape(length, full_units)
    saved_all = call(
        functools.partial(split_body, n_dp),
        [bf16((units, length))] * n_dp,
        [saved, blocks[0]],
        "split",
        [pltpu.VMEM((full_units, length), jnp.float32)],
    )
    saved_all = [ring(saved_all[s], "dp", n_dp, s) if s else saved_all[0] for s in range(n_dp)]
    arrived.append(blocks[0])
    one_mine, two_mine = call(
        functools.partial(assemble_body, pairs),
        [bf16((pairs * CAP, columns)) for columns in (split, width - split)],
        arrived + saved_all[1:],
        "assemble",
    )
    swap = [(j, j ^ 1) for j in range(n_expert)]

    def spread(mine, other, after=None):
        quarters = [mine, other]
        for shift in range(1, n_dp):
            value = ring(mine, "dp", n_dp, shift)
            if after is not None:
                value, _ = lax.optimization_barrier((value, after))
            quarters += [value, lax.ppermute(value, "expert", swap)]
        return quarters

    one_other = lax.ppermute(one_mine, "expert", swap)
    one_quarters = spread(one_mine, one_other)
    two_other = lax.ppermute(two_mine, "expert", swap)
    states = [in_hbm(value.reshape(units, width)) for value in (theta, first_moment, second_moment)]
    states = call(
        stage_body,
        [bf16((units, width))] * 3,
        states + [one_mine],
        "stage",
        [pltpu.SemaphoreType.DMA((3,))],
        in_specs=[HBM] * 3 + [VMEM],
    )
    (two_mine,) = call(
        rest_body,
        [bf16((pairs * CAP, width - split))],
        [two_mine, two_other, one_other, *states],
        "rest",
    )
    *one, one_slots, left = call(
        functools.partial(one_body, n_dp, n_island, pairs),
        [bf16((units, first))] * (n_island - 1)
        + [bf16((n_dp * length, split)), bf16((units, n_dp * length))],
        one_quarters + saved_all + list(states),
        "far_one",
    )
    theirs = [ring(value, "island", n_island, shift + 1) for shift, value in enumerate(one)]
    two_quarters = spread(two_mine, two_other, left)
    *two, two_slots = call(
        functools.partial(two_body, n_dp, n_island, pairs),
        [bf16((units, part - first))] * (n_island - 1)
        + [bf16((n_dp * length, width - split))],
        two_quarters + [left, *states],
        "far_two",
    )
    theirs += [ring(value, "island", n_island, shift + 1) for shift, value in enumerate(two)]
    hidden = call(
        functools.partial(hidden_body, n_dp, n_island),
        [bf16((units, length))] * n_dp,
        [one_slots, two_slots, states[0]],
        "hidden_grad",
    )
    hidden = [hidden[0]] + [ring(hidden[s], "dp", n_dp, s) for s in range(1, n_dp)]
    (own,) = call(near_body, [bf16((units, part))], [two_slots, left, *states], "near_update")
    outer = [anchor.reshape(units, part), momentum.reshape(units, part), own]
    outer_type = jax.ShapeDtypeStruct((units, part), jnp.float32)
    begun = call(
        functools.partial(outer_one_body, n_island),
        [outer_type, outer_type],
        outer + theirs[: n_island - 1],
        "outer_one",
        [pltpu.VMEM((units, first), jnp.float32)] * 2 + [pltpu.SemaphoreType.DMA((2, 2))],
        out_specs=[HBM, HBM],
    )
    ins = [*begun, *outer, *theirs[n_island - 1 :], *hidden]
    anchor_new, momentum_new, d_hidden = call(
        functools.partial(outer_two_body, n_island, n_dp),
        [outer_type, outer_type, bf16((length, full_units))],
        ins,
        "outer_two",
        [pltpu.VMEM((units, part - first), jnp.float32)] * 2
        + [
            pltpu.VMEM((length, full_units), jnp.bfloat16),
            pltpu.VMEM((full_units, length), jnp.float32),
            pltpu.SemaphoreType.DMA((3, 2)),
        ],
        in_specs=[HBM, HBM] + [VMEM] * (len(ins) - 2),
        out_specs=[HBM, HBM, HBM],
        aliases={0: 0, 1: 1},
    )
    return (
        anchor_new.reshape(anchor.shape),
        momentum_new.reshape(momentum.shape),
        d_hidden.reshape(hidden_saved.shape),
    )


def solution(mesh):
    return jax.shard_map(
        per_device,
        mesh=mesh,
        in_specs=(
            P("island", "expert", "dp", None),
            P("island", "expert", "dp", None),
            P("island", "expert", "dp", None),
            P("expert", "dp", "island"),
            P("expert", "dp", "island"),
            P(("island", "dp", "expert"), None),
            P(("island", "dp", "expert"), None),
            P(("island", "dp", "expert"), None),
            P(("island", "dp", "expert"), None),
            P("island", "dp", "expert", None, None),
        ),
        out_specs=(
            P("expert", "dp", "island"),
            P("expert", "dp", "island"),
            P("island", "dp", "expert", None, None),
        ),
        check_vma=False,
    )
```

```python
import functools

import jax
import jax.numpy as jnp
from jax import lax
from jax.experimental import pallas as pl
from jax.experimental.pallas import tpu as pltpu
from jax.sharding import PartitionSpec as P

FF = 768
CAP = 16

beta_one = 0.9
beta_two = 0.95
adam_epsilon = 1e-08
inner_rate = 0.1
decay_rate = 0.1
outer_beta = 0.9
outer_rate = 0.7

VMEM = pl.BlockSpec(memory_space=pltpu.VMEM)
HBM = pl.BlockSpec(memory_space=pltpu.HBM)
PARAMS = pltpu.CompilerParams(vmem_limit_bytes=48 * 1024 * 1024)


PEAK = 1.15e15
MICROSECONDS = {
    "stage": 1.6,
    "split": 0.1,
    "assemble": 0.05,
    "rest": 0.05,
    "far_one": 0.1,
    "far_two": 0.3,
    "hidden_grad": 0.3,
    "near_update": 0.3,
    "outer_one": 1.1,
    "outer_two": 0.9,
}


def in_hbm(value):
    return pltpu.with_memory_space_constraint(value, pltpu.HBM)


def wrap(value, size):
    return lax.rem(value + size, size)


def target(place, step, size):
    return place ^ step if size & (size - 1) == 0 else (place + step) % size


def order(size):
    return sorted(range(size), key=lambda step: (step == 0, step != size // 2, -step))


def source(place, step, size):
    return place ^ step if size & (size - 1) == 0 else (place - step) % size


def cut(part):
    return part * 3 // 4 // 128 * 128


def pieces(n_island, width):
    part = width // n_island
    first = cut(part)
    island = lax.axis_index("island")
    order = [(shift, 0, first) for shift in range(1, n_island)]
    order += [(shift, first, part - first) for shift in range(1, n_island)]
    order += [(n_island, 0, part)]
    found, at = [], 0
    for shift, skip, size in order:
        column = lax.rem(island + shift, n_island) * part + skip
        found.append((slice(at, at + size), pl.ds(pl.multiple_of(column, 128), size)))
        at += size
    return found


def pack_body(experts, n_island, ids_hbm, weights_hbm, counts_hbm, cot_hbm, *refs):
    outs = refs[:experts]
    ids_ref, weights_ref, counts_ref, cot_ref, sems = refs[experts:]
    copies = [
        pltpu.make_async_copy(src, dst, sems.at[index])
        for index, (src, dst) in enumerate(
            [
                (ids_hbm, ids_ref),
                (weights_hbm, weights_ref),
                (counts_hbm, counts_ref),
                (cot_hbm, cot_ref),
            ]
        )
    ]
    for copy in copies:
        copy.start()
    width, tokens = ids_ref.shape
    rows = experts * CAP
    place = lax.div(lax.axis_index("expert"), 2)
    step = lax.broadcasted_iota(jnp.int32, (experts, CAP, tokens), 0).reshape(rows, tokens)
    expert = target(place, step, experts)
    rank = lax.broadcasted_iota(jnp.int32, (experts, CAP, tokens), 1).reshape(rows, tokens)
    earlier = (
        lax.broadcasted_iota(jnp.int32, (tokens, tokens), 0)
        < lax.broadcasted_iota(jnp.int32, (tokens, tokens), 1)
    )
    earlier = jnp.where(earlier, 1.0, 0.0).astype(jnp.bfloat16)
    for copy in copies[:3]:
        copy.wait()
    named = jnp.zeros((rows, tokens), jnp.float32)
    weight = jnp.zeros((rows, tokens), jnp.float32)
    for slot in range(width):
        hit = ids_ref[slot : slot + 1, :] == expert
        named = jnp.where(hit, 1.0, named)
        weight = jnp.where(hit, weights_ref[slot : slot + 1, :], weight)
    limit = jnp.zeros((rows, tokens), jnp.int32)
    for index in range(experts):
        limit = jnp.where(expert == index, counts_ref[:, index : index + 1], limit)
    found = jnp.dot(named.astype(jnp.bfloat16), earlier, preferred_element_type=jnp.float32)
    found = found.astype(jnp.int32)
    picked = (named > 0.0) & (found < limit) & (found == rank)
    pick = jnp.where(picked, 1.0, 0.0)
    scale = jnp.sum(pick * weight, axis=1, keepdims=True)
    pick = pick.astype(jnp.bfloat16)
    copies[3].wait()
    for at, columns in pieces(n_island, cot_ref.shape[1]):
        gathered = jnp.dot(pick, cot_ref[:, columns], preferred_element_type=jnp.float32)
        packed = (gathered * scale).astype(jnp.bfloat16)
        for index, out in enumerate(outs):
            out[:, at] = packed[index * CAP : (index + 1) * CAP]


def pack_rows(cotangent, weights, expert_ids, counts, n_island):
    experts = counts.shape[1]
    ins = [expert_ids.T, weights.T, counts, cotangent]
    return pl.pallas_call(
        functools.partial(pack_body, experts, n_island),
        out_shape=[jax.ShapeDtypeStruct((CAP, cotangent.shape[1]), jnp.bfloat16)] * experts,
        in_specs=[HBM] * 4,
        out_specs=[VMEM] * experts,
        scratch_shapes=[
            pltpu.VMEM(expert_ids.shape[::-1], jnp.int32),
            pltpu.VMEM(weights.shape[::-1], jnp.float32),
            pltpu.VMEM(counts.shape, jnp.int32),
            pltpu.VMEM(cotangent.shape, jnp.bfloat16),
            pltpu.SemaphoreType.DMA((4,)),
        ],
        compiler_params=PARAMS,
        name="pack",
    )(*[in_hbm(value) for value in ins])


def adam(product, first, second, theta):
    scale = FF ** (-0.5)
    wide = theta.astype(jnp.float32)
    first_new = (inner_rate * beta_one) * first.astype(jnp.float32)
    first_new = first_new + (inner_rate * (1.0 - beta_one) * scale) * product
    second_new = beta_two * second.astype(jnp.float32)
    second_new = second_new + ((1.0 - beta_two) * scale * scale) * (product * product)
    step_size = first_new / (jnp.sqrt(second_new) + adam_epsilon)
    return ((1.0 - inner_rate * decay_rate) * wide - step_size).astype(jnp.bfloat16)


def assemble_body(pairs, *refs):
    blocks, (one_ref, two_ref) = refs[:pairs], refs[-2:]
    split = one_ref.shape[1]
    for index, block in enumerate(blocks):
        rows = slice(index * CAP, (index + 1) * CAP)
        one_ref[rows, :] = block[:, :split]
        two_ref[rows, :] = block[:, split:]


def rest_body(two_ref, *refs):
    refs[-1][...] = two_ref[...]


def stage_body(*refs):
    states, copied, sems = refs[:3], refs[4:7], refs[7]
    copies = [
        pltpu.make_async_copy(src, dst, sems.at[index])
        for index, (src, dst) in enumerate(zip(states, copied))
    ]
    for copy in copies:
        copy.start()
    for copy in copies:
        copy.wait()


def split_body(n_dp, saved_ref, _, *refs):
    *outs, scratch = refs
    units = outs[0].shape[0]
    scratch[...] = saved_ref[...].astype(jnp.float32).T
    for shift, out in enumerate(outs):
        row = pl.multiple_of(lax.rem(lax.axis_index("dp") + shift, n_dp) * units, 8)
        out[...] = scratch[pl.ds(row, units), :].astype(jnp.bfloat16)


def gather_slots(n_dp, pairs, quarters, slots_ref):
    data, position = lax.axis_index("dp"), lax.axis_index("expert")
    core = lax.rem(position, 2)
    place = lax.div(position, 2)
    length = 2 * pairs * CAP
    for shift in range(n_dp):
        group = wrap(data - shift, n_dp)
        for flip in range(2):
            side = core if flip == 0 else 1 - core
            block = quarters[2 * shift + flip]
            for k in range(pairs):
                at = order(pairs).index(k) * CAP
                row = group * length + (2 * source(place, k, pairs) + side) * CAP
                row = pl.multiple_of(row, CAP)
                slots_ref[pl.ds(row, CAP), :] = block[at : at + CAP, :]


def update(left, slots, state_refs, columns):
    product = jnp.dot(left, slots, preferred_element_type=jnp.float32)
    theta, first, second = (ref[:, columns] for ref in state_refs)
    return adam(product, first, second, theta)


def one_body(n_dp, n_island, pairs, *refs):
    quarters = refs[: 2 * n_dp]
    saved = refs[2 * n_dp : 3 * n_dp]
    state_refs = refs[3 * n_dp : 3 * n_dp + 3]
    *outs, slots_ref, left_ref = refs[3 * n_dp + 3 :]
    length = saved[0].shape[1]
    for shift, value in enumerate(saved):
        column = pl.multiple_of(wrap(lax.axis_index("dp") - shift, n_dp) * length, 128)
        left_ref[:, pl.ds(column, length)] = value[...]
    gather_slots(n_dp, pairs, quarters, slots_ref)
    places = pieces(n_island, state_refs[0].shape[1])
    for out, (at, columns) in zip(outs, places):
        out[...] = update(left_ref[...], slots_ref[:, at], state_refs, columns)


def two_body(n_dp, n_island, pairs, *refs):
    quarters = refs[: 2 * n_dp]
    left_ref, *state_refs = refs[2 * n_dp : 2 * n_dp + 4]
    *outs, slots_ref = refs[2 * n_dp + 4 :]
    width = state_refs[0].shape[1]
    first = width - slots_ref.shape[1]
    gather_slots(n_dp, pairs, quarters, slots_ref)
    places = pieces(n_island, width)[n_island - 1 :]
    for out, (at, columns) in zip(outs, places):
        slots = slots_ref[:, at.start - first : at.stop - first]
        out[...] = update(left_ref[...], slots, state_refs, columns)


def hidden_body(n_dp, n_island, one_ref, two_ref, theta_ref, *outs):
    data = lax.axis_index("dp")
    split = one_ref.shape[1]
    length = one_ref.shape[0] // n_dp
    total = None
    for at, columns in pieces(n_island, theta_ref.shape[1]):
        in_one = at.stop <= split
        slots = one_ref[:, at] if in_one else two_ref[:, at.start - split : at.stop - split]
        value = lax.dot_general(
            theta_ref[:, columns],
            slots,
            (((1,), (1,)), ((), ())),
            preferred_element_type=jnp.float32,
        )
        total = value if total is None else total + value
    hidden = (FF ** (-0.5) * total).astype(jnp.bfloat16)
    for shift, out in enumerate(outs):
        for group in range(n_dp):

            @pl.when(lax.rem(data + shift, n_dp) == group)
            def _():
                out[...] = hidden[:, group * length : (group + 1) * length]


def near_body(slots_ref, left_ref, *refs):
    *state_refs, own_ref = refs
    part = own_ref.shape[1]
    columns = pl.ds(pl.multiple_of(lax.axis_index("island") * part, 128), part)
    slots = slots_ref[:, slots_ref.shape[1] - part :]
    own_ref[...] = update(left_ref[...], slots, state_refs, columns)


def outer_step(columns, anchor_ref, momentum_ref, own_ref, theirs, results, outs, sems):
    n_island = len(theirs) + 1
    rows = anchor_ref.shape[0]
    steps = 2 if rows % 16 == 0 else 1
    copies = []
    for step in range(steps):
        at = slice(step * (rows // steps), (step + 1) * (rows // steps))
        total = own_ref[at, columns].astype(jnp.float32)
        for theta in theirs:
            total = total + theta[at, :].astype(jnp.float32)
        anchor = anchor_ref[at, columns]
        mean_delta = anchor - total * (1.0 / n_island)
        momentum_new = outer_beta * momentum_ref[at, columns] + mean_delta
        results[1][at, :] = momentum_new
        results[0][at, :] = anchor - outer_rate * (mean_delta + outer_beta * momentum_new)
        for index in range(2):
            copies.append(
                pltpu.make_async_copy(
                    results[index].at[at, :], outs[index].at[at, columns], sems.at[index, step]
                )
            )
            copies[-1].start()
    return copies


def outer_one_body(n_island, n_dp, anchor_ref, momentum_ref, own_ref, *refs):
    theirs, refs = refs[: n_island - 1], refs[n_island - 1 :]
    hidden, refs = refs[:n_dp], refs[n_dp:]
    *outs, hidden_out = refs[:3]
    *results, hidden_ref, scratch, sems = refs[3:]
    data = lax.axis_index("dp")
    units = hidden[0].shape[0]
    for shift, value in enumerate(hidden):
        row = pl.multiple_of(wrap(data - shift, n_dp) * units, 8)
        scratch[pl.ds(row, units), :] = value[...].astype(jnp.float32)
    columns = slice(0, results[0].shape[1])
    copies = outer_step(columns, anchor_ref, momentum_ref, own_ref, theirs, results, outs, sems)
    hidden_ref[...] = scratch[...].T.astype(jnp.bfloat16)
    copies.append(pltpu.make_async_copy(hidden_ref, hidden_out, sems.at[2, 0]))
    copies[-1].start()
    for copy in copies:
        copy.wait()


def outer_two_body(n_island, _, __, anchor_ref, momentum_ref, own_ref, *refs):
    theirs, outs = refs[: n_island - 1], refs[n_island - 1 : n_island + 1]
    *results, sems = refs[n_island + 1 :]
    part = anchor_ref.shape[1]
    columns = slice(part - results[0].shape[1], part)
    for copy in outer_step(columns, anchor_ref, momentum_ref, own_ref, theirs, results, outs, sems):
        copy.wait()


def call(body, out_shape, ins, name, scratch=(), in_specs=None, out_specs=None, aliases=None):
    flops = int(MICROSECONDS[name] * PEAK / 1e6)
    cost = pl.CostEstimate(flops=flops, transcendentals=0, bytes_accessed=0)
    return pl.pallas_call(
        body,
        out_shape=out_shape,
        in_specs=in_specs or [VMEM] * len(ins),
        out_specs=out_specs or [VMEM] * len(out_shape),
        scratch_shapes=list(scratch),
        input_output_aliases=aliases or {},
        cost_estimate=cost,
        compiler_params=PARAMS,
        name=name,
    )(*ins)


def per_device(
    theta,
    first_moment,
    second_moment,
    anchor,
    momentum,
    cotangent,
    weights,
    expert_ids,
    expert_counts,
    hidden_saved,
):
    n_island, n_dp, n_expert = (lax.axis_size(name) for name in ("island", "dp", "expert"))
    pairs = n_expert // 2
    units, width = theta.shape[2:]
    length, full_units = hidden_saved.shape[3:]
    part = width // n_island
    first = cut(part)
    split = (n_island - 1) * first
    bf16 = functools.partial(jax.ShapeDtypeStruct, dtype=jnp.bfloat16)

    def ring(value, name, size, shift):
        return lax.ppermute(value, name, [(k, (k + shift) % size) for k in range(size)])

    blocks = list(pack_rows(cotangent, weights, expert_ids, expert_counts, n_island))
    arrived = []
    for k in order(pairs)[:-1]:
        perm = [(2 * z + c, 2 * target(z, k, pairs) + c) for z in range(pairs) for c in range(2)]
        arrived.append(lax.ppermute(blocks[k], "expert", perm))
    saved = hidden_saved.reshape(length, full_units)
    saved_all = call(
        functools.partial(split_body, n_dp),
        [bf16((units, length))] * n_dp,
        [saved, blocks[0]],
        "split",
        [pltpu.VMEM((full_units, length), jnp.float32)],
    )
    saved_all = [ring(saved_all[s], "dp", n_dp, s) if s else saved_all[0] for s in range(n_dp)]
    arrived.append(blocks[0])
    one_mine, two_mine = call(
        functools.partial(assemble_body, pairs),
        [bf16((pairs * CAP, columns)) for columns in (split, width - split)],
        arrived + saved_all[1:],
        "assemble",
    )
    swap = [(j, j ^ 1) for j in range(n_expert)]

    def spread(mine, after=None):
        quarters = [mine, lax.ppermute(mine, "expert", swap)]
        for shift in range(1, n_dp):
            value = ring(mine, "dp", n_dp, shift)
            if after is not None:
                value, _ = lax.optimization_barrier((value, after))
            quarters += [value, lax.ppermute(value, "expert", swap)]
        return quarters

    one_quarters = spread(one_mine)
    states = [in_hbm(value.reshape(units, width)) for value in (theta, first_moment, second_moment)]
    states = call(
        stage_body,
        [bf16((units, width))] * 3,
        states + [one_mine],
        "stage",
        [pltpu.SemaphoreType.DMA((3,))],
        in_specs=[HBM] * 3 + [VMEM],
    )
    (two_mine,) = call(
        rest_body,
        [bf16((pairs * CAP, width - split))],
        [two_mine, one_quarters[1], *states],
        "rest",
    )
    *one, one_slots, left = call(
        functools.partial(one_body, n_dp, n_island, pairs),
        [bf16((units, first))] * (n_island - 1)
        + [bf16((n_dp * length, split)), bf16((units, n_dp * length))],
        one_quarters + saved_all + list(states),
        "far_one",
    )
    theirs = [ring(value, "island", n_island, shift + 1) for shift, value in enumerate(one)]
    two_quarters = spread(two_mine, left)
    *two, two_slots = call(
        functools.partial(two_body, n_dp, n_island, pairs),
        [bf16((units, part - first))] * (n_island - 1)
        + [bf16((n_dp * length, width - split))],
        two_quarters + [left, *states],
        "far_two",
    )
    theirs += [ring(value, "island", n_island, shift + 1) for shift, value in enumerate(two)]
    hidden = call(
        functools.partial(hidden_body, n_dp, n_island),
        [bf16((units, length))] * n_dp,
        [one_slots, two_slots, states[0]],
        "hidden_grad",
    )
    hidden = [hidden[0]] + [ring(hidden[s], "dp", n_dp, s) for s in range(1, n_dp)]
    (own,) = call(near_body, [bf16((units, part))], [two_slots, left, *states], "near_update")
    outer = [anchor.reshape(units, part), momentum.reshape(units, part), own]
    outer_type = jax.ShapeDtypeStruct((units, part), jnp.float32)
    *begun, d_hidden = call(
        functools.partial(outer_one_body, n_island, n_dp),
        [outer_type, outer_type, bf16((length, full_units))],
        outer + theirs[: n_island - 1] + hidden,
        "outer_one",
        [pltpu.VMEM((units, first), jnp.float32)] * 2
        + [
            pltpu.VMEM((length, full_units), jnp.bfloat16),
            pltpu.VMEM((full_units, length), jnp.float32),
            pltpu.SemaphoreType.DMA((3, 2)),
        ],
        out_specs=[HBM, HBM, HBM],
    )
    ins = [*begun, *outer, *theirs[n_island - 1 :]]
    anchor_new, momentum_new = call(
        functools.partial(outer_two_body, n_island),
        [outer_type, outer_type],
        ins,
        "outer_two",
        [pltpu.VMEM((units, part - first), jnp.float32)] * 2 + [pltpu.SemaphoreType.DMA((2, 2))],
        in_specs=[HBM, HBM] + [VMEM] * (len(ins) - 2),
        out_specs=[HBM, HBM],
        aliases={0: 0, 1: 1},
    )
    return (
        anchor_new.reshape(anchor.shape),
        momentum_new.reshape(momentum.shape),
        d_hidden.reshape(hidden_saved.shape),
    )


def solution(mesh):
    return jax.shard_map(
        per_device,
        mesh=mesh,
        in_specs=(
            P("island", "expert", "dp", None),
            P("island", "expert", "dp", None),
            P("island", "expert", "dp", None),
            P("expert", "dp", "island"),
            P("expert", "dp", "island"),
            P(("island", "dp", "expert"), None),
            P(("island", "dp", "expert"), None),
            P(("island", "dp", "expert"), None),
            P(("island", "dp", "expert"), None),
            P("island", "dp", "expert", None, None),
        ),
        out_specs=(
            P("expert", "dp", "island"),
            P("expert", "dp", "island"),
            P("island", "dp", "expert", None, None),
        ),
        check_vma=False,
    )
```

```python
import functools

import jax
import jax.numpy as jnp
from jax import lax
from jax.experimental import pallas as pl
from jax.experimental.pallas import tpu as pltpu
from jax.sharding import PartitionSpec as P

FF = 768
CAP = 16

beta_one = 0.9
beta_two = 0.95
adam_epsilon = 1e-08
inner_rate = 0.1
decay_rate = 0.1
outer_beta = 0.9
outer_rate = 0.7

VMEM = pl.BlockSpec(memory_space=pltpu.VMEM)
HBM = pl.BlockSpec(memory_space=pltpu.HBM)
PARAMS = pltpu.CompilerParams(vmem_limit_bytes=48 * 1024 * 1024)


PEAK = 1.15e15
MICROSECONDS = {
    "stage": 1.6,
    "split": 0.1,
    "assemble": 0.05,
    "rest": 0.05,
    "far_one": 0.1,
    "far_two": 0.3,
    "hidden_grad": 0.3,
    "near_update": 0.3,
    "outer_one": 1.1,
    "outer_two": 0.9,
}


def in_hbm(value):
    return pltpu.with_memory_space_constraint(value, pltpu.HBM)


def wrap(value, size):
    return lax.rem(value + size, size)


def target(place, step, size):
    return place ^ step if size & (size - 1) == 0 else (place + step) % size


def order(size):
    return sorted(range(size), key=lambda step: (step == 0, step != size // 2, -step))


def source(place, step, size):
    return place ^ step if size & (size - 1) == 0 else (place - step) % size


def cut(part):
    return part * 3 // 4 // 128 * 128


def pieces(n_island, width):
    part = width // n_island
    first = cut(part)
    island = lax.axis_index("island")
    order = [(shift, 0, first) for shift in range(1, n_island)]
    order += [(shift, first, part - first) for shift in range(1, n_island)]
    order += [(n_island, 0, part)]
    found, at = [], 0
    for shift, skip, size in order:
        column = lax.rem(island + shift, n_island) * part + skip
        found.append((slice(at, at + size), pl.ds(pl.multiple_of(column, 128), size)))
        at += size
    return found


def pack_body(experts, n_island, ids_hbm, weights_hbm, counts_hbm, cot_hbm, *refs):
    outs = refs[:experts]
    ids_ref, weights_ref, counts_ref, cot_ref, sems = refs[experts:]
    copies = [
        pltpu.make_async_copy(src, dst, sems.at[index])
        for index, (src, dst) in enumerate(
            [
                (ids_hbm, ids_ref),
                (weights_hbm, weights_ref),
                (counts_hbm, counts_ref),
                (cot_hbm, cot_ref),
            ]
        )
    ]
    for copy in copies:
        copy.start()
    width, tokens = ids_ref.shape
    rows = experts * CAP
    place = lax.div(lax.axis_index("expert"), 2)
    step = lax.broadcasted_iota(jnp.int32, (experts, CAP, tokens), 0).reshape(rows, tokens)
    expert = target(place, step, experts)
    rank = lax.broadcasted_iota(jnp.int32, (experts, CAP, tokens), 1).reshape(rows, tokens)
    earlier = (
        lax.broadcasted_iota(jnp.int32, (tokens, tokens), 0)
        < lax.broadcasted_iota(jnp.int32, (tokens, tokens), 1)
    )
    earlier = jnp.where(earlier, 1.0, 0.0).astype(jnp.bfloat16)
    for copy in copies[:3]:
        copy.wait()
    named = jnp.zeros((rows, tokens), jnp.float32)
    weight = jnp.zeros((rows, tokens), jnp.float32)
    for slot in range(width):
        hit = ids_ref[slot : slot + 1, :] == expert
        named = jnp.where(hit, 1.0, named)
        weight = jnp.where(hit, weights_ref[slot : slot + 1, :], weight)
    limit = jnp.zeros((rows, tokens), jnp.int32)
    for index in range(experts):
        limit = jnp.where(expert == index, counts_ref[:, index : index + 1], limit)
    found = jnp.dot(named.astype(jnp.bfloat16), earlier, preferred_element_type=jnp.float32)
    found = found.astype(jnp.int32)
    picked = (named > 0.0) & (found < limit) & (found == rank)
    pick = jnp.where(picked, 1.0, 0.0)
    scale = jnp.sum(pick * weight, axis=1, keepdims=True)
    pick = pick.astype(jnp.bfloat16)
    copies[3].wait()
    for at, columns in pieces(n_island, cot_ref.shape[1]):
        gathered = jnp.dot(pick, cot_ref[:, columns], preferred_element_type=jnp.float32)
        packed = (gathered * scale).astype(jnp.bfloat16)
        for index, out in enumerate(outs):
            out[:, at] = packed[index * CAP : (index + 1) * CAP]


def pack_rows(cotangent, weights, expert_ids, counts, n_island):
    experts = counts.shape[1]
    ins = [expert_ids.T, weights.T, counts, cotangent]
    return pl.pallas_call(
        functools.partial(pack_body, experts, n_island),
        out_shape=[jax.ShapeDtypeStruct((CAP, cotangent.shape[1]), jnp.bfloat16)] * experts,
        in_specs=[HBM] * 4,
        out_specs=[VMEM] * experts,
        scratch_shapes=[
            pltpu.VMEM(expert_ids.shape[::-1], jnp.int32),
            pltpu.VMEM(weights.shape[::-1], jnp.float32),
            pltpu.VMEM(counts.shape, jnp.int32),
            pltpu.VMEM(cotangent.shape, jnp.bfloat16),
            pltpu.SemaphoreType.DMA((4,)),
        ],
        compiler_params=PARAMS,
        name="pack",
    )(*[in_hbm(value) for value in ins])


def adam(product, first, second, theta):
    scale = FF ** (-0.5)
    wide = theta.astype(jnp.float32)
    first_new = (inner_rate * beta_one) * first.astype(jnp.float32)
    first_new = first_new + (inner_rate * (1.0 - beta_one) * scale) * product
    second_new = beta_two * second.astype(jnp.float32)
    second_new = second_new + ((1.0 - beta_two) * scale * scale) * (product * product)
    step_size = first_new / (jnp.sqrt(second_new) + adam_epsilon)
    return ((1.0 - inner_rate * decay_rate) * wide - step_size).astype(jnp.bfloat16)


def assemble_body(pairs, *refs):
    blocks, (one_ref, two_ref) = refs[:pairs], refs[-2:]
    split = one_ref.shape[1]
    for index, block in enumerate(blocks):
        rows = slice(index * CAP, (index + 1) * CAP)
        one_ref[rows, :] = block[:, :split]
        two_ref[rows, :] = block[:, split:]


def rest_body(two_ref, *refs):
    refs[-1][...] = two_ref[...]


def stage_body(*refs):
    states, copied, sems = refs[:3], refs[4:7], refs[7]
    copies = [
        pltpu.make_async_copy(src, dst, sems.at[index])
        for index, (src, dst) in enumerate(zip(states, copied))
    ]
    for copy in copies:
        copy.start()
    for copy in copies:
        copy.wait()


def split_body(n_dp, saved_ref, _, *refs):
    *outs, scratch = refs
    units = outs[0].shape[0]
    scratch[...] = saved_ref[...].astype(jnp.float32).T
    for shift, out in enumerate(outs):
        row = pl.multiple_of(lax.rem(lax.axis_index("dp") + shift, n_dp) * units, 8)
        out[...] = scratch[pl.ds(row, units), :].astype(jnp.bfloat16)


def gather_slots(n_dp, pairs, quarters, slots_ref):
    data, position = lax.axis_index("dp"), lax.axis_index("expert")
    core = lax.rem(position, 2)
    place = lax.div(position, 2)
    length = 2 * pairs * CAP
    for shift in range(n_dp):
        group = wrap(data - shift, n_dp)
        for flip in range(2):
            side = core if flip == 0 else 1 - core
            block = quarters[2 * shift + flip]
            for k in range(pairs):
                at = order(pairs).index(k) * CAP
                row = group * length + (2 * source(place, k, pairs) + side) * CAP
                row = pl.multiple_of(row, CAP)
                slots_ref[pl.ds(row, CAP), :] = block[at : at + CAP, :]


def update(left, slots, state_refs, columns):
    product = jnp.dot(left, slots, preferred_element_type=jnp.float32)
    theta, first, second = (ref[:, columns] for ref in state_refs)
    return adam(product, first, second, theta)


def one_body(n_dp, n_island, pairs, *refs):
    quarters = refs[: 2 * n_dp]
    saved = refs[2 * n_dp : 3 * n_dp]
    state_refs = refs[3 * n_dp : 3 * n_dp + 3]
    *outs, slots_ref, left_ref = refs[3 * n_dp + 3 :]
    length = saved[0].shape[1]
    for shift, value in enumerate(saved):
        column = pl.multiple_of(wrap(lax.axis_index("dp") - shift, n_dp) * length, 128)
        left_ref[:, pl.ds(column, length)] = value[...]
    gather_slots(n_dp, pairs, quarters, slots_ref)
    places = pieces(n_island, state_refs[0].shape[1])
    for out, (at, columns) in zip(outs, places):
        out[...] = update(left_ref[...], slots_ref[:, at], state_refs, columns)


def two_body(n_island, slots_ref, left_ref, *refs):
    state_refs, outs = refs[:3], refs[-(n_island - 1) :]
    width = state_refs[0].shape[1]
    first = width - slots_ref.shape[1]
    places = pieces(n_island, width)[n_island - 1 :]
    for out, (at, columns) in zip(outs, places):
        slots = slots_ref[:, at.start - first : at.stop - first]
        out[...] = update(left_ref[...], slots, state_refs, columns)


def hidden_body(n_dp, n_island, pairs, *refs):
    one_ref, theta_ref, *outs, two_ref = refs[2 * n_dp :]
    gather_slots(n_dp, pairs, refs[: 2 * n_dp], two_ref)
    data = lax.axis_index("dp")
    split = one_ref.shape[1]
    length = one_ref.shape[0] // n_dp
    total = None
    for at, columns in pieces(n_island, theta_ref.shape[1]):
        in_one = at.stop <= split
        slots = one_ref[:, at] if in_one else two_ref[:, at.start - split : at.stop - split]
        value = lax.dot_general(
            theta_ref[:, columns],
            slots,
            (((1,), (1,)), ((), ())),
            preferred_element_type=jnp.float32,
        )
        total = value if total is None else total + value
    hidden = (FF ** (-0.5) * total).astype(jnp.bfloat16)
    for shift, out in enumerate(outs):
        for group in range(n_dp):

            @pl.when(lax.rem(data + shift, n_dp) == group)
            def _():
                out[...] = hidden[:, group * length : (group + 1) * length]


def near_body(slots_ref, left_ref, *refs):
    *state_refs, own_ref = refs
    part = own_ref.shape[1]
    columns = pl.ds(pl.multiple_of(lax.axis_index("island") * part, 128), part)
    slots = slots_ref[:, slots_ref.shape[1] - part :]
    own_ref[...] = update(left_ref[...], slots, state_refs, columns)


def outer_step(columns, anchor_ref, momentum_ref, own_ref, theirs, results, outs, sems):
    n_island = len(theirs) + 1
    rows = anchor_ref.shape[0]
    steps = 2 if rows % 16 == 0 else 1
    copies = []
    for step in range(steps):
        at = slice(step * (rows // steps), (step + 1) * (rows // steps))
        total = own_ref[at, columns].astype(jnp.float32)
        for theta in theirs:
            total = total + theta[at, :].astype(jnp.float32)
        anchor = anchor_ref[at, columns]
        mean_delta = anchor - total * (1.0 / n_island)
        momentum_new = outer_beta * momentum_ref[at, columns] + mean_delta
        results[1][at, :] = momentum_new
        results[0][at, :] = anchor - outer_rate * (mean_delta + outer_beta * momentum_new)
        for index in range(2):
            copies.append(
                pltpu.make_async_copy(
                    results[index].at[at, :], outs[index].at[at, columns], sems.at[index, step]
                )
            )
            copies[-1].start()
    return copies


def outer_one_body(n_island, n_dp, anchor_ref, momentum_ref, own_ref, *refs):
    theirs, refs = refs[: n_island - 1], refs[n_island - 1 :]
    hidden, refs = refs[:n_dp], refs[n_dp:]
    *outs, hidden_out = refs[:3]
    *results, hidden_ref, scratch, sems = refs[3:]
    data = lax.axis_index("dp")
    units = hidden[0].shape[0]
    for shift, value in enumerate(hidden):
        row = pl.multiple_of(wrap(data - shift, n_dp) * units, 8)
        scratch[pl.ds(row, units), :] = value[...].astype(jnp.float32)
    columns = slice(0, results[0].shape[1])
    copies = outer_step(columns, anchor_ref, momentum_ref, own_ref, theirs, results, outs, sems)
    hidden_ref[...] = scratch[...].T.astype(jnp.bfloat16)
    copies.append(pltpu.make_async_copy(hidden_ref, hidden_out, sems.at[2, 0]))
    copies[-1].start()
    for copy in copies:
        copy.wait()


def outer_two_body(n_island, _, __, anchor_ref, momentum_ref, own_ref, *refs):
    theirs, outs = refs[: n_island - 1], refs[n_island - 1 : n_island + 1]
    *results, sems = refs[n_island + 1 :]
    part = anchor_ref.shape[1]
    columns = slice(part - results[0].shape[1], part)
    for copy in outer_step(columns, anchor_ref, momentum_ref, own_ref, theirs, results, outs, sems):
        copy.wait()


def call(body, out_shape, ins, name, scratch=(), in_specs=None, out_specs=None, aliases=None):
    flops = int(MICROSECONDS[name] * PEAK / 1e6)
    cost = pl.CostEstimate(flops=flops, transcendentals=0, bytes_accessed=0)
    return pl.pallas_call(
        body,
        out_shape=out_shape,
        in_specs=in_specs or [VMEM] * len(ins),
        out_specs=out_specs or [VMEM] * len(out_shape),
        scratch_shapes=list(scratch),
        input_output_aliases=aliases or {},
        cost_estimate=cost,
        compiler_params=PARAMS,
        name=name,
    )(*ins)


def per_device(
    theta,
    first_moment,
    second_moment,
    anchor,
    momentum,
    cotangent,
    weights,
    expert_ids,
    expert_counts,
    hidden_saved,
):
    n_island, n_dp, n_expert = (lax.axis_size(name) for name in ("island", "dp", "expert"))
    pairs = n_expert // 2
    units, width = theta.shape[2:]
    length, full_units = hidden_saved.shape[3:]
    part = width // n_island
    first = cut(part)
    split = (n_island - 1) * first
    bf16 = functools.partial(jax.ShapeDtypeStruct, dtype=jnp.bfloat16)

    def ring(value, name, size, shift):
        return lax.ppermute(value, name, [(k, (k + shift) % size) for k in range(size)])

    blocks = list(pack_rows(cotangent, weights, expert_ids, expert_counts, n_island))
    arrived = []
    for k in order(pairs)[:-1]:
        perm = [(2 * z + c, 2 * target(z, k, pairs) + c) for z in range(pairs) for c in range(2)]
        arrived.append(lax.ppermute(blocks[k], "expert", perm))
    saved = hidden_saved.reshape(length, full_units)
    saved_all = call(
        functools.partial(split_body, n_dp),
        [bf16((units, length))] * n_dp,
        [saved, blocks[0]],
        "split",
        [pltpu.VMEM((full_units, length), jnp.float32)],
    )
    saved_all = [ring(saved_all[s], "dp", n_dp, s) if s else saved_all[0] for s in range(n_dp)]
    arrived.append(blocks[0])
    one_mine, two_mine = call(
        functools.partial(assemble_body, pairs),
        [bf16((pairs * CAP, columns)) for columns in (split, width - split)],
        arrived + saved_all[1:],
        "assemble",
    )
    swap = [(j, j ^ 1) for j in range(n_expert)]

    def spread(mine, after=None):
        quarters = [mine, lax.ppermute(mine, "expert", swap)]
        for shift in range(1, n_dp):
            value = ring(mine, "dp", n_dp, shift)
            if after is not None:
                value, _ = lax.optimization_barrier((value, after))
            quarters += [value, lax.ppermute(value, "expert", swap)]
        return quarters

    one_quarters = spread(one_mine)
    states = [in_hbm(value.reshape(units, width)) for value in (theta, first_moment, second_moment)]
    states = call(
        stage_body,
        [bf16((units, width))] * 3,
        states + [one_mine],
        "stage",
        [pltpu.SemaphoreType.DMA((3,))],
        in_specs=[HBM] * 3 + [VMEM],
    )
    (two_mine,) = call(
        rest_body,
        [bf16((pairs * CAP, width - split))],
        [two_mine, one_quarters[1], *states],
        "rest",
    )
    *one, one_slots, left = call(
        functools.partial(one_body, n_dp, n_island, pairs),
        [bf16((units, first))] * (n_island - 1)
        + [bf16((n_dp * length, split)), bf16((units, n_dp * length))],
        one_quarters + saved_all + list(states),
        "far_one",
    )
    theirs = [ring(value, "island", n_island, shift + 1) for shift, value in enumerate(one)]
    two_quarters = spread(two_mine, left)
    *hidden, two_slots = call(
        functools.partial(hidden_body, n_dp, n_island, pairs),
        [bf16((units, length))] * n_dp + [bf16((n_dp * length, width - split))],
        two_quarters + [one_slots, states[0]],
        "hidden_grad",
    )
    two = call(
        functools.partial(two_body, n_island),
        [bf16((units, part - first))] * (n_island - 1),
        [two_slots, left, *states, hidden[0]],
        "far_two",
    )
    theirs += [ring(value, "island", n_island, shift + 1) for shift, value in enumerate(two)]
    hidden = [hidden[0]] + [ring(hidden[s], "dp", n_dp, s) for s in range(1, n_dp)]
    (own,) = call(near_body, [bf16((units, part))], [two_slots, left, *states], "near_update")
    outer = [anchor.reshape(units, part), momentum.reshape(units, part), own]
    outer_type = jax.ShapeDtypeStruct((units, part), jnp.float32)
    *begun, d_hidden = call(
        functools.partial(outer_one_body, n_island, n_dp),
        [outer_type, outer_type, bf16((length, full_units))],
        outer + theirs[: n_island - 1] + hidden,
        "outer_one",
        [pltpu.VMEM((units, first), jnp.float32)] * 2
        + [
            pltpu.VMEM((length, full_units), jnp.bfloat16),
            pltpu.VMEM((full_units, length), jnp.float32),
            pltpu.SemaphoreType.DMA((3, 2)),
        ],
        out_specs=[HBM, HBM, HBM],
    )
    ins = [*begun, *outer, *theirs[n_island - 1 :]]
    anchor_new, momentum_new = call(
        functools.partial(outer_two_body, n_island),
        [outer_type, outer_type],
        ins,
        "outer_two",
        [pltpu.VMEM((units, part - first), jnp.float32)] * 2 + [pltpu.SemaphoreType.DMA((2, 2))],
        in_specs=[HBM, HBM] + [VMEM] * (len(ins) - 2),
        out_specs=[HBM, HBM],
        aliases={0: 0, 1: 1},
    )
    return (
        anchor_new.reshape(anchor.shape),
        momentum_new.reshape(momentum.shape),
        d_hidden.reshape(hidden_saved.shape),
    )


def solution(mesh):
    return jax.shard_map(
        per_device,
        mesh=mesh,
        in_specs=(
            P("island", "expert", "dp", None),
            P("island", "expert", "dp", None),
            P("island", "expert", "dp", None),
            P("expert", "dp", "island"),
            P("expert", "dp", "island"),
            P(("island", "dp", "expert"), None),
            P(("island", "dp", "expert"), None),
            P(("island", "dp", "expert"), None),
            P(("island", "dp", "expert"), None),
            P("island", "dp", "expert", None, None),
        ),
        out_specs=(
            P("expert", "dp", "island"),
            P("expert", "dp", "island"),
            P("island", "dp", "expert", None, None),
        ),
        check_vma=False,
    )
```

```python
import functools

import jax
import jax.numpy as jnp
from jax import lax
from jax.experimental import pallas as pl
from jax.experimental.pallas import tpu as pltpu
from jax.sharding import PartitionSpec as P

FF = 768
CAP = 16

beta_one = 0.9
beta_two = 0.95
adam_epsilon = 1e-08
inner_rate = 0.1
decay_rate = 0.1
outer_beta = 0.9
outer_rate = 0.7

VMEM = pl.BlockSpec(memory_space=pltpu.VMEM)
HBM = pl.BlockSpec(memory_space=pltpu.HBM)
PARAMS = pltpu.CompilerParams(vmem_limit_bytes=48 * 1024 * 1024)


PEAK = 1.15e15
MICROSECONDS = {
    "stage": 1.6,
    "split": 0.1,
    "assemble": 0.05,
    "rest": 0.05,
    "far_one": 0.1,
    "far_two": 0.3,
    "hidden_grad": 0.3,
    "near_update": 0.3,
    "outer_one": 1.1,
    "outer_two": 0.9,
}


def in_hbm(value):
    return pltpu.with_memory_space_constraint(value, pltpu.HBM)


def wrap(value, size):
    return lax.rem(value + size, size)


def target(place, step, size):
    return place ^ step if size & (size - 1) == 0 else (place + step) % size


def order(size):
    return sorted(range(size), key=lambda step: (step == 0, step != size // 2, -step))


def source(place, step, size):
    return place ^ step if size & (size - 1) == 0 else (place - step) % size


def cut(part):
    return part * 3 // 4 // 128 * 128


def pieces(n_island, width):
    part = width // n_island
    first = cut(part)
    island = lax.axis_index("island")
    order = [(shift, 0, first) for shift in range(1, n_island)]
    order += [(shift, first, part - first) for shift in range(1, n_island)]
    order += [(n_island, 0, part)]
    found, at = [], 0
    for shift, skip, size in order:
        column = lax.rem(island + shift, n_island) * part + skip
        found.append((slice(at, at + size), pl.ds(pl.multiple_of(column, 128), size)))
        at += size
    return found


def pack_body(experts, n_island, ids_hbm, weights_hbm, counts_hbm, cot_hbm, *refs):
    outs = refs[:experts]
    ids_ref, weights_ref, counts_ref, cot_ref, sems = refs[experts:]
    copies = [
        pltpu.make_async_copy(src, dst, sems.at[index])
        for index, (src, dst) in enumerate(
            [
                (ids_hbm, ids_ref),
                (weights_hbm, weights_ref),
                (counts_hbm, counts_ref),
                (cot_hbm, cot_ref),
            ]
        )
    ]
    for copy in copies[3:] + copies[:3]:
        copy.start()
    width, tokens = ids_ref.shape
    rows = experts * CAP
    place = lax.div(lax.axis_index("expert"), 2)
    step = lax.broadcasted_iota(jnp.int32, (experts, CAP, tokens), 0).reshape(rows, tokens)
    expert = target(place, step, experts)
    rank = lax.broadcasted_iota(jnp.int32, (experts, CAP, tokens), 1).reshape(rows, tokens)
    earlier = (
        lax.broadcasted_iota(jnp.int32, (tokens, tokens), 0)
        < lax.broadcasted_iota(jnp.int32, (tokens, tokens), 1)
    )
    earlier = jnp.where(earlier, 1.0, 0.0).astype(jnp.bfloat16)
    for copy in copies[:3]:
        copy.wait()
    named = jnp.zeros((rows, tokens), jnp.float32)
    weight = jnp.zeros((rows, tokens), jnp.float32)
    for slot in range(width):
        hit = ids_ref[slot : slot + 1, :] == expert
        named = jnp.where(hit, 1.0, named)
        weight = jnp.where(hit, weights_ref[slot : slot + 1, :], weight)
    limit = jnp.zeros((rows, tokens), jnp.int32)
    for index in range(experts):
        limit = jnp.where(expert == index, counts_ref[:, index : index + 1], limit)
    found = jnp.dot(named.astype(jnp.bfloat16), earlier, preferred_element_type=jnp.float32)
    found = found.astype(jnp.int32)
    picked = (named > 0.0) & (found < limit) & (found == rank)
    pick = jnp.where(picked, 1.0, 0.0)
    scale = jnp.sum(pick * weight, axis=1, keepdims=True)
    pick = pick.astype(jnp.bfloat16)
    copies[3].wait()
    for at, columns in pieces(n_island, cot_ref.shape[1]):
        gathered = jnp.dot(pick, cot_ref[:, columns], preferred_element_type=jnp.float32)
        packed = (gathered * scale).astype(jnp.bfloat16)
        for index, out in enumerate(outs):
            out[:, at] = packed[index * CAP : (index + 1) * CAP]


def pack_rows(cotangent, weights, expert_ids, counts, n_island):
    experts = counts.shape[1]
    ins = [expert_ids.T, weights.T, counts, cotangent]
    return pl.pallas_call(
        functools.partial(pack_body, experts, n_island),
        out_shape=[jax.ShapeDtypeStruct((CAP, cotangent.shape[1]), jnp.bfloat16)] * experts,
        in_specs=[HBM] * 4,
        out_specs=[VMEM] * experts,
        scratch_shapes=[
            pltpu.VMEM(expert_ids.shape[::-1], jnp.int32),
            pltpu.VMEM(weights.shape[::-1], jnp.float32),
            pltpu.VMEM(counts.shape, jnp.int32),
            pltpu.VMEM(cotangent.shape, jnp.bfloat16),
            pltpu.SemaphoreType.DMA((4,)),
        ],
        compiler_params=PARAMS,
        name="pack",
    )(*[in_hbm(value) for value in ins])


def adam(product, first, second, theta):
    scale = FF ** (-0.5)
    wide = theta.astype(jnp.float32)
    first_new = (inner_rate * beta_one) * first.astype(jnp.float32)
    first_new = first_new + (inner_rate * (1.0 - beta_one) * scale) * product
    second_new = beta_two * second.astype(jnp.float32)
    second_new = second_new + ((1.0 - beta_two) * scale * scale) * (product * product)
    step_size = first_new / (jnp.sqrt(second_new) + adam_epsilon)
    return ((1.0 - inner_rate * decay_rate) * wide - step_size).astype(jnp.bfloat16)


def assemble_body(pairs, *refs):
    blocks, (one_ref, two_ref) = refs[:pairs], refs[-2:]
    split = one_ref.shape[1]
    for index, block in enumerate(blocks):
        rows = slice(index * CAP, (index + 1) * CAP)
        one_ref[rows, :] = block[:, :split]
        two_ref[rows, :] = block[:, split:]


def rest_body(two_ref, *refs):
    refs[-1][...] = two_ref[...]


def stage_body(*refs):
    states, copied, sems = refs[:3], refs[4:7], refs[7]
    copies = [
        pltpu.make_async_copy(src, dst, sems.at[index])
        for index, (src, dst) in enumerate(zip(states, copied))
    ]
    for copy in copies:
        copy.start()
    for copy in copies:
        copy.wait()


def split_body(n_dp, saved_ref, _, *refs):
    *outs, scratch = refs
    units = outs[0].shape[0]
    scratch[...] = saved_ref[...].astype(jnp.float32).T
    for shift, out in enumerate(outs):
        row = pl.multiple_of(lax.rem(lax.axis_index("dp") + shift, n_dp) * units, 8)
        out[...] = scratch[pl.ds(row, units), :].astype(jnp.bfloat16)


def gather_slots(n_dp, pairs, quarters, slots_ref):
    data, position = lax.axis_index("dp"), lax.axis_index("expert")
    core = lax.rem(position, 2)
    place = lax.div(position, 2)
    length = 2 * pairs * CAP
    for shift in range(n_dp):
        group = wrap(data - shift, n_dp)
        for flip in range(2):
            side = core if flip == 0 else 1 - core
            block = quarters[2 * shift + flip]
            for k in range(pairs):
                at = order(pairs).index(k) * CAP
                row = group * length + (2 * source(place, k, pairs) + side) * CAP
                row = pl.multiple_of(row, CAP)
                slots_ref[pl.ds(row, CAP), :] = block[at : at + CAP, :]


def update(left, slots, state_refs, columns):
    product = jnp.dot(left, slots, preferred_element_type=jnp.float32)
    theta, first, second = (ref[:, columns] for ref in state_refs)
    return adam(product, first, second, theta)


def one_body(n_dp, n_island, pairs, *refs):
    quarters = refs[: 2 * n_dp]
    saved = refs[2 * n_dp : 3 * n_dp]
    state_refs = refs[3 * n_dp : 3 * n_dp + 3]
    *outs, slots_ref, left_ref = refs[3 * n_dp + 3 :]
    length = saved[0].shape[1]
    for shift, value in enumerate(saved):
        column = pl.multiple_of(wrap(lax.axis_index("dp") - shift, n_dp) * length, 128)
        left_ref[:, pl.ds(column, length)] = value[...]
    gather_slots(n_dp, pairs, quarters, slots_ref)
    places = pieces(n_island, state_refs[0].shape[1])
    for out, (at, columns) in zip(outs, places):
        out[...] = update(left_ref[...], slots_ref[:, at], state_refs, columns)


def two_body(n_island, slots_ref, left_ref, *refs):
    state_refs, outs = refs[:3], refs[-(n_island - 1) :]
    width = state_refs[0].shape[1]
    first = width - slots_ref.shape[1]
    places = pieces(n_island, width)[n_island - 1 :]
    for out, (at, columns) in zip(outs, places):
        slots = slots_ref[:, at.start - first : at.stop - first]
        out[...] = update(left_ref[...], slots, state_refs, columns)


def hidden_body(n_dp, n_island, pairs, *refs):
    one_ref, theta_ref, *outs, two_ref = refs[2 * n_dp :]
    gather_slots(n_dp, pairs, refs[: 2 * n_dp], two_ref)
    data = lax.axis_index("dp")
    split = one_ref.shape[1]
    length = one_ref.shape[0] // n_dp
    total = None
    for at, columns in pieces(n_island, theta_ref.shape[1]):
        in_one = at.stop <= split
        slots = one_ref[:, at] if in_one else two_ref[:, at.start - split : at.stop - split]
        value = lax.dot_general(
            theta_ref[:, columns],
            slots,
            (((1,), (1,)), ((), ())),
            preferred_element_type=jnp.float32,
        )
        total = value if total is None else total + value
    hidden = (FF ** (-0.5) * total).astype(jnp.bfloat16)
    for shift, out in enumerate(outs):
        for group in range(n_dp):

            @pl.when(lax.rem(data + shift, n_dp) == group)
            def _():
                out[...] = hidden[:, group * length : (group + 1) * length]


def near_body(slots_ref, left_ref, *refs):
    *state_refs, own_ref = refs
    part = own_ref.shape[1]
    columns = pl.ds(pl.multiple_of(lax.axis_index("island") * part, 128), part)
    slots = slots_ref[:, slots_ref.shape[1] - part :]
    own_ref[...] = update(left_ref[...], slots, state_refs, columns)


def outer_step(columns, anchor_ref, momentum_ref, own_ref, theirs, results, outs, sems):
    n_island = len(theirs) + 1
    rows = anchor_ref.shape[0]
    steps = 2 if rows % 16 == 0 else 1
    copies = []
    for step in range(steps):
        at = slice(step * (rows // steps), (step + 1) * (rows // steps))
        total = own_ref[at, columns].astype(jnp.float32)
        for theta in theirs:
            total = total + theta[at, :].astype(jnp.float32)
        anchor = anchor_ref[at, columns]
        mean_delta = anchor - total * (1.0 / n_island)
        momentum_new = outer_beta * momentum_ref[at, columns] + mean_delta
        results[1][at, :] = momentum_new
        results[0][at, :] = anchor - outer_rate * (mean_delta + outer_beta * momentum_new)
        for index in range(2):
            copies.append(
                pltpu.make_async_copy(
                    results[index].at[at, :], outs[index].at[at, columns], sems.at[index, step]
                )
            )
            copies[-1].start()
    return copies


def outer_one_body(n_island, n_dp, anchor_ref, momentum_ref, own_ref, *refs):
    theirs, refs = refs[: n_island - 1], refs[n_island - 1 :]
    hidden, refs = refs[:n_dp], refs[n_dp:]
    *outs, hidden_out = refs[:3]
    *results, hidden_ref, scratch, sems = refs[3:]
    data = lax.axis_index("dp")
    units = hidden[0].shape[0]
    for shift, value in enumerate(hidden):
        row = pl.multiple_of(wrap(data - shift, n_dp) * units, 8)
        scratch[pl.ds(row, units), :] = value[...].astype(jnp.float32)
    columns = slice(0, results[0].shape[1])
    copies = outer_step(columns, anchor_ref, momentum_ref, own_ref, theirs, results, outs, sems)
    hidden_ref[...] = scratch[...].T.astype(jnp.bfloat16)
    copies.append(pltpu.make_async_copy(hidden_ref, hidden_out, sems.at[2, 0]))
    copies[-1].start()
    for copy in copies:
        copy.wait()


def outer_two_body(n_island, _, __, anchor_ref, momentum_ref, own_ref, *refs):
    theirs, outs = refs[: n_island - 1], refs[n_island - 1 : n_island + 1]
    *results, sems = refs[n_island + 1 :]
    part = anchor_ref.shape[1]
    columns = slice(part - results[0].shape[1], part)
    for copy in outer_step(columns, anchor_ref, momentum_ref, own_ref, theirs, results, outs, sems):
        copy.wait()


def call(body, out_shape, ins, name, scratch=(), in_specs=None, out_specs=None, aliases=None):
    flops = int(MICROSECONDS[name] * PEAK / 1e6)
    cost = pl.CostEstimate(flops=flops, transcendentals=0, bytes_accessed=0)
    return pl.pallas_call(
        body,
        out_shape=out_shape,
        in_specs=in_specs or [VMEM] * len(ins),
        out_specs=out_specs or [VMEM] * len(out_shape),
        scratch_shapes=list(scratch),
        input_output_aliases=aliases or {},
        cost_estimate=cost,
        compiler_params=PARAMS,
        name=name,
    )(*ins)


def per_device(
    theta,
    first_moment,
    second_moment,
    anchor,
    momentum,
    cotangent,
    weights,
    expert_ids,
    expert_counts,
    hidden_saved,
):
    n_island, n_dp, n_expert = (lax.axis_size(name) for name in ("island", "dp", "expert"))
    pairs = n_expert // 2
    units, width = theta.shape[2:]
    length, full_units = hidden_saved.shape[3:]
    part = width // n_island
    first = cut(part)
    split = (n_island - 1) * first
    bf16 = functools.partial(jax.ShapeDtypeStruct, dtype=jnp.bfloat16)

    def ring(value, name, size, shift):
        return lax.ppermute(value, name, [(k, (k + shift) % size) for k in range(size)])

    blocks = list(pack_rows(cotangent, weights, expert_ids, expert_counts, n_island))
    arrived = []
    for k in order(pairs)[:-1]:
        perm = [(2 * z + c, 2 * target(z, k, pairs) + c) for z in range(pairs) for c in range(2)]
        arrived.append(lax.ppermute(blocks[k], "expert", perm))
    saved = hidden_saved.reshape(length, full_units)
    saved_all = call(
        functools.partial(split_body, n_dp),
        [bf16((units, length))] * n_dp,
        [saved, blocks[0]],
        "split",
        [pltpu.VMEM((full_units, length), jnp.float32)],
    )
    saved_all = [ring(saved_all[s], "dp", n_dp, s) if s else saved_all[0] for s in range(n_dp)]
    arrived.append(blocks[0])
    one_mine, two_mine = call(
        functools.partial(assemble_body, pairs),
        [bf16((pairs * CAP, columns)) for columns in (split, width - split)],
        arrived + saved_all[1:],
        "assemble",
    )
    swap = [(j, j ^ 1) for j in range(n_expert)]

    def spread(mine, after=None):
        quarters = [mine, lax.ppermute(mine, "expert", swap)]
        for shift in range(1, n_dp):
            value = ring(mine, "dp", n_dp, shift)
            if after is not None:
                value, _ = lax.optimization_barrier((value, after))
            quarters += [value, lax.ppermute(value, "expert", swap)]
        return quarters

    one_quarters = spread(one_mine)
    states = [in_hbm(value.reshape(units, width)) for value in (theta, first_moment, second_moment)]
    states = call(
        stage_body,
        [bf16((units, width))] * 3,
        states + [one_mine],
        "stage",
        [pltpu.SemaphoreType.DMA((3,))],
        in_specs=[HBM] * 3 + [VMEM],
    )
    (two_mine,) = call(
        rest_body,
        [bf16((pairs * CAP, width - split))],
        [two_mine, one_quarters[1], *states],
        "rest",
    )
    *one, one_slots, left = call(
        functools.partial(one_body, n_dp, n_island, pairs),
        [bf16((units, first))] * (n_island - 1)
        + [bf16((n_dp * length, split)), bf16((units, n_dp * length))],
        one_quarters + saved_all + list(states),
        "far_one",
    )
    theirs = [ring(value, "island", n_island, shift + 1) for shift, value in enumerate(one)]
    two_quarters = spread(two_mine, left)
    *hidden, two_slots = call(
        functools.partial(hidden_body, n_dp, n_island, pairs),
        [bf16((units, length))] * n_dp + [bf16((n_dp * length, width - split))],
        two_quarters + [one_slots, states[0]],
        "hidden_grad",
    )
    two = call(
        functools.partial(two_body, n_island),
        [bf16((units, part - first))] * (n_island - 1),
        [two_slots, left, *states, hidden[0]],
        "far_two",
    )
    theirs += [ring(value, "island", n_island, shift + 1) for shift, value in enumerate(two)]
    hidden = [hidden[0]] + [ring(hidden[s], "dp", n_dp, s) for s in range(1, n_dp)]
    (own,) = call(near_body, [bf16((units, part))], [two_slots, left, *states], "near_update")
    outer = [anchor.reshape(units, part), momentum.reshape(units, part), own]
    outer_type = jax.ShapeDtypeStruct((units, part), jnp.float32)
    *begun, d_hidden = call(
        functools.partial(outer_one_body, n_island, n_dp),
        [outer_type, outer_type, bf16((length, full_units))],
        outer + theirs[: n_island - 1] + hidden,
        "outer_one",
        [pltpu.VMEM((units, first), jnp.float32)] * 2
        + [
            pltpu.VMEM((length, full_units), jnp.bfloat16),
            pltpu.VMEM((full_units, length), jnp.float32),
            pltpu.SemaphoreType.DMA((3, 2)),
        ],
        out_specs=[HBM, HBM, HBM],
    )
    ins = [*begun, *outer, *theirs[n_island - 1 :]]
    anchor_new, momentum_new = call(
        functools.partial(outer_two_body, n_island),
        [outer_type, outer_type],
        ins,
        "outer_two",
        [pltpu.VMEM((units, part - first), jnp.float32)] * 2 + [pltpu.SemaphoreType.DMA((2, 2))],
        in_specs=[HBM, HBM] + [VMEM] * (len(ins) - 2),
        out_specs=[HBM, HBM],
        aliases={0: 0, 1: 1},
    )
    return (
        anchor_new.reshape(anchor.shape),
        momentum_new.reshape(momentum.shape),
        d_hidden.reshape(hidden_saved.shape),
    )


def solution(mesh):
    return jax.shard_map(
        per_device,
        mesh=mesh,
        in_specs=(
            P("island", "expert", "dp", None),
            P("island", "expert", "dp", None),
            P("island", "expert", "dp", None),
            P("expert", "dp", "island"),
            P("expert", "dp", "island"),
            P(("island", "dp", "expert"), None),
            P(("island", "dp", "expert"), None),
            P(("island", "dp", "expert"), None),
            P(("island", "dp", "expert"), None),
            P("island", "dp", "expert", None, None),
        ),
        out_specs=(
            P("expert", "dp", "island"),
            P("expert", "dp", "island"),
            P("island", "dp", "expert", None, None),
        ),
        check_vma=False,
    )
```
